32 devices in a mesh: gz: 4 (over z), xy: 8 (over y, x, core).
Axes of the slice: x: 2, y: 2, z: 4, core: 2. Of those that a mesh axis runs over, the one named last changes fastest.
Arguments:
- positions: float32 [3, 4096], P(None, ('gz', 'xy')), may hold values from 0 to 16, as said below
- velocities: float32 [3, 4096], P(None, ('gz', 'xy')), may hold values from -6 to 6
- forces: float32 [3, 4096], P(None, ('gz', 'xy')), may hold values from -6 to 6
- species: int32 [4096], P(('gz', 'xy')), may hold values from 0 to 3
- counts: int32 [32], P(('gz', 'xy')), may hold values from 16 to 128, as said below
- neighbours: int32 [24, 4096], P(None, ('gz', 'xy')), may hold values from 0 to 320, as said below
- send_inplane: int32 [2, 1024], P(None, ('gz', 'xy')), may hold values from 0 to 127
- send_normal: int32 [2, 2048], P(None, ('gz', 'xy')), may hold values from 0 to 191
- embedding: float32 [4, 128], replicated, may hold values from -6 to 6
- inverse_mass: float32 [4], replicated, may hold values from 0.25 to 1
- radial_weight: float32 [16, 128], replicated, may hold values from -1.5 to 1.5
- mix_weight: float32 [128, 128], replicated, may hold values from -0.5 to 0.5
- self_weight: float32 [128, 128], replicated, may hold values from -0.5 to 0.5
- charge_weight: float32 [128, 128], replicated, may hold values from -0.5 to 0.5
- readout_weight: float32 [128, 128], replicated, may hold values from -0.5 to 0.5
- readout_vector: float32 [128], replicated, may hold values from -0.5 to 0.5
- kernel_filter: float32 [512, 128], replicated, may hold values from 0.2 to 2
Outputs:
- positions_new: float32 [3, 4096], P(None, ('gz', 'xy'))
- velocities_new: float32 [3, 4096], P(None, ('gz', 'xy'))
- forces_new: float32 [3, 4096], P(None, ('gz', 'xy'))
- energy: float32 [], replicated
The draws below stay inside these ranges and needn't reach their ends.
Inputs may be any that keep to these rules, and one draw needn't show every extreme that they name: `positions`: coordinates of domain (g, p) lie in [2 p, 2 p + 2) x [0, 4) x [2 g, 2 g + 2). `counts`: the first domain is full; filling falls along the slab-normal axis. `neighbours`: slots of the extended list: own 128, then 32 from the lower and 32 from the upper in-plane neighbour, 64 from the lower and 64 from the upper slab-normal neighbour, then the padding slot 320.
All inputs are finite; a program needn't handle non-finite values.
Results may differ from the reference program's by a relative error of at most 0.0003.
Values sent between devices are 32-bit elements; how exact they have to be, the bound alone decides.
No kernel may reach another device: no remote copies, remote signals or barrier semaphores. Data moves between devices by JAX's collectives and lax.ppermute only.
A program may use at most 64 MiB of HBM per device.

```python
import math
import jax
import jax.numpy as jnp
from jax import lax

C = 128
KGRID = 8
NB = 16
SPECIES = 4
NEIGH = 24
ATOMS_DEV = 128
NK = 512
GXY = 32
GGZ = 64
EXT = 321
DOMAINS = 32
ATOMS = 4096
N_GZ = 4
N_XY = 8


def draw_positions(key, part):
    all_atoms = ATOMS_DEV * N_GZ * N_XY
    column = jnp.arange(all_atoms)
    domain = column // ATOMS_DEV
    layer_index = (domain // N_XY).astype(jnp.float32)
    strip_index = (domain % N_XY).astype(jnp.float32)
    uniform_draw = jax.random.uniform(key, (3, all_atoms), jnp.float32)
    along_x = (strip_index + uniform_draw[0]) * 2.0
    along_y = uniform_draw[1] * 4.0
    along_z = (layer_index + uniform_draw[2]) * 2.0
    return jnp.stack([along_x, along_y, along_z], axis=0).astype(jnp.float32)


def draw_counts(key, part):
    domain = jnp.arange(N_GZ * N_XY)
    layer_index = domain // N_XY
    dropped = jax.random.randint(key, (N_GZ * N_XY,), 0, ATOMS_DEV // 4 + 1)
    baseline = ATOMS_DEV - layer_index * ATOMS_DEV * 3 // (4 * N_GZ)
    filled = jnp.maximum(baseline - dropped, ATOMS_DEV // 8)
    return jnp.where(domain == 0, ATOMS_DEV, filled).astype(jnp.int32)


def draw_neighbours(key, part):
    all_atoms = ATOMS_DEV * N_GZ * N_XY
    key_first = jax.random.fold_in(key, 11)
    key_second = jax.random.fold_in(key, 23)
    chosen = jax.random.randint(key_first, (NEIGH, all_atoms), 0, EXT - 1)
    filled = jax.random.randint(key_second, (all_atoms,), NEIGH // 2, NEIGH + 1)
    slot_index = jnp.arange(NEIGH)[:, None]
    return jnp.where(slot_index < filled[None, :], chosen, EXT - 1).astype(jnp.int32)


def place_ends(drawn, rng, least, top_value):
    longest = drawn.shape.index(max(drawn.shape))
    spots = []
    for shift in (0, 1):
        where = [jax.random.randint(jax.random.fold_in(rng, axis), (), 0, length) for axis, length in enumerate(drawn.shape)]
        where[longest] = (where[longest] + shift) % drawn.shape[longest]
        spots.append(tuple(where))
    return drawn.at[spots[0]].set(least).at[spots[1]].set(top_value)


def level_of(rng, dims, cuts, least, top_value):
    factor_of, own = 1.0, jax.random.fold_in(rng, 6)
    for position, parts in cuts:
        steps = jnp.exp(jax.random.uniform(jax.random.fold_in(own, position), (parts,), jnp.float32, least / len(cuts), top_value / len(cuts)))
        factor_of = factor_of * jnp.repeat(steps, dims[position] // parts).reshape([-1 if axis == position else 1 for axis in range(len(dims))])
    return factor_of


def noise(own_key, dims, width, bound, cuts=(), kind=jnp.bfloat16):
    values = width * jax.random.normal(own_key, dims, jnp.float32)
    if cuts:
        values = values * level_of(own_key, dims, cuts, -0.22, 0.18)
    return jnp.clip(values, -bound, bound).astype(kind)


def setup_inputs(seed: int = 0) -> dict:
    key_of = jax.random.split(jax.random.key(seed), 18)
    positions = draw_positions(jax.random.fold_in(key_of[17], 71), 0)
    velocities = noise(key_of[1], (3, ATOMS), 1.0, 6.0, ((1, 32),), jnp.float32)
    forces = noise(key_of[2], (3, ATOMS), 1.0, 6.0, ((1, 32),), jnp.float32)
    species = place_ends(jax.random.randint(key_of[3], (ATOMS,), 0, SPECIES), jax.random.fold_in(key_of[3], 1), 0, SPECIES - 1).astype(jnp.int32)
    counts = draw_counts(jax.random.fold_in(key_of[17], 71), 0)
    neighbours = draw_neighbours(jax.random.fold_in(key_of[17], 71), 0)
    send_inplane = place_ends(jax.random.randint(key_of[6], (2, DOMAINS * GXY), 0, ATOMS_DEV), jax.random.fold_in(key_of[6], 1), 0, ATOMS_DEV - 1).astype(jnp.int32)
    send_normal = place_ends(jax.random.randint(key_of[7], (2, DOMAINS * GGZ), 0, ATOMS_DEV + 2 * GXY), jax.random.fold_in(key_of[7], 1), 0, (ATOMS_DEV + 2 * GXY) - 1).astype(jnp.int32)
    embedding = noise(key_of[8], (SPECIES, C), 1.0, 6.0, (), jnp.float32)
    inverse_mass = jnp.clip(jnp.exp(jax.random.uniform(key_of[9], (SPECIES,), jnp.float32, math.log(0.25), math.log(1.0))), 0.25, 1.0)
    radial_weight = noise(key_of[10], (NB, C), NB ** -0.5, 1.5, (), jnp.float32)
    mix_weight = noise(key_of[11], (C, C), C ** -0.5, 0.5, (), jnp.float32)
    self_weight = noise(key_of[12], (C, C), C ** -0.5, 0.5, (), jnp.float32)
    charge_weight = noise(key_of[13], (C, C), C ** -0.5, 0.5, (), jnp.float32)
    readout_weight = noise(key_of[14], (C, C), C ** -0.5, 0.5, (), jnp.float32)
    readout_vector = noise(key_of[15], (C,), C ** -0.5, 0.5, (), jnp.float32)
    kernel_filter = jnp.clip(jnp.exp(jax.random.uniform(key_of[16], (NK, C), jnp.float32, math.log(0.2), math.log(2.0))), 0.2, 2.0)
    return {"positions": positions, "velocities": velocities, "forces": forces, "species": species, "counts": counts, "neighbours": neighbours, "send_inplane": send_inplane, "send_normal": send_normal, "embedding": embedding, "inverse_mass": inverse_mass, "radial_weight": radial_weight, "mix_weight": mix_weight, "self_weight": self_weight, "charge_weight": charge_weight, "readout_weight": readout_weight, "readout_vector": readout_vector, "kernel_filter": kernel_filter}


time_step = 0.5
width_x = 2.0
width_y = 4.0
width_z = 2.0
far_away = 1000.0
softening = 0.25
basis_reach = 6.0
envelope_reach = 4.0
highest = lax.Precision.HIGHEST

def wave_vectors(grid_side, layers, strips):
    wave_index = jnp.arange(grid_side ** 3)
    along_x = (wave_index // (grid_side * grid_side)).astype(jnp.float32) / (strips * width_x)
    along_y = (wave_index // grid_side % grid_side - grid_side // 2).astype(jnp.float32) / width_y
    along_z = (wave_index % grid_side - grid_side // 2).astype(jnp.float32) / (layers * width_z)
    wave_rows = 2.0 * jnp.pi * jnp.stack([along_x, along_y, along_z], axis=1)
    keeper = (wave_index != grid_side // 2 * grid_side + grid_side // 2).astype(jnp.float32)
    return (wave_rows, keeper)

def local_terms(ext_pos, ext_kind, ext_live, neighbour_rows, embedding, radial_weight, mix_weight, self_weight, readout_weight, readout_vector, charge_weight):
    own_atoms = neighbour_rows.shape[1]
    kind_values = jnp.arange(embedding.shape[0]).astype(jnp.float32)
    one_hot = (ext_kind[:, None] == kind_values[None, :]).astype(jnp.float32)
    embedded = jnp.dot(one_hot, embedding, precision=highest)
    outgoing = jnp.dot(embedded, mix_weight, precision=highest) * ext_live[:, None]
    centre = ext_pos[:, :own_atoms]
    partner = jnp.take(ext_pos, neighbour_rows, axis=1)
    offsets = partner - centre[:, None, :]
    distance = jnp.sqrt(lax.optimization_barrier(jnp.sum(offsets * offsets, axis=0)) + softening)
    basis_count = radial_weight.shape[0]
    spacing = basis_reach / (basis_count - 1)
    centres = spacing * jnp.arange(basis_count).astype(jnp.float32)
    scaled = (distance[None, :, :] - centres[:, None, None]) / spacing
    envelope = 1.0 / (1.0 + (distance / envelope_reach) ** 4)
    radial_basis = jnp.exp(-scaled * scaled) * envelope[None, :, :]
    filters = jnp.einsum('bma,bc->mac', radial_basis, radial_weight, precision=highest)
    gathered = jnp.take(outgoing, neighbour_rows, axis=0)
    message = lax.optimization_barrier(jnp.sum(filters * gathered, axis=0))
    hidden = jax.nn.silu(jnp.dot(embedded[:own_atoms], self_weight, precision=highest) + message)
    own_live = ext_live[:own_atoms]
    readout = jnp.dot(jax.nn.silu(jnp.dot(hidden, readout_weight, precision=highest)), readout_vector, precision=highest)
    charges = jnp.dot(hidden, charge_weight, precision=highest) * own_live[:, None]
    return (jnp.sum(readout * own_live), charges)

def structure_terms(wave_rows, own_pos, charges):
    phase = jnp.dot(wave_rows, own_pos, precision=highest)
    cosine_sum = jnp.dot(jnp.cos(phase), charges, precision=highest)
    sine_sum = jnp.dot(jnp.sin(phase), charges, precision=highest)
    return (cosine_sum, sine_sum)

def pick_slots(table, slot_rows):
    return jnp.take_along_axis(table, slot_rows[None], axis=3)

def build_records(moved, species, counts, send_inplane, send_normal):
    live_slots = (jnp.arange(ATOMS_DEV)[None, :] < counts[:, None]).astype(jnp.float32).reshape(-1)
    records = jnp.concatenate([moved, species.astype(jnp.float32)[None, :], live_slots[None, :]], axis=0)
    records = records.reshape(5, N_GZ, N_XY, ATOMS_DEV)
    inplane_lists = send_inplane.reshape(2, N_GZ, N_XY, GXY)
    to_lower = pick_slots(records, inplane_lists[0])
    to_upper = pick_slots(records, inplane_lists[1])
    strip_index = jnp.arange(N_XY)
    box_x = N_XY * width_x
    row_pick = (jnp.arange(5) == 0).astype(jnp.float32)[:, None, None, None]
    at_start = (strip_index == 0).astype(jnp.float32)[None, None, :, None]
    at_end = (strip_index == N_XY - 1).astype(jnp.float32)[None, None, :, None]
    from_lower = jnp.roll(to_upper, 1, axis=2) - row_pick * box_x * at_start
    from_upper = jnp.roll(to_lower, -1, axis=2) + row_pick * box_x * at_end
    first_section = jnp.concatenate([records, from_lower, from_upper], axis=3)
    normal_lists = send_normal.reshape(2, N_GZ, N_XY, GGZ)
    to_below = pick_slots(first_section, normal_lists[0])
    to_above = pick_slots(first_section, normal_lists[1])
    zero_layer = jnp.zeros_like(to_below[:, :1])
    from_below = jnp.concatenate([zero_layer, to_above[:, :-1]], axis=1)
    from_above = jnp.concatenate([to_below[:, 1:], zero_layer], axis=1)
    padding = jnp.array([far_away, far_away, far_away, 0.0, 0.0], dtype=jnp.float32)[:, None, None, None]
    padding = jnp.broadcast_to(padding, (5, N_GZ, N_XY, 1))
    return jnp.concatenate([first_section, from_below, from_above, padding], axis=3)

def total_energy(moved, species, counts, neighbours, send_inplane, send_normal, embedding, radial_weight, mix_weight, self_weight, charge_weight, readout_weight, readout_vector, kernel_filter):
    extended = build_records(moved, species, counts, send_inplane, send_normal)
    domain_count = N_GZ * N_XY
    per_domain = jnp.moveaxis(extended.reshape(5, domain_count, EXT), 1, 0)
    domain_lists = jnp.moveaxis(neighbours.reshape(NEIGH, domain_count, ATOMS_DEV), 1, 0)
    wave_rows, keeper = wave_vectors(KGRID, N_GZ, N_XY)

    def one_domain(running, pieces):
        record, neighbour_rows = pieces
        local_sum, charges = local_terms(record[:3], record[3], record[4], neighbour_rows, embedding, radial_weight, mix_weight, self_weight, readout_weight, readout_vector, charge_weight)
        cosine_part, sine_part = structure_terms(wave_rows, record[:3, :ATOMS_DEV], charges)
        return ((running[0] + local_sum, running[1] + cosine_part, running[2] + sine_part), None)
    start_values = (jnp.zeros((), jnp.float32), jnp.zeros((NK, C), jnp.float32), jnp.zeros((NK, C), jnp.float32))
    finals, unused = lax.scan(jax.checkpoint(one_domain), start_values, (per_domain, domain_lists))
    local_total, cosine_sum, sine_sum = finals
    ewald = jnp.sum(keeper[:, None] * kernel_filter * (cosine_sum * cosine_sum + sine_sum * sine_sum)) / (2.0 * ATOMS)
    return local_total + ewald

def reference(positions, velocities, forces, species, counts, neighbours, send_inplane, send_normal, embedding, inverse_mass, radial_weight, mix_weight, self_weight, charge_weight, readout_weight, readout_vector, kernel_filter):
    mass_factor = inverse_mass[species]
    half_velocity = velocities + 0.5 * time_step * forces * mass_factor[None, :]
    moved = positions + time_step * half_velocity

    def energy_of(moved_now):
        return total_energy(moved_now, species, counts, neighbours, send_inplane, send_normal, embedding, radial_weight, mix_weight, self_weight, charge_weight, readout_weight, readout_vector, kernel_filter)
    energy_total, pullback = jax.vjp(energy_of, moved)
    gradient = pullback(jnp.ones((), jnp.float32))[0]
    forces_new = -gradient
    velocities_new = half_velocity + 0.5 * time_step * forces_new * mass_factor[None, :]
    return (moved, velocities_new, forces_new, energy_total / ATOMS)
```

```python
import functools
import math

import jax
import jax.numpy as jnp
from jax import lax
from jax.experimental import pallas as pl
from jax.experimental.pallas import tpu as pltpu
from jax.sharding import PartitionSpec as P

KGRID = 8

time_step = 0.5
width_x = 2.0
width_y = 4.0
width_z = 2.0
far_away = 1000.0
softening = 0.25
basis_reach = 6.0
envelope_reach = 4.0
highest = lax.Precision.HIGHEST
f32 = jnp.float32
bf16 = jnp.bfloat16
i32 = jnp.int32

ROW_KIND = 3
ROW_ID = 4
ROW_INPLANE = 5
ROW_ABOVE = 6
ROW_BELOW = 7
ROW_LISTS = 8
PAIR_BLOCKS = 6


def split(x):
    high = x.astype(bf16)
    return high, (x - high.astype(f32)).astype(bf16)


def mm(a, b):
    return jnp.dot(a, b, preferred_element_type=f32)


def mm_nt(a, b):
    return lax.dot_general(a, b, (((1,), (1,)), ((), ())), preferred_element_type=f32)


def left3(x):
    high, low = split(x)
    return jnp.concatenate([high, high, low], axis=1)


def right3(x):
    high, low = split(x)
    return jnp.concatenate([high, low, high], axis=0)


def lanes(shape):
    return lax.broadcasted_iota(i32, shape, len(shape) - 1)


def rows(shape):
    return lax.broadcasted_iota(i32, shape, len(shape) - 2)


def pick(table, index):
    return jnp.take_along_axis(table, index, axis=1)


def sigmoid(x):
    return 1.0 / (1.0 + jnp.exp(-x))


def cos_sin(turns):
    half = math.pi * (turns - jnp.floor(turns + 0.5))
    sq = half * half
    sine = half * (
        1.0
        + sq
        * (
            -1.0 / 6
            + sq * (1.0 / 120 + sq * (-1.0 / 5040 + sq * (1.0 / 362880 - sq / 39916800.0)))
        )
    )
    cosine = 1.0 + sq * (
        -0.5
        + sq
        * (
            1.0 / 24
            + sq
            * (-1.0 / 720 + sq * (1.0 / 40320 + sq * (-1.0 / 3628800 + sq / 479001600.0)))
        )
    )
    return 1.0 - 2.0 * sine * sine, 2.0 * sine * cosine


def phase_tables(record, layers, strips):
    shape = (KGRID, record.shape[1])
    number = rows(shape).astype(f32)
    centred = number - float(KGRID // 2)
    cos_x, sin_x = cos_sin(number * record[0:1] / (strips * width_x))
    cos_y, sin_y = cos_sin(centred * record[1:2] / width_y)
    cos_z, sin_z = cos_sin(centred * record[2:3] / (layers * width_z))
    cos_yz, sin_yz = [], []
    for k in range(KGRID):
        c, s = cos_y[k : k + 1], sin_y[k : k + 1]
        cos_yz.append(c * cos_z - s * sin_z)
        sin_yz.append(s * cos_z + c * sin_z)
    return cos_x, sin_x, jnp.concatenate(cos_yz, axis=0), jnp.concatenate(sin_yz, axis=0)


def store_phases(record, layers, strips, high_ref, low_ref, column, keep=None):
    cos_x, sin_x, cos_yz, sin_yz = phase_tables(record, layers, strips)
    side = KGRID * KGRID
    half = KGRID * side
    at = pl.ds(column, record.shape[1])
    for k in range(KGRID):
        c, s = cos_x[k : k + 1], sin_x[k : k + 1]
        cosine = c * cos_yz - s * sin_yz
        sine = s * cos_yz + c * sin_yz
        if keep is not None:
            keep[k * side : (k + 1) * side, :] = cosine
            keep[half + k * side : half + (k + 1) * side, :] = sine
        for value, start in ((cosine, k * side), (sine, half + k * side)):
            high, low = split(value)
            high_ref[start : start + side, at] = high
            low_ref[start : start + side, at] = low


def domain_of(index, here, sizes):
    layer, strip, step = here
    layers, strips = sizes
    g = lax.rem(layer - 1 + lax.rem(index, layers) + layers, layers)
    p = lax.rem(strip + step * (index // layers) + strips, strips)
    return g, p


def slot_of(g, p, here, sizes):
    layer, strip, step = here
    layers, strips = sizes
    x = p ^ strip
    return (g ^ layer) + layers * ((x >> 1) + (strips // 2) * (x & 1))


def position_here(strips):
    layer = lax.axis_index("gz").astype(i32)
    strip = lax.axis_index("xy").astype(i32)
    return layer, strip, 2 * (strip & 1) - 1


def pack_kernel(sizes, pos, vel, frc, spec, cnt, nbr, inplane, normal, mass, out):
    layers, strips = sizes
    own = pos.shape[1]
    layer, strip, _ = position_here(strips)
    kind = spec[...]
    factor = jnp.zeros(kind.shape, f32)
    for s in range(mass.shape[0]):
        factor = factor + jnp.where(kind == s, mass[s], 0.0)
    half_velocity = vel[...] + 0.5 * time_step * frc[...] * factor
    moved = pos[...] + time_step * half_velocity
    lane = lanes((1, own))
    code = jnp.where(lane < cnt[0], kind, -1).astype(f32)
    number = ((layer * strips + strip) * own + lane).astype(f32)
    out[0:3, :] = moved
    out[ROW_KIND : ROW_KIND + 1, :] = code
    out[ROW_ID : ROW_ID + 1, :] = number
    lists = inplane[...].astype(f32)
    width = lists.shape[1]
    out[ROW_INPLANE : ROW_BELOW + 1, :] = jnp.zeros((3, own), f32)
    out[ROW_INPLANE : ROW_INPLANE + 1, 0:width] = lists[1:2]
    out[ROW_INPLANE : ROW_INPLANE + 1, width : 2 * width] = lists[0:1]
    lists = normal[...].astype(f32)
    tall = lists.shape[1]
    out[ROW_ABOVE : ROW_ABOVE + 1, 2 * width : 2 * width + tall] = lists[1:2]
    out[ROW_BELOW : ROW_BELOW + 1, 0:tall] = lists[0:1]
    out[ROW_LISTS:, :] = nbr[...].astype(f32)


def pair_basis(u, b):
    t = u - b
    return t, jnp.exp(-(t * t))


def forward_kernel(
    sizes,
    dims,
    chunk,
    data,
    embedding,
    radial,
    mix,
    self_w,
    charge_w,
    readout_w,
    readout_v,
    s_out,
    pair_out,
    slope_out,
    readout_out,
    charge_out,
    first,
    high_ref,
    low_ref,
    q_ref,
    u_ref,
    w_ref,
    rex3,
    wcu3,
    rv_ref,
    energy_ref,
    near_layers,
):
    layers, strips = sizes
    own, width, tall, slots = dims
    here = position_here(strips)
    kinds = embedding.shape[0]
    basis = radial.shape[0]
    channels = embedding.shape[1]
    total = layers * (strips // 2)
    lane8 = lanes((8, own))
    row8 = rows((8, own))

    emb = embedding[...]
    mixed = jnp.dot(emb, mix[...], precision=highest, preferred_element_type=f32)
    selfed = jnp.dot(emb, self_w[...], precision=highest, preferred_element_type=f32)
    table = [mixed[s : s + 1] * radial[...] for s in range(kinds)]
    tail = -(-kinds // 16) * 16
    table.append(selfed)
    table.append(jnp.zeros((channels - kinds * basis - kinds, channels), f32))
    wide = jnp.concatenate(table, axis=0).T[:, : kinds * basis + tail]
    rex3[...] = left3(wide)
    wcu3[...] = left3(jnp.concatenate([charge_w[...].T, readout_w[...].T], axis=0))
    rv_ref[...] = jnp.broadcast_to(readout_v[...], (channels, channels)).T
    energy_ref[...] = jnp.zeros_like(energy_ref)

    def get(g, p):
        return data[slot_of(g, p, here, sizes), 0:8, :]

    box = strips * width_x

    def first_step(i, carry):
        g, p = domain_of(i, here, sizes)
        lower = get(g, lax.rem(p + strips - 1, strips))
        upper = get(g, lax.rem(p + 1, strips))
        at = jnp.broadcast_to(lower[ROW_INPLANE : ROW_INPLANE + 1], (8, own)).astype(i32)
        from_lower = pick(lower, at)
        at = jnp.broadcast_to(upper[ROW_INPLANE : ROW_INPLANE + 1], (8, own)).astype(i32)
        from_upper = pick(upper, at)
        down = jnp.where(p == 0, -box, 0.0)
        up = jnp.where(p == strips - 1, box, 0.0)
        shift = jnp.where(row8 == 0, jnp.where(lane8 < width, down, up), 0.0)
        first[i] = jnp.where(lane8 < width, from_lower, from_upper) + shift
        return carry

    lax.fori_loop(0, total, first_step, 0)

    bound = jnp.where((row8 == ROW_KIND) | (row8 == ROW_ID), -1.0, 0.0)
    padding = jnp.where(row8 < 3, far_away, -1.0)
    spacing = basis_reach / (basis - 1)

    def normal_ghosts(i, g, p, move, row):
        other = lax.rem(g + move + layers, layers)
        strip_start = (i // layers) * layers
        j = strip_start + lax.rem(i - strip_start + move + layers, layers)
        near = get(other, p)
        at = jnp.broadcast_to(near[row : row + 1], (8, own)).astype(i32)
        inside = at < own
        at = at & (own - 1)
        found = jnp.where(inside, pick(near, at), pick(first[j], at))
        beyond = (g + move < 0) | (g + move >= layers)
        return jnp.where(beyond, bound, found)

    def domain_step(i, place):
        g, p = domain_of(i, here, sizes)
        slot = slot_of(g, p, here, sizes)
        record = data[slot, 0:8, :]
        below = normal_ghosts(i, g, p, -1, ROW_ABOVE)
        above = normal_ghosts(i, g, p, 1, ROW_BELOW)
        parts = (
            record,
            jnp.where(lane8 < 2 * width, first[i], below),
            jnp.where(lane8 < tall, above, padding),
        )
        index = data[slot, ROW_LISTS : ROW_LISTS + slots, :].astype(i32)
        part = index // own
        at = index & (own - 1)

        def gathered(r):
            a, b, c = [pick(jnp.broadcast_to(q[r : r + 1], (slots, own)), at) for q in parts]
            return jnp.where(part == 0, a, jnp.where(part == 1, b, c))

        dx = gathered(0) - record[0:1]
        dy = gathered(1) - record[1:2]
        dz = gathered(2) - record[2:3]
        code = gathered(ROW_KIND)
        d = jnp.sqrt(dx * dx + dy * dy + dz * dz + softening)
        quarter = d * (1.0 / envelope_reach)
        square = quarter * quarter
        envelope = 1.0 / (1.0 + square * square)
        u_ref[...] = d * (1.0 / spacing)
        for s in range(kinds):
            w_ref[s] = jnp.where(code == float(s), envelope, 0.0)
        centre = rows((basis, own)).astype(f32)
        sums = [jnp.zeros((basis, own), f32) for s in range(kinds)]
        for m in range(slots):
            t, e = pair_basis(u_ref[m : m + 1, :], centre)
            for s in range(kinds):
                sums[s] = sums[s] + e * w_ref[s, m : m + 1, :]
        kind_row = record[ROW_KIND : ROW_KIND + 1]
        one_hot = jnp.where(rows((tail, own)).astype(f32) == kind_row, 1.0, 0.0)
        pre = mm(rex3[...], right3(jnp.concatenate(sums + [one_hot], axis=0)))
        gate = sigmoid(pre)
        hidden = pre * gate
        both = mm(wcu3[...], right3(hidden))
        live = kind_row >= 0.0
        charges = jnp.where(live, both[:channels], 0.0)
        readout = both[channels:]
        readout_gate = sigmoid(readout)
        scaled = jnp.where(live, rv_ref[...] * readout_gate, 0.0)
        local = scaled * readout
        energy_ref[...] += jnp.sum(local.reshape(channels // 8, 8, own), axis=0)
        column = pl.multiple_of(place * own, own)
        high, low = split(charges)
        q_ref[0:channels, pl.ds(column, own)] = high
        q_ref[channels : 2 * channels, pl.ds(column, own)] = low
        store_phases(record, layers, strips, high_ref, low_ref, column)

        strip_step = i // layers
        layer_step = lax.rem(i, layers)

        @pl.when((strip_step < 2) & (layer_step < near_layers))
        def _():
            j = strip_step * near_layers + layer_step
            pair_out[j, 0] = dx
            pair_out[j, 1] = dy
            pair_out[j, 2] = dz
            pair_out[j, 3] = code
            pair_out[j, 4] = gathered(ROW_ID)
            pair_out[j, 5] = d
            slope_out[j] = gate * (1.0 + pre * (1.0 - gate))
            readout_out[j] = scaled * (1.0 + readout * (1.0 - readout_gate))

        @pl.when((strip_step == 0) & (layer_step == 1))
        def _():
            charge_out[...] = charges

    def chunk_step(n, carry):
        def body(k, c):
            domain_step(n * chunk + k, k)
            return c

        lax.fori_loop(0, chunk, body, 0)
        wide_sum = mm_nt(high_ref[...], q_ref[...])
        part_sum = wide_sum[:, :channels] + wide_sum[:, channels:]
        part_sum = part_sum + mm_nt(low_ref[...], q_ref[0:channels, :])

        @pl.when(n == 0)
        def _():
            s_out[...] = part_sum

        @pl.when(n > 0)
        def _():
            s_out[...] += part_sum

        return carry

    lax.fori_loop(0, total // chunk, chunk_step, 0)
    zero_row = (KGRID // 2) * KGRID + KGRID // 2
    s_out[zero_row : zero_row + 1, :] = jnp.sum(energy_ref[...], axis=0, keepdims=True)


def backward_kernel(
    sizes,
    dims,
    all_atoms,
    near_layers,
    data,
    s_own,
    s_other,
    kernel_filter,
    embedding,
    radial,
    mix,
    charge_w,
    readout_w,
    pair_in,
    slope_in,
    readout_in,
    charge_in,
    own_out,
    other_out,
    energy_out,
    high_ref,
    low_ref,
    keep_ref,
    weight_ref,
    wt_ref,
    cg_ref,
    wb3,
    re3,
    b_ref,
    f_ref,
    t_ref,
    hot_ref,
    col_ref,
    sum_ref,
    centre_ref,
):
    layers, strips = sizes
    own, width, tall, slots = dims
    here = position_here(strips)
    layer, strip, step = here
    kinds = embedding.shape[0]
    basis = radial.shape[0]
    channels = embedding.shape[1]
    waves = KGRID**3
    domains = 2 * near_layers
    spacing = basis_reach / (basis - 1)
    zero_row = (KGRID // 2) * KGRID + KGRID // 2

    sums = s_own[...] + s_other[...]
    local = sums[zero_row : zero_row + 1]
    keeper = jnp.where(rows((waves, channels)) == zero_row, 0.0, 1.0 / all_atoms)
    scale = keeper * kernel_filter[...]
    weights = jnp.concatenate([scale, scale], axis=0) * sums
    ewald = jnp.sum(weights * sums, axis=0, keepdims=True)
    energy = jnp.sum(local + 0.5 * ewald, axis=1, keepdims=True)
    energy_out[...] = jnp.broadcast_to(energy / all_atoms, energy_out.shape)
    high, low = split(weights)
    weight_ref[:, 0:channels] = high
    weight_ref[:, channels : 2 * channels] = high
    weight_ref[:, 2 * channels : 3 * channels] = low
    turned = weights.T
    high, low = split(turned)
    wt_ref[0:channels, :] = high
    wt_ref[channels : 2 * channels, :] = low

    emb = embedding[...]
    mixed = jnp.dot(emb, mix[...], precision=highest, preferred_element_type=f32)
    re3[...] = left3(
        jnp.concatenate([mixed[s : s + 1] * radial[...] for s in range(kinds)], axis=0)
    )
    wb3[...] = left3(jnp.concatenate([charge_w[...], readout_w[...]], axis=1))

    for j in range(domains):
        i = (j // near_layers) * layers + j % near_layers
        g, p = domain_of(jnp.int32(i), here, sizes)
        record = data[slot_of(g, p, here, sizes), 0:8, :]
        store_phases(
            record, layers, strips, high_ref, low_ref, j * own, keep_ref if j == 1 else None
        )
    wide = mm(wt_ref[...], high_ref[...])
    cg_ref[...] = (
        wide[:channels] + wide[channels:] + mm(wt_ref[0:channels, :], low_ref[...])
    )

    base = ((layer * strips + (strip - (strip & 1))) * own).astype(f32)
    groups = 2 * own // 16
    sum_ref[...] = jnp.zeros_like(sum_ref)

    def domain_step(j, carry):
        i = (j // near_layers) * layers + lax.rem(j, near_layers)
        g, p = domain_of(i, here, sizes)
        record = data[slot_of(g, p, here, sizes), 0:8, :]
        live = record[ROW_KIND : ROW_KIND + 1] >= 0.0
        column = pl.multiple_of(j * own, own)
        grad = jnp.where(live, cg_ref[:, pl.ds(column, own)], 0.0)
        grad = mm(wb3[...], right3(jnp.concatenate([grad, readout_in[j]], axis=0)))
        grad = grad * slope_in[j]
        b_ref[...] = mm(re3[...], right3(grad))
        code = pair_in[j, 3]
        d = pair_in[j, 5]
        quarter = d * (1.0 / envelope_reach)
        square = quarter * quarter
        envelope = 1.0 / (1.0 + square * square)
        slope = -envelope * envelope * (4.0 / envelope_reach) * square * quarter
        lean = envelope * (-2.0 / spacing)
        u = d * (1.0 / spacing)
        same = [code == float(s) for s in range(kinds)]
        force = jnp.zeros((slots, own), f32)
        for b in range(basis):
            t, e = pair_basis(u, float(b))
            chosen = jnp.zeros((slots, own), f32)
            for s in range(kinds):
                k = s * basis + b
                chosen = jnp.where(same[s], b_ref[k : k + 1, :], chosen)
            force = force + e * (lean * t + slope) * chosen
        force = force / d
        target = (pair_in[j, 4] - base).astype(i32)
        t_ref[0] = target // 16
        t_ref[1] = target & 15
        for r in range(3):
            part = force * pair_in[j, r]
            high = part.astype(bf16).astype(f32)
            f_ref[2 * r] = high
            f_ref[2 * r + 1] = part - high

            @pl.when(j == 1)
            def _():
                centre_ref[r : r + 1, :] = jnp.sum(part, axis=0, keepdims=True)

        group = rows((groups, own))
        lane16 = rows((16, own))
        for m in range(slots):
            at = slice(m * own, (m + 1) * own)
            hit = t_ref[0, m : m + 1, :] == group
            for r in range(6):
                hot = jnp.where(hit, f_ref[r, m : m + 1, :], 0.0)
                hot_ref[r * groups : (r + 1) * groups, at] = hot.astype(bf16)
            col_ref[:, at] = jnp.where(t_ref[1, m : m + 1, :] == lane16, 1.0, 0.0).astype(bf16)
        sum_ref[...] += mm_nt(hot_ref[...], col_ref[...])
        return carry

    lax.fori_loop(0, domains, domain_step, 0)

    along = mm(weight_ref[...], right3(charge_in[...]))
    turn = keep_ref[0:waves, :] * along[waves:] - keep_ref[waves:, :] * along[:waves]
    index = lanes((8, waves))
    axis = rows((8, waves))
    part_x = (index // (KGRID * KGRID)).astype(f32) / (strips * width_x)
    part_y = ((index // KGRID) % KGRID - KGRID // 2).astype(f32) / width_y
    part_z = (index % KGRID - KGRID // 2).astype(f32) / (layers * width_z)
    wave = jnp.where(axis == 0, part_x, jnp.where(axis == 1, part_y, part_z))
    wave = jnp.where(axis < 3, wave * (2.0 * math.pi), 0.0)
    ewald_grad = mm(left3(wave), right3(turn))

    spread = jnp.where(rows((16, own)) == (lanes((16, own)) & 15), 1.0, 0.0)
    wide = jnp.dot(sum_ref[...], spread, precision=highest, preferred_element_type=f32)
    half = groups // 2
    mine = rows((half, own)) == lanes((half, own)) // 16
    zero = jnp.zeros((1, own), f32)
    sides = [[], []]
    for r in range(3):
        both = wide[2 * r * groups : (2 * r + 1) * groups]
        both = both + wide[(2 * r + 1) * groups : (2 * r + 2) * groups]
        for side in range(2):
            part = both[side * half : (side + 1) * half]
            sides[side].append(jnp.sum(jnp.where(mine, part, 0.0), axis=0, keepdims=True))
    sides = [jnp.concatenate(side + [zero] * 5, axis=0) for side in sides]
    odd = (strip & 1) == 1
    own_grad = jnp.where(odd, sides[1], sides[0])
    own_out[...] = own_grad + ewald_grad
    own_out[0:3, :] += -centre_ref[0:3, :]
    other_out[...] = jnp.where(odd, sides[0], sides[1])


def final_kernel(pos, vel, frc, spec, mass, own, other, moved_out, vel_out, frc_out):
    kind = spec[...]
    factor = jnp.zeros(kind.shape, f32)
    for s in range(mass.shape[0]):
        factor = factor + jnp.where(kind == s, mass[s], 0.0)
    half_velocity = vel[...] + 0.5 * time_step * frc[...] * factor
    moved_out[...] = pos[...] + time_step * half_velocity
    forces_new = -(own[0:3, :] + other[0:3, :])
    frc_out[...] = forces_new
    vel_out[...] = half_velocity + 0.5 * time_step * forces_new * factor


def exchange(x, axis, bit):
    count = lax.axis_size(axis)
    return lax.ppermute(x, axis, [(i, i ^ bit) for i in range(count)])


def local(
    positions,
    velocities,
    forces,
    species,
    counts,
    neighbours,
    send_inplane,
    send_normal,
    embedding,
    inverse_mass,
    radial_weight,
    mix_weight,
    self_weight,
    charge_weight,
    readout_weight,
    readout_vector,
    kernel_filter,
):
    layers = lax.axis_size("gz")
    strips = lax.axis_size("xy")
    sizes = (layers, strips)
    own = positions.shape[1]
    slots = neighbours.shape[0]
    dims = (own, send_inplane.shape[1], send_normal.shape[1], slots)
    channels = embedding.shape[1]
    kinds = embedding.shape[0]
    basis = radial_weight.shape[0]
    all_atoms = own * layers * strips
    waves = KGRID**3
    vmem = pl.BlockSpec(memory_space=pltpu.VMEM)
    smem = pl.BlockSpec(memory_space=pltpu.SMEM)
    params = pltpu.CompilerParams(vmem_limit_bytes=48 * 1024 * 1024)
    kind_row = species[None, :]

    block = pl.pallas_call(
        functools.partial(pack_kernel, sizes),
        out_shape=jax.ShapeDtypeStruct((ROW_LISTS + slots, own), f32),
        in_specs=[vmem] * 4 + [smem] + [vmem] * 3 + [smem],
        out_specs=vmem,
        name="pack",
    )(
        positions,
        velocities,
        forces,
        kind_row,
        counts,
        neighbours,
        send_inplane,
        send_normal,
        inverse_mass,
    )
    data = block[None]
    bit = 1
    while bit < layers:
        data = jnp.concatenate([data, exchange(data, "gz", bit)], axis=0)
        bit *= 2
    bit = 2
    while bit < strips:
        data = jnp.concatenate([data, exchange(data, "xy", bit)], axis=0)
        bit *= 2
    data = jnp.concatenate([data, exchange(data, "xy", 1)], axis=0)

    total = layers * (strips // 2)
    chunk = min(16, total)
    near_layers = min(3, layers)
    near = 2 * near_layers
    tail = -(-kinds // 16) * 16
    depth = kinds * basis + tail
    sums, pairs, slope, readout, charges = pl.pallas_call(
        functools.partial(
            lambda *refs: forward_kernel(sizes, dims, chunk, *refs, near_layers)
        ),
        out_shape=[
            jax.ShapeDtypeStruct((2 * waves, channels), f32),
            jax.ShapeDtypeStruct((near, PAIR_BLOCKS, slots, own), f32),
            jax.ShapeDtypeStruct((near, channels, own), f32),
            jax.ShapeDtypeStruct((near, channels, own), f32),
            jax.ShapeDtypeStruct((channels, own), f32),
        ],
        in_specs=[vmem] * 8,
        out_specs=[vmem] * 5,
        scratch_shapes=[
            pltpu.VMEM((total, 8, own), f32),
            pltpu.VMEM((2 * waves, chunk * own), bf16),
            pltpu.VMEM((2 * waves, chunk * own), bf16),
            pltpu.VMEM((2 * channels, chunk * own), bf16),
            pltpu.VMEM((slots, own), f32),
            pltpu.VMEM((kinds, slots, own), f32),
            pltpu.VMEM((channels, 3 * depth), bf16),
            pltpu.VMEM((2 * channels, 3 * channels), bf16),
            pltpu.VMEM((channels, channels), f32),
            pltpu.VMEM((8, own), f32),
        ],
        compiler_params=params,
        name="forward",
    )(
        data,
        embedding,
        radial_weight,
        mix_weight,
        self_weight,
        charge_weight,
        readout_weight,
        readout_vector[None, :],
    )
    other_sums = exchange(sums, "xy", 1)
    groups = 2 * own // 16
    own_grad, other_grad, energy = pl.pallas_call(
        functools.partial(backward_kernel, sizes, dims, all_atoms, near_layers),
        out_shape=[
            jax.ShapeDtypeStruct((8, own), f32),
            jax.ShapeDtypeStruct((8, own), f32),
            jax.ShapeDtypeStruct((1, channels), f32),
        ],
        in_specs=[vmem] * 13,
        out_specs=[vmem] * 3,
        scratch_shapes=[
            pltpu.VMEM((2 * waves, near * own), bf16),
            pltpu.VMEM((2 * waves, near * own), bf16),
            pltpu.VMEM((2 * waves, own), f32),
            pltpu.VMEM((2 * waves, 3 * channels), bf16),
            pltpu.VMEM((2 * channels, 2 * waves), bf16),
            pltpu.VMEM((channels, near * own), f32),
            pltpu.VMEM((channels, 6 * channels), bf16),
            pltpu.VMEM((kinds * basis, 3 * channels), bf16),
            pltpu.VMEM((kinds * basis, own), f32),
            pltpu.VMEM((6, slots, own), f32),
            pltpu.VMEM((2, slots, own), i32),
            pltpu.VMEM((6 * groups, slots * own), bf16),
            pltpu.VMEM((16, slots * own), bf16),
            pltpu.VMEM((6 * groups, 16), f32),
            pltpu.VMEM((8, own), f32),
        ],
        compiler_params=params,
        name="backward",
    )(
        data,
        sums,
        other_sums,
        kernel_filter,
        embedding,
        radial_weight,
        mix_weight,
        charge_weight,
        readout_weight,
        pairs,
        slope,
        readout,
        charges,
    )
    arrived = exchange(other_grad, "xy", 1)
    moved, velocities_new, forces_new = pl.pallas_call(
        final_kernel,
        out_shape=[jax.ShapeDtypeStruct((3, own), f32)] * 3,
        in_specs=[vmem] * 4 + [smem] + [vmem] * 2,
        out_specs=[vmem] * 3,
        name="final",
    )(positions, velocities, forces, kind_row, inverse_mass, own_grad, arrived)
    return (moved, velocities_new, forces_new, energy[0, 0])


def solution(mesh):
    return jax.shard_map(
        local,
        mesh=mesh,
        in_specs=(
            P(None, ("gz", "xy")),
            P(None, ("gz", "xy")),
            P(None, ("gz", "xy")),
            P(("gz", "xy")),
            P(("gz", "xy")),
            P(None, ("gz", "xy")),
            P(None, ("gz", "xy")),
            P(None, ("gz", "xy")),
            P(),
            P(),
            P(),
            P(),
            P(),
            P(),
            P(),
            P(),
            P(),
        ),
        out_specs=(P(None, ("gz", "xy")), P(None, ("gz", "xy")), P(None, ("gz", "xy")), P()),
        check_vma=False,
    )
```

```python
import functools
import math

import jax
import jax.numpy as jnp
from jax import lax
from jax.experimental import pallas as pl
from jax.experimental.pallas import tpu as pltpu
from jax.sharding import PartitionSpec as P

KGRID = 8

time_step = 0.5
width_x = 2.0
width_y = 4.0
width_z = 2.0
far_away = 1000.0
softening = 0.25
basis_reach = 6.0
envelope_reach = 4.0
highest = lax.Precision.HIGHEST
f32 = jnp.float32
bf16 = jnp.bfloat16
i32 = jnp.int32

ROW_KIND = 3
ROW_ID = 4
ROW_INPLANE = 5
ROW_ABOVE = 6
ROW_BELOW = 7
ROW_LISTS = 8
PAIR_BLOCKS = 6


def split(x):
    high = x.astype(bf16)
    return high, (x - high.astype(f32)).astype(bf16)


def mm(a, b):
    return jnp.dot(a, b, preferred_element_type=f32)


def mm_nt(a, b):
    return lax.dot_general(a, b, (((1,), (1,)), ((), ())), preferred_element_type=f32)


def left3(x):
    high, low = split(x)
    return jnp.concatenate([high, high, low], axis=1)


def right3(x):
    high, low = split(x)
    return jnp.concatenate([high, low, high], axis=0)


def lanes(shape):
    return lax.broadcasted_iota(i32, shape, len(shape) - 1)


def rows(shape):
    return lax.broadcasted_iota(i32, shape, len(shape) - 2)


def pick(table, index):
    return jnp.take_along_axis(table, index, axis=1)


def sigmoid(x):
    return 1.0 / (1.0 + jnp.exp(-x))


def cos_sin(turns):
    half = math.pi * (turns - jnp.floor(turns + 0.5))
    sq = half * half
    sine = half * (
        1.0
        + sq
        * (
            -1.0 / 6
            + sq * (1.0 / 120 + sq * (-1.0 / 5040 + sq * (1.0 / 362880 - sq / 39916800.0)))
        )
    )
    cosine = 1.0 + sq * (
        -0.5
        + sq
        * (
            1.0 / 24
            + sq
            * (-1.0 / 720 + sq * (1.0 / 40320 + sq * (-1.0 / 3628800 + sq / 479001600.0)))
        )
    )
    return 1.0 - 2.0 * sine * sine, 2.0 * sine * cosine


def phase_tables(record, layers, strips):
    shape = (KGRID, record.shape[1])
    number = rows(shape).astype(f32)
    centred = number - float(KGRID // 2)
    cos_x, sin_x = cos_sin(number * record[0:1] / (strips * width_x))
    cos_y, sin_y = cos_sin(centred * record[1:2] / width_y)
    cos_z, sin_z = cos_sin(centred * record[2:3] / (layers * width_z))
    cos_yz, sin_yz = [], []
    for k in range(KGRID):
        c, s = cos_y[k : k + 1], sin_y[k : k + 1]
        cos_yz.append(c * cos_z - s * sin_z)
        sin_yz.append(s * cos_z + c * sin_z)
    return cos_x, sin_x, jnp.concatenate(cos_yz, axis=0), jnp.concatenate(sin_yz, axis=0)


def store_phases(record, layers, strips, refs, column):
    cos_high, cos_low, sin_high, sin_low = refs
    cos_x, sin_x, cos_yz, sin_yz = phase_tables(record, layers, strips)
    side = KGRID * KGRID
    at = pl.ds(column, record.shape[1])
    for k in range(KGRID):
        c, s = cos_x[k : k + 1], sin_x[k : k + 1]
        cosine = c * cos_yz - s * sin_yz
        sine = s * cos_yz + c * sin_yz
        here = slice(k * side, (k + 1) * side)
        cos_high[here, at], cos_low[here, at] = split(cosine)
        sin_high[here, at], sin_low[here, at] = split(sine)


def domain_at(slot, here, sizes):
    layer, strip = here
    layers, strips = sizes
    return layer ^ (slot & (layers - 1)), strip ^ (2 * (slot // layers))


def slot_of(g, p, here, sizes):
    layer, strip = here
    layers, strips = sizes
    return (g ^ layer) + layers * ((p ^ strip) >> 1)


def near_domain(j, here, sizes, near_layers):
    layer, strip = here
    layers, strips = sizes
    g = lax.rem(layer - 1 + j % near_layers + layers, layers)
    step = (j // near_layers) * (2 - 4 * (strip & 1))
    return g, lax.rem(strip + step + strips, strips)


def position_here():
    return lax.axis_index("gz").astype(i32), lax.axis_index("xy").astype(i32)


def mass_of(kind, mass):
    factor = jnp.zeros(kind.shape, f32)
    for s in range(mass.shape[0]):
        factor = factor + jnp.where(kind == s, mass[s], 0.0)
    return factor


def pack_kernel(sizes, pos, vel, frc, spec, cnt, nbr, inplane, normal, mass, out):
    layers, strips = sizes
    own = pos.shape[1]
    layer, strip = position_here()
    kind = spec[...]
    half_velocity = vel[...] + 0.5 * time_step * frc[...] * mass_of(kind, mass)
    moved = pos[...] + time_step * half_velocity
    lane = lanes((1, own))
    code = jnp.where(lane < cnt[0], kind, -1).astype(f32)
    number = ((layer * strips + strip) * own + lane).astype(f32)
    out[0:3, :] = moved
    out[ROW_KIND : ROW_KIND + 1, :] = code
    out[ROW_ID : ROW_ID + 1, :] = number
    lists = inplane[...].astype(f32)
    width = lists.shape[1]
    out[ROW_INPLANE : ROW_BELOW + 1, :] = jnp.zeros((3, own), f32)
    out[ROW_INPLANE : ROW_INPLANE + 1, 0:width] = lists[1:2]
    out[ROW_INPLANE : ROW_INPLANE + 1, width : 2 * width] = lists[0:1]
    lists = normal[...].astype(f32)
    tall = lists.shape[1]
    out[ROW_ABOVE : ROW_ABOVE + 1, 2 * width : 2 * width + tall] = lists[1:2]
    out[ROW_BELOW : ROW_BELOW + 1, 0:tall] = lists[0:1]
    out[ROW_LISTS:, :] = nbr[...].astype(f32)


def weights_kernel(
    embedding, radial, mix, self_w, charge_w, readout_w, readout_v, rex3, wcu3, wb3, re3, rv_out
):
    kinds, channels = embedding.shape
    basis = radial.shape[0]
    emb = embedding[...]
    mixed = jnp.dot(emb, mix[...], precision=highest, preferred_element_type=f32)
    selfed = jnp.dot(emb, self_w[...], precision=highest, preferred_element_type=f32)
    table = jnp.concatenate([mixed[s : s + 1] * radial[...] for s in range(kinds)], axis=0)
    re3[...] = left3(table)
    rest = jnp.zeros((channels - kinds * basis - kinds, channels), f32)
    wide = jnp.concatenate([table, selfed, rest], axis=0).T
    rex3[...] = left3(wide[:, : rex3.shape[1] // 3])
    wcu3[...] = left3(jnp.concatenate([charge_w[...].T, readout_w[...].T], axis=0))
    wb3[...] = left3(jnp.concatenate([charge_w[...], readout_w[...]], axis=1))
    rv_out[...] = jnp.broadcast_to(readout_v[...], (channels, channels)).T


def tables_kernel(sizes, data, *refs):
    own = data.shape[2]
    for n in range(data.shape[0]):
        store_phases(data[n, 0:8, :], *sizes, refs, n * own)


def pair_basis(u, b):
    t = u - b
    return t, jnp.exp(-(t * t))


def forward_kernel(
    sizes,
    dims,
    group,
    near_layers,
    early,
    mine,
    theirs,
    rex3,
    wcu3,
    rv_ref,
    radial,
    q_out,
    energy_out,
    pair_out,
    slope_out,
    readout_out,
    *rest,
):
    layers, strips = sizes
    own, width, tall, slots, kinds = dims
    if early:
        first, u_ref, w_ref, x_ref, energy_ref = rest
    else:
        cos_out, sin_out, first, u_ref, w_ref, x_ref, energy_ref, *tables = rest
    here = position_here()
    basis = radial.shape[0]
    channels = rv_ref.shape[0]
    total = mine.shape[0]
    near = 2 * near_layers
    lane8 = lanes((8, own))
    row8 = rows((8, own))
    energy_ref[...] = jnp.zeros_like(energy_ref)
    box = strips * width_x
    partner = (here[0], here[1] ^ 1)

    def first_step(i):
        g, p = domain_at(i, here, sizes)
        lower = theirs[slot_of(g, lax.rem(p + strips - 1, strips), partner, sizes)]
        upper = theirs[slot_of(g, lax.rem(p + 1, strips), partner, sizes)]
        at = jnp.broadcast_to(lower[ROW_INPLANE : ROW_INPLANE + 1], (8, own)).astype(i32)
        from_lower = pick(lower, at)
        at = jnp.broadcast_to(upper[ROW_INPLANE : ROW_INPLANE + 1], (8, own)).astype(i32)
        from_upper = pick(upper, at)
        down = jnp.where(p == 0, -box, 0.0)
        up = jnp.where(p == strips - 1, box, 0.0)
        shift = jnp.where(row8 == 0, jnp.where(lane8 < width, down, up), 0.0)
        first[i] = jnp.where(lane8 < width, from_lower, from_upper) + shift

    def first_steps(n, carry):
        for k in range(group):
            first_step(n * group + k)
        return carry

    lax.fori_loop(0, total // group, first_steps, 0)

    bound = jnp.where((row8 == ROW_KIND) | (row8 == ROW_ID), -1.0, 0.0)
    padding = jnp.where(row8 < 3, far_away, -1.0)
    spacing = basis_reach / (basis - 1)

    def normal_ghosts(g, p, move, row):
        other = lax.rem(g + move + layers, layers)
        j = slot_of(other, p, here, sizes)
        near_by = mine[j, 0:8, :]
        at = jnp.broadcast_to(near_by[row : row + 1], (8, own)).astype(i32)
        inside = at < own
        at = at & (own - 1)
        found = jnp.where(inside, pick(near_by, at), pick(first[j], at))
        beyond = (g + move < 0) | (g + move >= layers)
        return jnp.where(beyond, bound, found)

    def geometry(i, k):
        g, p = domain_at(i, here, sizes)
        record = mine[i, 0:8, :]
        below = normal_ghosts(g, p, -1, ROW_ABOVE)
        above = normal_ghosts(g, p, 1, ROW_BELOW)
        parts = (
            record,
            jnp.where(lane8 < 2 * width, first[i], below),
            jnp.where(lane8 < tall, above, padding),
        )
        index = mine[i, ROW_LISTS : ROW_LISTS + slots, :].astype(i32)
        part = index // own
        at = index & (own - 1)

        def gathered(r):
            a, b, c = [pick(jnp.broadcast_to(q[r : r + 1], (slots, own)), at) for q in parts]
            return jnp.where(part == 0, a, jnp.where(part == 1, b, c))

        dx = gathered(0) - record[0:1]
        dy = gathered(1) - record[1:2]
        dz = gathered(2) - record[2:3]
        code = gathered(ROW_KIND)
        d = jnp.sqrt(dx * dx + dy * dy + dz * dz + softening)
        quarter = d * (1.0 / envelope_reach)
        square = quarter * quarter
        envelope = 1.0 / (1.0 + square * square)
        u_ref[k] = d * (1.0 / spacing)
        for s in range(kinds):
            w_ref[k, s] = jnp.where(code == float(s), envelope, 0.0)
        turn = lax.rem(g - here[0] + 1 + layers, layers)
        side = here[1] + 2 - 4 * (here[1] & 1)
        strip_step = jnp.where(p == here[1], 0, jnp.where(p == lax.rem(side + strips, strips), 1, 2))
        j = jnp.where((turn < near_layers) & (strip_step < 2), strip_step * near_layers + turn, near)
        pair_out[j, 0] = dx
        pair_out[j, 1] = dy
        pair_out[j, 2] = dz
        pair_out[j, 3] = code
        pair_out[j, 4] = gathered(ROW_ID)
        pair_out[j, 5] = d
        return record[ROW_KIND : ROW_KIND + 1], j

    def basis_sums(k, kind_row):
        centre = rows((basis, own)).astype(f32)
        sums = [jnp.zeros((basis, own), f32) for s in range(kinds)]
        for m in range(slots):
            t, e = pair_basis(u_ref[k, m : m + 1, :], centre)
            for s in range(kinds):
                sums[s] = sums[s] + e * w_ref[k, s, m : m + 1, :]
        tail = x_ref.shape[0] // 3 - kinds * basis
        one_hot = jnp.where(rows((tail, own)).astype(f32) == kind_row, 1.0, 0.0)
        x_ref[:, k * own : (k + 1) * own] = right3(jnp.concatenate(sums + [one_hot], axis=0))

    def group_step(n, place):
        start = n * group
        found = [geometry(start + k, k) for k in range(group)]
        for k in range(group):
            basis_sums(k, found[k][0])
        live = jnp.concatenate([kind_row for kind_row, _ in found], axis=1) >= 0.0
        pre = mm(rex3[...], x_ref[...])
        gate = sigmoid(pre)
        hidden = pre * gate
        both = mm(wcu3[...], right3(hidden))
        charges = jnp.where(live, both[:channels], 0.0)
        readout = both[channels:]
        readout_gate = sigmoid(readout)
        rv = jnp.concatenate([rv_ref[...]] * group, axis=1)
        scaled = jnp.where(live, rv * readout_gate, 0.0)
        local = scaled * readout
        slope = gate * (1.0 + pre * (1.0 - gate))
        back = scaled * (1.0 + readout * (1.0 - readout_gate))
        wide = jnp.sum(local.reshape(channels // 8, 8, group * own), axis=0)
        for k in range(group):
            energy_ref[...] += wide[:, k * own : (k + 1) * own]
        column = pl.multiple_of(place * own, own)
        high, low = split(charges)
        q_out[0:channels, pl.ds(column, group * own)] = high
        q_out[channels : 2 * channels, pl.ds(column, group * own)] = low
        for k in range(group):
            column = pl.multiple_of(found[k][1] * own, own)
            slope_out[:, pl.ds(column, own)] = slope[:, k * own : (k + 1) * own]
            readout_out[:, pl.ds(column, own)] = back[:, k * own : (k + 1) * own]

    if early:

        def steps(n, carry):
            group_step(n, n * group)
            return carry

        lax.fori_loop(0, total // group, steps, 0)
    else:
        chunk = q_out.shape[1] // own

        def chunk_step(c, carry):
            def steps(n, inner):
                group_step(c * (chunk // group) + n, n * group)
                return inner

            def phases(n, inner):
                record = mine[c * chunk + n, 0:8, :]
                store_phases(record, layers, strips, tables, pl.multiple_of(n * own, own))
                return inner

            lax.fori_loop(0, chunk // group, steps, 0)
            lax.fori_loop(0, chunk, phases, 0)
            for out, high, low in ((cos_out, *tables[:2]), (sin_out, *tables[2:])):
                part = structure_part(high, low, q_out, 0)

                @pl.when(c == 0)
                def _():
                    out[...] = part

                @pl.when(c > 0)
                def _():
                    out[...] += part

            return carry

        lax.fori_loop(0, total // chunk, chunk_step, 0)
    energy_out[...] = jnp.sum(energy_ref[...], axis=0, keepdims=True)
    if not early:
        cos_out[zero_row : zero_row + 1, :] = energy_out[...]


zero_row = (KGRID // 2) * KGRID + KGRID // 2


def structure_part(high, low, q, column):
    channels = q.shape[0] // 2
    at = slice(column, column + high.shape[1])
    wide = mm_nt(high[...], q[:, at])
    return wide[:, :channels] + wide[:, channels:] + mm_nt(low[...], q[0:channels, at])


def structure_kernel(first_half, chunks, *refs):
    *tables, q, energy, out = refs
    column = 0
    part = None
    for n in range(chunks):
        high, low = tables[2 * n : 2 * n + 2]
        more = structure_part(high, low, q, column)
        part = more if part is None else part + more
        column += high.shape[1]
    out[...] = part
    if first_half:
        out[zero_row : zero_row + 1, :] = energy[...]


def near_kernel(sizes, near_layers, basis, kinds, starts, mine, pairs, *refs):
    layers, strips = sizes
    *tables, cos_high, cos_low, sin_high, sin_low, live_out, fall_out = refs
    own = mine.shape[2]
    here = position_here()
    spacing = basis_reach / (basis - 1)
    outs = (cos_high, cos_low, sin_high, sin_low)
    for j in range(2 * near_layers):
        at = slice(j * own, (j + 1) * own)
        slot = slot_of(*near_domain(j, here, sizes, near_layers), here, sizes)
        record = mine[slot, 0:8, :]
        live = jnp.where(record[ROW_KIND : ROW_KIND + 1] >= 0.0, 1.0, 0.0)
        live_out[:, at] = jnp.broadcast_to(live, (8, own))
        if not starts:
            store_phases(record, layers, strips, outs, j * own)
        for n, start in enumerate(starts):
            parts = tables[4 * n : 4 * n + 4]
            if j < near_layers and n > 0:
                continue
            if j >= near_layers and n == 0:
                continue
            end = start + parts[0].shape[1] // own

            @pl.when((slot >= start) & (slot < end))
            def _():
                column = pl.multiple_of((slot - start) * own, own)
                for part, out in zip(parts, outs):
                    out[:, at] = part[:, pl.ds(column, own)]

        d = pairs[j, 5]
        quarter = d * (1.0 / envelope_reach)
        square = quarter * quarter
        envelope = 1.0 / (1.0 + square * square)
        over = 1.0 / d
        slope = -envelope * envelope * (4.0 / envelope_reach) * square * quarter * over
        lean = envelope * (-2.0 / spacing) * over
        u = d * (1.0 / spacing)
        for b in range(basis):
            t, e = pair_basis(u, float(b))
            fall_out[j, b] = e * (lean * t + slope)


def backward_kernel(
    sizes,
    dims,
    all_atoms,
    near_layers,
    cos_own,
    cos_other,
    sin_own,
    sin_other,
    kernel_filter,
    cos_high,
    cos_low,
    sin_high,
    sin_low,
    live_in,
    fall_in,
    wb3,
    re3,
    pair_in,
    slope_in,
    readout_in,
    q_in,
    own_out,
    other_out,
    energy_out,
    weight_ref,
    b_ref,
    f_ref,
    t_ref,
    hot_ref,
    col_ref,
):
    layers, strips = sizes
    own, width, tall, slots, kinds = dims
    layer, strip = position_here()
    basis = fall_in.shape[1]
    channels = slope_in.shape[0]
    waves = KGRID**3
    domains = 2 * near_layers
    lanes_all = domains * own

    cos_sum = cos_own[...] + cos_other[...]
    sin_sum = sin_own[...] + sin_other[...]
    local = cos_sum[zero_row : zero_row + 1]
    keeper = jnp.where(rows((waves, channels)) == zero_row, 0.0, 1.0 / all_atoms)
    scale = keeper * kernel_filter[...]
    weight_cos = scale * cos_sum
    weight_sin = scale * sin_sum
    ewald = jnp.sum(weight_cos * cos_sum + weight_sin * sin_sum, axis=0, keepdims=True)
    energy = jnp.sum(local + 0.5 * ewald, axis=1, keepdims=True)
    energy_out[...] = jnp.broadcast_to(energy / all_atoms, energy_out.shape)

    grad = None
    for n, (weight, high, low) in enumerate(
        ((weight_cos, cos_high, cos_low), (weight_sin, sin_high, sin_low))
    ):
        top, bottom = split(weight.T)
        wide = mm(jnp.concatenate([top, bottom], axis=0), high[...])
        part = wide[:channels] + wide[channels:] + mm(top, low[...])
        grad = part if grad is None else grad + part
        weight_ref[n * waves : (n + 1) * waves, :] = left3(weight)
    grad = grad * live_in[0:1, :]
    both = jnp.concatenate([grad, readout_in[:, 0:lanes_all]], axis=0)
    grad = mm(wb3[...], right3(both)) * slope_in[:, 0:lanes_all]
    b_ref[...] = mm(re3[...], right3(grad))

    mine = slice(own, 2 * own)
    charge_high = q_in[0:channels, 0:own]
    charge_low = q_in[channels : 2 * channels, 0:own]
    along = mm(
        weight_ref[...], jnp.concatenate([charge_high, charge_low, charge_high], axis=0)
    )
    cosine = cos_high[:, mine].astype(f32) + cos_low[:, mine].astype(f32)
    sine = sin_high[:, mine].astype(f32) + sin_low[:, mine].astype(f32)
    turn = cosine * along[waves:] - sine * along[:waves]
    index = lanes((8, waves))
    axis = rows((8, waves))
    part_x = (index // (KGRID * KGRID)).astype(f32) / (strips * width_x)
    part_y = ((index // KGRID) % KGRID - KGRID // 2).astype(f32) / width_y
    part_z = (index % KGRID - KGRID // 2).astype(f32) / (layers * width_z)
    wave = jnp.where(axis == 0, part_x, jnp.where(axis == 1, part_y, part_z))
    wave = jnp.where(axis < 3, wave * (2.0 * math.pi), 0.0)
    own_out[...] = mm(left3(wave), right3(turn))

    base = ((layer * strips + (strip - (strip & 1))) * own).astype(f32)
    groups = 2 * own // 16
    group = rows((groups, own))
    lane16 = rows((16, own))
    for j in range(domains):
        code = pair_in[j, 3]
        same = [code == float(s) for s in range(kinds)]
        force = jnp.zeros((slots, own), f32)
        for b in range(basis):
            chosen = jnp.zeros((slots, own), f32)
            for s in range(kinds):
                k = s * basis + b
                row = b_ref[k : k + 1, j * own : (j + 1) * own]
                chosen = jnp.where(same[s], row, chosen)
            force = force + fall_in[j, b] * chosen
        target = (pair_in[j, 4] - base).astype(i32)
        t_ref[j, 0] = target // 16
        t_ref[j, 1] = target & 15
        for r in range(3):
            part = force * pair_in[j, r]
            high = part.astype(bf16).astype(f32)
            f_ref[j, 2 * r] = high
            f_ref[j, 2 * r + 1] = part - high
            if j == 1:
                own_out[r : r + 1, :] += -jnp.sum(part, axis=0, keepdims=True)
    for j in range(domains):
        for m in range(slots):
            at = slice((j * slots + m) * own, (j * slots + m + 1) * own)
            hit = t_ref[j, 0, m : m + 1, :] == group
            for r in range(6):
                hot = jnp.where(hit, f_ref[j, r, m : m + 1, :], 0.0)
                hot_ref[r * groups : (r + 1) * groups, at] = hot.astype(bf16)
            one = jnp.where(t_ref[j, 1, m : m + 1, :] == lane16, 1.0, 0.0)
            col_ref[:, at] = one.astype(bf16)
    found = mm_nt(hot_ref[...], col_ref[...])

    spread = jnp.where(rows((16, own)) == (lanes((16, own)) & 15), 1.0, 0.0)
    wide = jnp.dot(found, spread, precision=highest, preferred_element_type=f32)
    half = groups // 2
    fits = rows((half, own)) == lanes((half, own)) // 16
    odd = (strip & 1) == 1
    other_out[...] = jnp.zeros_like(other_out)
    for r in range(3):
        both = wide[2 * r * groups : (2 * r + 1) * groups]
        both = both + wide[(2 * r + 1) * groups : (2 * r + 2) * groups]
        sides = [
            jnp.sum(jnp.where(fits, both[n * half : (n + 1) * half], 0.0), axis=0, keepdims=True)
            for n in range(2)
        ]
        own_out[r : r + 1, :] += jnp.where(odd, sides[1], sides[0])
        other_out[r : r + 1, :] = jnp.where(odd, sides[0], sides[1])


def final_kernel(pos, vel, frc, spec, mass, own, other, moved_out, vel_out, frc_out):
    factor = mass_of(spec[...], mass)
    half_velocity = vel[...] + 0.5 * time_step * frc[...] * factor
    moved_out[...] = pos[...] + time_step * half_velocity
    forces_new = -(own[0:3, :] + other[0:3, :])
    frc_out[...] = forces_new
    vel_out[...] = half_velocity + 0.5 * time_step * forces_new * factor


def exchange(x, axis, bit):
    count = lax.axis_size(axis)
    return lax.ppermute(x, axis, [(i, i ^ bit) for i in range(count)])


MIB = 1024 * 1024
vmem = pl.BlockSpec(memory_space=pltpu.VMEM)
smem = pl.BlockSpec(memory_space=pltpu.SMEM)


def call(kernel, name, outs, ins, scratch=(), limit=8, scalars=(), work=10**8):
    return pl.pallas_call(
        kernel,
        out_shape=[jax.ShapeDtypeStruct(shape, dtype) for shape, dtype in outs],
        in_specs=[smem if n in scalars else vmem for n in range(len(ins))],
        out_specs=[vmem] * len(outs),
        scratch_shapes=[pltpu.VMEM(shape, dtype) for shape, dtype in scratch],
        compiler_params=pltpu.CompilerParams(vmem_limit_bytes=limit * MIB),
        cost_estimate=pl.CostEstimate(flops=work, bytes_accessed=MIB, transcendentals=0),
        name=name,
    )(*ins)


def local(
    positions,
    velocities,
    forces,
    species,
    counts,
    neighbours,
    send_inplane,
    send_normal,
    embedding,
    inverse_mass,
    radial_weight,
    mix_weight,
    self_weight,
    charge_weight,
    readout_weight,
    readout_vector,
    kernel_filter,
):
    layers = lax.axis_size("gz")
    strips = lax.axis_size("xy")
    sizes = (layers, strips)
    own = positions.shape[1]
    slots = neighbours.shape[0]
    kinds, channels = embedding.shape
    basis = radial_weight.shape[0]
    dims = (own, send_inplane.shape[1], send_normal.shape[1], slots, kinds)
    all_atoms = own * layers * strips
    waves = KGRID**3
    kind_row = species[None, :]
    total = layers * (strips // 2)
    early = total <= 16
    group = min(4, total)
    near_layers = min(3, layers)
    near = 2 * near_layers
    depth = kinds * basis + -(-kinds // 16) * 16

    (block,) = call(
        functools.partial(pack_kernel, sizes),
        "pack",
        [((ROW_LISTS + slots, own), f32)],
        (
            positions,
            velocities,
            forces,
            kind_row,
            counts,
            neighbours,
            send_inplane,
            send_normal,
            inverse_mass,
        ),
        scalars=(4, 8),
        limit=1,
    )
    rex3, wcu3, wb3, re3, rv = call(
        weights_kernel,
        "weights",
        [
            ((channels, 3 * depth), bf16),
            ((2 * channels, 3 * channels), bf16),
            ((channels, 6 * channels), bf16),
            ((kinds * basis, 3 * channels), bf16),
            ((channels, channels), f32),
        ],
        (
            embedding,
            radial_weight,
            mix_weight,
            self_weight,
            charge_weight,
            readout_weight,
            readout_vector[None, :],
        ),
    )

    def phases(data):
        wide = data.shape[0] * own
        return call(
            functools.partial(tables_kernel, sizes),
            "tables",
            [((waves, wide), bf16)] * 4,
            (data,),
        )

    data = block[None]
    bit = 1
    while bit < layers:
        data = jnp.concatenate([data, exchange(data, "gz", bit)], axis=0)
        bit *= 2
    tables, starts = [], []
    if early:
        tables.append(phases(data))
        starts.append(0)
    bit = 2
    while bit < strips:
        arrived = exchange(data, "xy", bit)
        if early:
            tables.append(phases(arrived))
            starts.append(data.shape[0])
        data = jnp.concatenate([data, arrived], axis=0)
        bit *= 2
    theirs = exchange(data[:, 0:8, :], "xy", 1)

    chunk = min(16, total)
    outs = [
        ((2 * channels, chunk * own), bf16),
        ((1, channels), f32),
        ((near + 1, PAIR_BLOCKS, slots, own), f32),
        ((channels, (near + 1) * own), f32),
        ((channels, (near + 1) * own), f32),
    ]
    scratch = [
        ((total, 8, own), f32),
        ((group, slots, own), f32),
        ((group, kinds, slots, own), f32),
        ((3 * depth, group * own), bf16),
        ((8, own), f32),
    ]
    if not early:
        outs += [((waves, channels), f32)] * 2
        scratch += [((waves, chunk * own), bf16)] * 4
    q, energy_row, pairs, slope, readout, *sums = call(
        functools.partial(forward_kernel, sizes, dims, group, near_layers, early),
        "forward",
        outs,
        (data, theirs, rex3, wcu3, rv, radial_weight),
        scratch,
        limit=16 if early else 48,
    )
    for n in range(2 if early else 0):
        parts = [t for table in tables for t in table[2 * n : 2 * n + 2]]
        sums += call(
            functools.partial(structure_kernel, n == 0, len(tables)),
            "structure",
            [((waves, channels), f32)],
            (*parts, q, energy_row),
            limit=16,
            work=10**9,
        )
    others = [exchange(part, "xy", 1) for part in sums]
    near_parts = call(
        functools.partial(near_kernel, sizes, near_layers, basis, kinds, starts),
        "near",
        [((waves, near * own), bf16)] * 4
        + [((8, near * own), f32), ((near, basis, slots, own), f32)],
        (data, pairs, *[t for table in tables for t in table]),
        limit=8 if early else 32,
    )
    groups = 2 * own // 16
    own_grad, other_grad, energy = call(
        functools.partial(backward_kernel, sizes, dims, all_atoms, near_layers),
        "backward",
        [((8, own), f32), ((8, own), f32), ((1, channels), f32)],
        (
            sums[0],
            others[0],
            sums[1],
            others[1],
            kernel_filter,
            *near_parts,
            wb3,
            re3,
            pairs,
            slope,
            readout,
            q,
        ),
        [
            ((2 * waves, 3 * channels), bf16),
            ((kinds * basis, near * own), f32),
            ((near, 6, slots, own), f32),
            ((near, 2, slots, own), i32),
            ((6 * groups, near * slots * own), bf16),
            ((16, near * slots * own), bf16),
        ],
        limit=24,
    )
    arrived = exchange(other_grad, "xy", 1)
    moved, velocities_new, forces_new = call(
        final_kernel,
        "final",
        [((3, own), f32)] * 3,
        (positions, velocities, forces, kind_row, inverse_mass, own_grad, arrived),
        scalars=(4,),
        limit=1,
    )
    return (moved, velocities_new, forces_new, energy[0, 0])


def solution(mesh):
    return jax.shard_map(
        local,
        mesh=mesh,
        in_specs=(
            P(None, ("gz", "xy")),
            P(None, ("gz", "xy")),
            P(None, ("gz", "xy")),
            P(("gz", "xy")),
            P(("gz", "xy")),
            P(None, ("gz", "xy")),
            P(None, ("gz", "xy")),
            P(None, ("gz", "xy")),
            P(),
            P(),
            P(),
            P(),
            P(),
            P(),
            P(),
            P(),
            P(),
        ),
        out_specs=(P(None, ("gz", "xy")), P(None, ("gz", "xy")), P(None, ("gz", "xy")), P()),
        check_vma=False,
    )
```

```python
import functools
import math

import jax
import jax.numpy as jnp
from jax import lax
from jax.experimental import pallas as pl
from jax.experimental.pallas import tpu as pltpu
from jax.sharding import PartitionSpec as P

KGRID = 8

time_step = 0.5
width_x = 2.0
width_y = 4.0
width_z = 2.0
far_away = 1000.0
softening = 0.25
basis_reach = 6.0
envelope_reach = 4.0
highest = lax.Precision.HIGHEST
f32 = jnp.float32
bf16 = jnp.bfloat16
i32 = jnp.int32

ROW_KIND = 3
ROW_ID = 4
ROW_INPLANE = 5
ROW_ABOVE = 6
ROW_BELOW = 7
ROW_LISTS = 8
PAIR_BLOCKS = 6


def split(x):
    high = x.astype(bf16)
    return high, (x - high.astype(f32)).astype(bf16)


def mm(a, b):
    return jnp.dot(a, b, preferred_element_type=f32)


def mm_nt(a, b):
    return lax.dot_general(a, b, (((1,), (1,)), ((), ())), preferred_element_type=f32)


def left3(x):
    high, low = split(x)
    return jnp.concatenate([high, high, low], axis=1)


def right3(x):
    high, low = split(x)
    return jnp.concatenate([high, low, high], axis=0)


def lanes(shape):
    return lax.broadcasted_iota(i32, shape, len(shape) - 1)


def rows(shape):
    return lax.broadcasted_iota(i32, shape, len(shape) - 2)


def pick(table, index):
    return jnp.take_along_axis(table, index, axis=1)


def sigmoid(x):
    return 1.0 / (1.0 + jnp.exp(-x))


def cos_sin(turns):
    half = math.pi * (turns - jnp.floor(turns + 0.5))
    sq = half * half
    sine = half * (
        1.0
        + sq
        * (
            -1.0 / 6
            + sq * (1.0 / 120 + sq * (-1.0 / 5040 + sq * (1.0 / 362880 - sq / 39916800.0)))
        )
    )
    cosine = 1.0 + sq * (
        -0.5
        + sq
        * (
            1.0 / 24
            + sq
            * (-1.0 / 720 + sq * (1.0 / 40320 + sq * (-1.0 / 3628800 + sq / 479001600.0)))
        )
    )
    return 1.0 - 2.0 * sine * sine, 2.0 * sine * cosine


def phase_tables(record, layers, strips):
    shape = (KGRID, record.shape[1])
    number = rows(shape).astype(f32)
    centred = number - float(KGRID // 2)
    cos_x, sin_x = cos_sin(number * record[0:1] / (strips * width_x))
    cos_y, sin_y = cos_sin(centred * record[1:2] / width_y)
    cos_z, sin_z = cos_sin(centred * record[2:3] / (layers * width_z))
    cos_yz, sin_yz = [], []
    for k in range(KGRID):
        c, s = cos_y[k : k + 1], sin_y[k : k + 1]
        cos_yz.append(c * cos_z - s * sin_z)
        sin_yz.append(s * cos_z + c * sin_z)
    return cos_x, sin_x, jnp.concatenate(cos_yz, axis=0), jnp.concatenate(sin_yz, axis=0)


def store_phases(record, layers, strips, refs, column):
    cos_high, cos_low, sin_high, sin_low = refs
    cos_x, sin_x, cos_yz, sin_yz = phase_tables(record, layers, strips)
    side = KGRID * KGRID
    at = pl.ds(column, record.shape[1])
    for k in range(KGRID):
        c, s = cos_x[k : k + 1], sin_x[k : k + 1]
        cosine = c * cos_yz - s * sin_yz
        sine = s * cos_yz + c * sin_yz
        here = slice(k * side, (k + 1) * side)
        cos_high[here, at], cos_low[here, at] = split(cosine)
        sin_high[here, at], sin_low[here, at] = split(sine)


def domain_at(slot, here, sizes):
    layer, strip = here
    layers, strips = sizes
    return layer ^ (slot & (layers - 1)), strip ^ (2 * (slot // layers))


def slot_of(g, p, here, sizes):
    layer, strip = here
    layers, strips = sizes
    return (g ^ layer) + layers * ((p ^ strip) >> 1)


def near_domain(j, here, sizes, near_layers):
    layer, strip = here
    layers, strips = sizes
    g = lax.rem(layer - 1 + j % near_layers + layers, layers)
    step = (j // near_layers) * (2 - 4 * (strip & 1))
    return g, lax.rem(strip + step + strips, strips)


def position_here():
    return lax.axis_index("gz").astype(i32), lax.axis_index("xy").astype(i32)


def mass_of(kind, mass):
    factor = jnp.zeros(kind.shape, f32)
    for s in range(mass.shape[0]):
        factor = factor + jnp.where(kind == s, mass[s], 0.0)
    return factor


def pack_kernel(sizes, cnt, mass, pos, vel, frc, spec, nbr, inplane, normal, out):
    layers, strips = sizes
    own = pos.shape[1]
    layer, strip = position_here()
    kind = spec[...]
    half_velocity = vel[...] + 0.5 * time_step * frc[...] * mass_of(kind, mass)
    moved = pos[...] + time_step * half_velocity
    lane = lanes((1, own))
    code = jnp.where(lane < cnt[0], kind, -1).astype(f32)
    number = ((layer * strips + strip) * own + lane).astype(f32)
    out[0:3, :] = moved
    out[ROW_KIND : ROW_KIND + 1, :] = code
    out[ROW_ID : ROW_ID + 1, :] = number
    lists = inplane[...].astype(f32)
    width = lists.shape[1]
    out[ROW_INPLANE : ROW_BELOW + 1, :] = jnp.zeros((3, own), f32)
    out[ROW_INPLANE : ROW_INPLANE + 1, 0:width] = lists[1:2]
    out[ROW_INPLANE : ROW_INPLANE + 1, width : 2 * width] = lists[0:1]
    lists = normal[...].astype(f32)
    tall = lists.shape[1]
    out[ROW_ABOVE : ROW_ABOVE + 1, 2 * width : 2 * width + tall] = lists[1:2]
    out[ROW_BELOW : ROW_BELOW + 1, 0:tall] = lists[0:1]
    out[ROW_LISTS:, :] = nbr[...].astype(f32)


def weights_kernel(
    embedding, radial, mix, self_w, charge_w, readout_w, readout_v, step, rex3, wcu3, wb3, re3, rv_out
):
    kinds, channels = embedding.shape
    basis = radial.shape[0]
    emb = embedding[...]
    mixed = jnp.dot(emb, mix[...], precision=highest, preferred_element_type=f32)
    selfed = jnp.dot(emb, self_w[...], precision=highest, preferred_element_type=f32)
    table = jnp.concatenate([mixed[s : s + 1] * radial[...] for s in range(kinds)], axis=0)
    re3[...] = left3(table)
    rest = jnp.zeros((channels - kinds * basis - kinds, channels), f32)
    wide = jnp.concatenate([table, selfed, rest], axis=0).T
    rex3[...] = left3(wide[:, : rex3.shape[1] // 3])
    wcu3[...] = left3(jnp.concatenate([charge_w[...].T, readout_w[...].T], axis=0))
    wb3[...] = left3(jnp.concatenate([charge_w[...], readout_w[...]], axis=1))
    rv_out[...] = jnp.broadcast_to(readout_v[...], (channels, channels)).T


def lift_kernel(block, out):
    out[0] = block[...]


def tables_kernel(sizes, data, *refs):
    own = data.shape[2]
    for n in range(data.shape[0]):
        store_phases(data[n, 0:8, :], *sizes, refs, n * own)


def pair_basis(u, b):
    t = u - b
    return t, jnp.exp(-(t * t))


def forward_kernel(
    sizes,
    dims,
    group,
    near_layers,
    early,
    mine,
    theirs,
    rex3,
    wcu3,
    rv_ref,
    radial,
    q_out,
    energy_out,
    pair_out,
    slope_out,
    readout_out,
    *rest,
):
    layers, strips = sizes
    own, width, tall, slots, kinds = dims
    if early:
        first, u_ref, w_ref, x_ref, energy_ref = rest
    else:
        cos_out, sin_out, first, u_ref, w_ref, x_ref, energy_ref, *tables = rest
    here = position_here()
    basis = radial.shape[0]
    channels = rv_ref.shape[0]
    total = mine.shape[0]
    near = 2 * near_layers
    lane8 = lanes((8, own))
    row8 = rows((8, own))
    energy_ref[...] = jnp.zeros_like(energy_ref)
    box = strips * width_x
    partner = (here[0], here[1] ^ 1)

    def first_step(i):
        g, p = domain_at(i, here, sizes)
        lower = theirs[slot_of(g, lax.rem(p + strips - 1, strips), partner, sizes)]
        upper = theirs[slot_of(g, lax.rem(p + 1, strips), partner, sizes)]
        at = jnp.broadcast_to(lower[ROW_INPLANE : ROW_INPLANE + 1], (8, own)).astype(i32)
        from_lower = pick(lower, at)
        at = jnp.broadcast_to(upper[ROW_INPLANE : ROW_INPLANE + 1], (8, own)).astype(i32)
        from_upper = pick(upper, at)
        down = jnp.where(p == 0, -box, 0.0)
        up = jnp.where(p == strips - 1, box, 0.0)
        shift = jnp.where(row8 == 0, jnp.where(lane8 < width, down, up), 0.0)
        first[i] = jnp.where(lane8 < width, from_lower, from_upper) + shift

    def first_steps(n, carry):
        for k in range(group):
            first_step(n * group + k)
        return carry

    lax.fori_loop(0, total // group, first_steps, 0)

    bound = jnp.where((row8 == ROW_KIND) | (row8 == ROW_ID), -1.0, 0.0)
    padding = jnp.where(row8 < 3, far_away, -1.0)
    spacing = basis_reach / (basis - 1)

    def normal_ghosts(g, p, move, row):
        other = lax.rem(g + move + layers, layers)
        j = slot_of(other, p, here, sizes)
        near_by = mine[j, 0:8, :]
        at = jnp.broadcast_to(near_by[row : row + 1], (8, own)).astype(i32)
        inside = at < own
        at = at & (own - 1)
        found = jnp.where(inside, pick(near_by, at), pick(first[j], at))
        beyond = (g + move < 0) | (g + move >= layers)
        return jnp.where(beyond, bound, found)

    def geometry(i, k):
        g, p = domain_at(i, here, sizes)
        record = mine[i, 0:8, :]
        below = normal_ghosts(g, p, -1, ROW_ABOVE)
        above = normal_ghosts(g, p, 1, ROW_BELOW)
        parts = (
            record,
            jnp.where(lane8 < 2 * width, first[i], below),
            jnp.where(lane8 < tall, above, padding),
        )
        index = mine[i, ROW_LISTS : ROW_LISTS + slots, :].astype(i32)
        part = index // own
        at = index & (own - 1)

        def gathered(r):
            a, b, c = [pick(jnp.broadcast_to(q[r : r + 1], (slots, own)), at) for q in parts]
            return jnp.where(part == 0, a, jnp.where(part == 1, b, c))

        dx = gathered(0) - record[0:1]
        dy = gathered(1) - record[1:2]
        dz = gathered(2) - record[2:3]
        code = gathered(ROW_KIND)
        d = jnp.sqrt(dx * dx + dy * dy + dz * dz + softening)
        quarter = d * (1.0 / envelope_reach)
        square = quarter * quarter
        envelope = 1.0 / (1.0 + square * square)
        u_ref[k] = d * (1.0 / spacing)
        for s in range(kinds):
            w_ref[k, s] = jnp.where(code == float(s), envelope, 0.0)
        turn = lax.rem(g - here[0] + 1 + layers, layers)
        side = here[1] + 2 - 4 * (here[1] & 1)
        strip_step = jnp.where(p == here[1], 0, jnp.where(p == lax.rem(side + strips, strips), 1, 2))
        j = jnp.where((turn < near_layers) & (strip_step < 2), strip_step * near_layers + turn, near)
        pair_out[j, 0] = dx
        pair_out[j, 1] = dy
        pair_out[j, 2] = dz
        pair_out[j, 3] = code
        pair_out[j, 4] = gathered(ROW_ID)
        pair_out[j, 5] = d
        return record[ROW_KIND : ROW_KIND + 1], j

    def basis_sums(k, kind_row):
        centre = rows((basis, own)).astype(f32)
        sums = [jnp.zeros((basis, own), f32) for s in range(kinds)]
        for m in range(slots):
            t, e = pair_basis(u_ref[k, m : m + 1, :], centre)
            for s in range(kinds):
                sums[s] = sums[s] + e * w_ref[k, s, m : m + 1, :]
        tail = x_ref.shape[0] // 3 - kinds * basis
        one_hot = jnp.where(rows((tail, own)).astype(f32) == kind_row, 1.0, 0.0)
        x_ref[:, k * own : (k + 1) * own] = right3(jnp.concatenate(sums + [one_hot], axis=0))

    def group_step(n, place):
        start = n * group
        found = [geometry(start + k, k) for k in range(group)]
        for k in range(group):
            basis_sums(k, found[k][0])
        live = jnp.concatenate([kind_row for kind_row, _ in found], axis=1) >= 0.0
        pre = mm(rex3[...], x_ref[...])
        gate = sigmoid(pre)
        hidden = pre * gate
        both = mm(wcu3[...], right3(hidden))
        charges = jnp.where(live, both[:channels], 0.0)
        readout = both[channels:]
        readout_gate = sigmoid(readout)
        rv = jnp.concatenate([rv_ref[...]] * group, axis=1)
        scaled = jnp.where(live, rv * readout_gate, 0.0)
        local = scaled * readout
        slope = gate * (1.0 + pre * (1.0 - gate))
        back = scaled * (1.0 + readout * (1.0 - readout_gate))
        wide = jnp.sum(local.reshape(channels // 8, 8, group * own), axis=0)
        for k in range(group):
            energy_ref[...] += wide[:, k * own : (k + 1) * own]
        column = pl.multiple_of(place * own, own)
        high, low = split(charges)
        q_out[0:channels, pl.ds(column, group * own)] = high
        q_out[channels : 2 * channels, pl.ds(column, group * own)] = low
        for k in range(group):
            column = pl.multiple_of(found[k][1] * own, own)
            slope_out[:, pl.ds(column, own)] = slope[:, k * own : (k + 1) * own]
            readout_out[:, pl.ds(column, own)] = back[:, k * own : (k + 1) * own]

    if early:

        def steps(n, carry):
            group_step(n, n * group)
            return carry

        lax.fori_loop(0, total // group, steps, 0)
    else:
        chunk = q_out.shape[1] // own

        def chunk_step(c, carry):
            def steps(n, inner):
                group_step(c * (chunk // group) + n, n * group)
                return inner

            def phases(n, inner):
                record = mine[c * chunk + n, 0:8, :]
                store_phases(record, layers, strips, tables, pl.multiple_of(n * own, own))
                return inner

            lax.fori_loop(0, chunk // group, steps, 0)
            lax.fori_loop(0, chunk, phases, 0)
            for out, high, low in ((cos_out, *tables[:2]), (sin_out, *tables[2:])):
                part = structure_part(high, low, q_out, 0)

                @pl.when(c == 0)
                def _():
                    out[...] = part

                @pl.when(c > 0)
                def _():
                    out[...] += part

            return carry

        lax.fori_loop(0, total // chunk, chunk_step, 0)
    energy_out[...] = jnp.sum(energy_ref[...], axis=0, keepdims=True)
    if not early:
        cos_out[zero_row : zero_row + 1, :] = energy_out[...]


zero_row = (KGRID // 2) * KGRID + KGRID // 2


def structure_part(high, low, q, column):
    channels = q.shape[0] // 2
    at = slice(column, column + high.shape[1])
    wide = mm_nt(high[...], q[:, at])
    return wide[:, :channels] + wide[:, channels:] + mm_nt(low[...], q[0:channels, at])


def structure_kernel(first_half, chunks, *refs):
    *tables, q, energy, out = refs
    column = 0
    part = None
    for n in range(chunks):
        high, low = tables[2 * n : 2 * n + 2]
        more = structure_part(high, low, q, column)
        part = more if part is None else part + more
        column += high.shape[1]
    out[...] = part
    if first_half:
        out[zero_row : zero_row + 1, :] = energy[...]


def near_kernel(sizes, near_layers, basis, kinds, starts, mine, pairs, *refs):
    layers, strips = sizes
    *tables, cos_high, cos_low, sin_high, sin_low, live_out, fall_out = refs
    own = mine.shape[2]
    here = position_here()
    spacing = basis_reach / (basis - 1)
    outs = (cos_high, cos_low, sin_high, sin_low)
    for j in range(2 * near_layers):
        at = slice(j * own, (j + 1) * own)
        slot = slot_of(*near_domain(j, here, sizes, near_layers), here, sizes)
        record = mine[slot, 0:8, :]
        live = jnp.where(record[ROW_KIND : ROW_KIND + 1] >= 0.0, 1.0, 0.0)
        live_out[:, at] = jnp.broadcast_to(live, (8, own))
        if not starts:
            store_phases(record, layers, strips, outs, j * own)
        for n, start in enumerate(starts):
            parts = tables[4 * n : 4 * n + 4]
            if j < near_layers and n > 0:
                continue
            if j >= near_layers and n == 0:
                continue
            end = start + parts[0].shape[1] // own

            @pl.when((slot >= start) & (slot < end))
            def _():
                column = pl.multiple_of((slot - start) * own, own)
                for part, out in zip(parts, outs):
                    out[:, at] = part[:, pl.ds(column, own)]

        d = pairs[j, 5]
        quarter = d * (1.0 / envelope_reach)
        square = quarter * quarter
        envelope = 1.0 / (1.0 + square * square)
        over = 1.0 / d
        slope = -envelope * envelope * (4.0 / envelope_reach) * square * quarter * over
        lean = envelope * (-2.0 / spacing) * over
        u = d * (1.0 / spacing)
        for b in range(basis):
            t, e = pair_basis(u, float(b))
            fall_out[j, b] = e * (lean * t + slope)


def backward_kernel(
    sizes,
    dims,
    all_atoms,
    near_layers,
    cos_own,
    cos_other,
    sin_own,
    sin_other,
    kernel_filter,
    cos_high,
    cos_low,
    sin_high,
    sin_low,
    live_in,
    fall_in,
    wb3,
    re3,
    pair_in,
    slope_in,
    readout_in,
    q_in,
    own_out,
    other_out,
    energy_out,
    weight_ref,
    b_ref,
    f_ref,
    t_ref,
    hot_ref,
    col_ref,
):
    layers, strips = sizes
    own, width, tall, slots, kinds = dims
    layer, strip = position_here()
    basis = fall_in.shape[1]
    channels = slope_in.shape[0]
    waves = KGRID**3
    domains = 2 * near_layers
    lanes_all = domains * own

    cos_sum = cos_own[...] + cos_other[...]
    sin_sum = sin_own[...] + sin_other[...]
    local = cos_sum[zero_row : zero_row + 1]
    keeper = jnp.where(rows((waves, channels)) == zero_row, 0.0, 1.0 / all_atoms)
    scale = keeper * kernel_filter[...]
    weight_cos = scale * cos_sum
    weight_sin = scale * sin_sum
    ewald = jnp.sum(weight_cos * cos_sum + weight_sin * sin_sum, axis=0, keepdims=True)
    energy = jnp.sum(local + 0.5 * ewald, axis=1, keepdims=True)
    energy_out[...] = jnp.broadcast_to(energy / all_atoms, energy_out.shape)

    grad = None
    for n, (weight, high, low) in enumerate(
        ((weight_cos, cos_high, cos_low), (weight_sin, sin_high, sin_low))
    ):
        top, bottom = split(weight.T)
        wide = mm(jnp.concatenate([top, bottom], axis=0), high[...])
        part = wide[:channels] + wide[channels:] + mm(top, low[...])
        grad = part if grad is None else grad + part
        weight_ref[n * waves : (n + 1) * waves, :] = left3(weight)
    grad = grad * live_in[0:1, :]
    both = jnp.concatenate([grad, readout_in[:, 0:lanes_all]], axis=0)
    grad = mm(wb3[...], right3(both)) * slope_in[:, 0:lanes_all]
    b_ref[...] = mm(re3[...], right3(grad))

    mine = slice(own, 2 * own)
    charge_high = q_in[0:channels, 0:own]
    charge_low = q_in[channels : 2 * channels, 0:own]
    along = mm(
        weight_ref[...], jnp.concatenate([charge_high, charge_low, charge_high], axis=0)
    )
    cosine = cos_high[:, mine].astype(f32) + cos_low[:, mine].astype(f32)
    sine = sin_high[:, mine].astype(f32) + sin_low[:, mine].astype(f32)
    turn = cosine * along[waves:] - sine * along[:waves]
    index = lanes((8, waves))
    axis = rows((8, waves))
    part_x = (index // (KGRID * KGRID)).astype(f32) / (strips * width_x)
    part_y = ((index // KGRID) % KGRID - KGRID // 2).astype(f32) / width_y
    part_z = (index % KGRID - KGRID // 2).astype(f32) / (layers * width_z)
    wave = jnp.where(axis == 0, part_x, jnp.where(axis == 1, part_y, part_z))
    wave = jnp.where(axis < 3, wave * (2.0 * math.pi), 0.0)
    own_out[...] = mm(left3(wave), right3(turn))

    base = ((layer * strips + (strip - (strip & 1))) * own).astype(f32)
    groups = 2 * own // 16
    group = rows((groups, own))
    lane16 = rows((16, own))
    for j in range(domains):
        code = pair_in[j, 3]
        same = [code == float(s) for s in range(kinds)]
        force = jnp.zeros((slots, own), f32)
        for b in range(basis):
            chosen = jnp.zeros((slots, own), f32)
            for s in range(kinds):
                k = s * basis + b
                row = b_ref[k : k + 1, j * own : (j + 1) * own]
                chosen = jnp.where(same[s], row, chosen)
            force = force + fall_in[j, b] * chosen
        target = (pair_in[j, 4] - base).astype(i32)
        t_ref[j, 0] = target // 16
        t_ref[j, 1] = target & 15
        for r in range(3):
            part = force * pair_in[j, r]
            high = part.astype(bf16).astype(f32)
            f_ref[j, 2 * r] = high
            f_ref[j, 2 * r + 1] = part - high
            if j == 1:
                own_out[r : r + 1, :] += -jnp.sum(part, axis=0, keepdims=True)
    for j in range(domains):
        for m in range(slots):
            at = slice((j * slots + m) * own, (j * slots + m + 1) * own)
            hit = t_ref[j, 0, m : m + 1, :] == group
            for r in range(6):
                hot = jnp.where(hit, f_ref[j, r, m : m + 1, :], 0.0)
                hot_ref[r * groups : (r + 1) * groups, at] = hot.astype(bf16)
            one = jnp.where(t_ref[j, 1, m : m + 1, :] == lane16, 1.0, 0.0)
            col_ref[:, at] = one.astype(bf16)
    found = mm_nt(hot_ref[...], col_ref[...])

    spread = jnp.where(rows((16, own)) == (lanes((16, own)) & 15), 1.0, 0.0)
    wide = jnp.dot(found, spread, precision=highest, preferred_element_type=f32)
    half = groups // 2
    fits = rows((half, own)) == lanes((half, own)) // 16
    odd = (strip & 1) == 1
    other_out[...] = jnp.zeros_like(other_out)
    for r in range(3):
        both = wide[2 * r * groups : (2 * r + 1) * groups]
        both = both + wide[(2 * r + 1) * groups : (2 * r + 2) * groups]
        sides = [
            jnp.sum(jnp.where(fits, both[n * half : (n + 1) * half], 0.0), axis=0, keepdims=True)
            for n in range(2)
        ]
        own_out[r : r + 1, :] += jnp.where(odd, sides[1], sides[0])
        other_out[r : r + 1, :] = jnp.where(odd, sides[0], sides[1])


def final_kernel(pos, vel, frc, spec, mass, own, other, moved_out, vel_out, frc_out):
    factor = mass_of(spec[...], mass)
    half_velocity = vel[...] + 0.5 * time_step * frc[...] * factor
    moved_out[...] = pos[...] + time_step * half_velocity
    forces_new = -(own[0:3, :] + other[0:3, :])
    frc_out[...] = forces_new
    vel_out[...] = half_velocity + 0.5 * time_step * forces_new * factor


def exchange(x, axis, bit):
    count = lax.axis_size(axis)
    return lax.ppermute(x, axis, [(i, i ^ bit) for i in range(count)])


MIB = 1024 * 1024
vmem = pl.BlockSpec(memory_space=pltpu.VMEM)
smem = pl.BlockSpec(memory_space=pltpu.SMEM)


def call(kernel, name, outs, ins, scratch=(), limit=8, scalars=(), unread=(), work=10**8):
    def spec(n):
        if n in unread:
            return pl.BlockSpec(memory_space=pl.ANY)
        return smem if n in scalars else vmem

    return pl.pallas_call(
        kernel,
        out_shape=[jax.ShapeDtypeStruct(shape, dtype) for shape, dtype in outs],
        in_specs=[spec(n) for n in range(len(ins))],
        out_specs=[vmem] * len(outs),
        scratch_shapes=[pltpu.VMEM(shape, dtype) for shape, dtype in scratch],
        compiler_params=pltpu.CompilerParams(vmem_limit_bytes=limit and limit * MIB),
        cost_estimate=pl.CostEstimate(flops=work, bytes_accessed=MIB, transcendentals=0),
        name=name,
    )(*ins)


def local(
    positions,
    velocities,
    forces,
    species,
    counts,
    neighbours,
    send_inplane,
    send_normal,
    embedding,
    inverse_mass,
    radial_weight,
    mix_weight,
    self_weight,
    charge_weight,
    readout_weight,
    readout_vector,
    kernel_filter,
):
    layers = lax.axis_size("gz")
    strips = lax.axis_size("xy")
    sizes = (layers, strips)
    own = positions.shape[1]
    slots = neighbours.shape[0]
    kinds, channels = embedding.shape
    basis = radial_weight.shape[0]
    dims = (own, send_inplane.shape[1], send_normal.shape[1], slots, kinds)
    all_atoms = own * layers * strips
    waves = KGRID**3
    kind_row = species[None, :]
    total = layers * (strips // 2)
    early = total <= 16
    group = min(4, total)
    near_layers = min(3, layers)
    near = 2 * near_layers
    depth = kinds * basis + -(-kinds // 16) * 16

    (block,) = call(
        functools.partial(pack_kernel, sizes),
        "pack",
        [((ROW_LISTS + slots, own), f32)],
        (
            counts,
            inverse_mass,
            positions,
            velocities,
            forces,
            kind_row,
            neighbours,
            send_inplane,
            send_normal,
        ),
        scalars=(0, 1),
        limit=None,
    )
    def phases(data):
        wide = data.shape[0] * own
        return call(
            functools.partial(tables_kernel, sizes),
            "tables",
            [((waves, wide), bf16)] * 4,
            (data,),
            work=4 * 10**9,
        )

    arrived = exchange(block, "gz", 1)[None]
    (data,) = call(
        lift_kernel, "lift", [((1, *block.shape), f32)], (block,), limit=1, work=8 * 10**9
    )
    data = jnp.concatenate([data, arrived], axis=0)
    rex3, wcu3, wb3, re3, rv = call(
        weights_kernel,
        "weights",
        [
            ((channels, 3 * depth), bf16),
            ((2 * channels, 3 * channels), bf16),
            ((channels, 6 * channels), bf16),
            ((kinds * basis, 3 * channels), bf16),
            ((channels, channels), f32),
        ],
        (
            embedding,
            radial_weight,
            mix_weight,
            self_weight,
            charge_weight,
            readout_weight,
            readout_vector[None, :],
            data,
        ),
        limit=None,
        unread=(7,),
        work=4 * 10**9,
    )

    bit = 2
    while bit < layers:
        data = jnp.concatenate([data, exchange(data, "gz", bit)], axis=0)
        bit *= 2
    tables, starts = [], []
    bit, fresh, start = 2, data, 0
    while bit < strips:
        arrived = exchange(data, "xy", bit)
        if early:
            tables.append(phases(fresh))
            starts.append(start)
            start = data.shape[0]
        data = jnp.concatenate([data, arrived], axis=0)
        fresh = arrived
        bit *= 2
    theirs = exchange(data[:, 0:8, :], "xy", 1)
    if early:
        tables.append(phases(fresh))
        starts.append(start)

    chunk = min(16, total)
    outs = [
        ((2 * channels, chunk * own), bf16),
        ((1, channels), f32),
        ((near + 1, PAIR_BLOCKS, slots, own), f32),
        ((channels, (near + 1) * own), f32),
        ((channels, (near + 1) * own), f32),
    ]
    scratch = [
        ((total, 8, own), f32),
        ((group, slots, own), f32),
        ((group, kinds, slots, own), f32),
        ((3 * depth, group * own), bf16),
        ((8, own), f32),
    ]
    if not early:
        outs += [((waves, channels), f32)] * 2
        scratch += [((waves, chunk * own), bf16)] * 4
    q, energy_row, pairs, slope, readout, *sums = call(
        functools.partial(forward_kernel, sizes, dims, group, near_layers, early),
        "forward",
        outs,
        (data, theirs, rex3, wcu3, rv, radial_weight),
        scratch,
        limit=16 if early else 48,
    )
    for n in range(2 if early else 0):
        parts = [t for table in tables for t in table[2 * n : 2 * n + 2]]
        sums += call(
            functools.partial(structure_kernel, n == 0, len(tables)),
            "structure",
            [((waves, channels), f32)],
            (*parts, q, energy_row),
            limit=16,
            work=10**9,
        )
    others = [exchange(part, "xy", 1) for part in sums]
    near_parts = call(
        functools.partial(near_kernel, sizes, near_layers, basis, kinds, starts),
        "near",
        [((waves, near * own), bf16)] * 4
        + [((8, near * own), f32), ((near, basis, slots, own), f32)],
        (data, pairs, *[t for table in tables for t in table]),
        limit=8 if early else 32,
    )
    groups = 2 * own // 16
    own_grad, other_grad, energy = call(
        functools.partial(backward_kernel, sizes, dims, all_atoms, near_layers),
        "backward",
        [((8, own), f32), ((8, own), f32), ((1, channels), f32)],
        (
            sums[0],
            others[0],
            sums[1],
            others[1],
            kernel_filter,
            *near_parts,
            wb3,
            re3,
            pairs,
            slope,
            readout,
            q,
        ),
        [
            ((2 * waves, 3 * channels), bf16),
            ((kinds * basis, near * own), f32),
            ((near, 6, slots, own), f32),
            ((near, 2, slots, own), i32),
            ((6 * groups, near * slots * own), bf16),
            ((16, near * slots * own), bf16),
        ],
        limit=24,
    )
    arrived = exchange(other_grad, "xy", 1)
    moved, velocities_new, forces_new = call(
        final_kernel,
        "final",
        [((3, own), f32)] * 3,
        (positions, velocities, forces, kind_row, inverse_mass, own_grad, arrived),
        scalars=(4,),
        limit=1,
    )
    return (moved, velocities_new, forces_new, energy[0, 0])


def solution(mesh):
    return jax.shard_map(
        local,
        mesh=mesh,
        in_specs=(
            P(None, ("gz", "xy")),
            P(None, ("gz", "xy")),
            P(None, ("gz", "xy")),
            P(("gz", "xy")),
            P(("gz", "xy")),
            P(None, ("gz", "xy")),
            P(None, ("gz", "xy")),
            P(None, ("gz", "xy")),
            P(),
            P(),
            P(),
            P(),
            P(),
            P(),
            P(),
            P(),
            P(),
        ),
        out_specs=(P(None, ("gz", "xy")), P(None, ("gz", "xy")), P(None, ("gz", "xy")), P()),
        check_vma=False,
    )
```

```python
import functools
import math

import jax
import jax.numpy as jnp
from jax import lax
from jax.experimental import pallas as pl
from jax.experimental.pallas import tpu as pltpu
from jax.sharding import PartitionSpec as P

KGRID = 8

time_step = 0.5
width_x = 2.0
width_y = 4.0
width_z = 2.0
far_away = 1000.0
softening = 0.25
basis_reach = 6.0
envelope_reach = 4.0
highest = lax.Precision.HIGHEST
f32 = jnp.float32
bf16 = jnp.bfloat16
i32 = jnp.int32

ROW_KIND = 3
ROW_ID = 4
ROW_INPLANE = 5
ROW_ABOVE = 6
ROW_BELOW = 7
ROW_LISTS = 8
PAIR_BLOCKS = 6


def split(x):
    high = x.astype(bf16)
    return high, (x - high.astype(f32)).astype(bf16)


def mm(a, b):
    return jnp.dot(a, b, preferred_element_type=f32)


def mm_nt(a, b):
    return lax.dot_general(a, b, (((1,), (1,)), ((), ())), preferred_element_type=f32)


def left3(x):
    high, low = split(x)
    return jnp.concatenate([high, high, low], axis=1)


def right3(x):
    high, low = split(x)
    return jnp.concatenate([high, low, high], axis=0)


def lanes(shape):
    return lax.broadcasted_iota(i32, shape, len(shape) - 1)


def rows(shape):
    return lax.broadcasted_iota(i32, shape, len(shape) - 2)


def pick(table, index):
    return jnp.take_along_axis(table, index, axis=1)


def sigmoid(x):
    return 1.0 / (1.0 + jnp.exp(-x))


def cos_sin(turns):
    half = math.pi * (turns - jnp.floor(turns + 0.5))
    sq = half * half
    sine = half * (
        1.0
        + sq
        * (
            -1.0 / 6
            + sq * (1.0 / 120 + sq * (-1.0 / 5040 + sq * (1.0 / 362880 - sq / 39916800.0)))
        )
    )
    cosine = 1.0 + sq * (
        -0.5
        + sq
        * (
            1.0 / 24
            + sq
            * (-1.0 / 720 + sq * (1.0 / 40320 + sq * (-1.0 / 3628800 + sq / 479001600.0)))
        )
    )
    return 1.0 - 2.0 * sine * sine, 2.0 * sine * cosine


def phase_tables(record, layers, strips):
    shape = (KGRID, record.shape[1])
    number = rows(shape).astype(f32)
    centred = number - float(KGRID // 2)
    cos_x, sin_x = cos_sin(number * record[0:1] / (strips * width_x))
    cos_y, sin_y = cos_sin(centred * record[1:2] / width_y)
    cos_z, sin_z = cos_sin(centred * record[2:3] / (layers * width_z))
    cos_yz, sin_yz = [], []
    for k in range(KGRID):
        c, s = cos_y[k : k + 1], sin_y[k : k + 1]
        cos_yz.append(c * cos_z - s * sin_z)
        sin_yz.append(s * cos_z + c * sin_z)
    return cos_x, sin_x, jnp.concatenate(cos_yz, axis=0), jnp.concatenate(sin_yz, axis=0)


def store_phases(record, layers, strips, refs, column):
    cos_high, cos_low, sin_high, sin_low = refs
    cos_x, sin_x, cos_yz, sin_yz = phase_tables(record, layers, strips)
    side = KGRID * KGRID
    at = pl.ds(column, record.shape[1])
    for k in range(KGRID):
        c, s = cos_x[k : k + 1], sin_x[k : k + 1]
        cosine = c * cos_yz - s * sin_yz
        sine = s * cos_yz + c * sin_yz
        here = slice(k * side, (k + 1) * side)
        cos_high[here, at], cos_low[here, at] = split(cosine)
        sin_high[here, at], sin_low[here, at] = split(sine)


def by_digits(x, strips, change):
    result, shift = 0, 0
    while 1 << (shift + 2) < strips:
        result = result | (change((x >> shift) & 3) << shift)
        shift += 2
    return result | ((x >> shift) << shift)


def to_place(d):
    return jnp.where(d == 0, 0, jnp.where(d == 3, 1, d + 1))


def from_place(d):
    return jnp.where(d == 0, 0, jnp.where(d == 1, 3, d - 1))


def domain_at(slot, here, sizes):
    layer, strip = here
    layers, strips = sizes
    x = by_digits(slot // layers, strips, from_place)
    return layer ^ (slot & (layers - 1)), strip ^ (2 * x)


def slot_of(g, p, here, sizes):
    layer, strip = here
    layers, strips = sizes
    return (g ^ layer) + layers * by_digits((p ^ strip) >> 1, strips, to_place)


def near_domain(j, here, sizes, near_layers):
    layer, strip = here
    layers, strips = sizes
    g = lax.rem(layer - 1 + j % near_layers + layers, layers)
    step = (j // near_layers) * (2 - 4 * (strip & 1))
    return g, lax.rem(strip + step + strips, strips)


def position_here():
    return lax.axis_index("gz").astype(i32), lax.axis_index("xy").astype(i32)


def mass_of(kind, mass):
    factor = jnp.zeros(kind.shape, f32)
    for s in range(mass.shape[0]):
        factor = factor + jnp.where(kind == s, mass[s], 0.0)
    return factor


def pack_kernel(sizes, cnt, mass, pos, vel, frc, spec, nbr, inplane, normal, out):
    layers, strips = sizes
    own = pos.shape[1]
    layer, strip = position_here()
    kind = spec[...]
    half_velocity = vel[...] + 0.5 * time_step * frc[...] * mass_of(kind, mass)
    moved = pos[...] + time_step * half_velocity
    lane = lanes((1, own))
    code = jnp.where(lane < cnt[0], kind, -1).astype(f32)
    number = ((layer * strips + strip) * own + lane).astype(f32)
    out[0:3, :] = moved
    out[ROW_KIND : ROW_KIND + 1, :] = code
    out[ROW_ID : ROW_ID + 1, :] = number
    lists = inplane[...].astype(f32)
    width = lists.shape[1]
    out[ROW_INPLANE : ROW_BELOW + 1, :] = jnp.zeros((3, own), f32)
    out[ROW_INPLANE : ROW_INPLANE + 1, 0:width] = lists[1:2]
    out[ROW_INPLANE : ROW_INPLANE + 1, width : 2 * width] = lists[0:1]
    lists = normal[...].astype(f32)
    tall = lists.shape[1]
    out[ROW_ABOVE : ROW_ABOVE + 1, 2 * width : 2 * width + tall] = lists[1:2]
    out[ROW_BELOW : ROW_BELOW + 1, 0:tall] = lists[0:1]
    out[ROW_LISTS:, :] = nbr[...].astype(f32)


def weights_kernel(
    embedding, radial, mix, self_w, charge_w, readout_w, readout_v, step, rex3, wcu3, wb3, re3, rv_out
):
    kinds, channels = embedding.shape
    basis = radial.shape[0]
    emb = embedding[...]
    mixed = jnp.dot(emb, mix[...], precision=highest, preferred_element_type=f32)
    selfed = jnp.dot(emb, self_w[...], precision=highest, preferred_element_type=f32)
    table = jnp.concatenate([mixed[s : s + 1] * radial[...] for s in range(kinds)], axis=0)
    re3[...] = left3(table)
    rest = jnp.zeros((channels - kinds * basis - kinds, channels), f32)
    wide = jnp.concatenate([table, selfed, rest], axis=0).T
    rex3[...] = left3(wide[:, : rex3.shape[1] // 3])
    wcu3[...] = left3(jnp.concatenate([charge_w[...].T, readout_w[...].T], axis=0))
    wb3[...] = left3(jnp.concatenate([charge_w[...], readout_w[...]], axis=1))
    rv_out[...] = jnp.broadcast_to(readout_v[...], (channels, channels)).T


def lift_kernel(block, out):
    out[0] = block[...]


def tables_kernel(sizes, data, *refs):
    own = data.shape[2]
    refs[4][...] = jnp.zeros_like(refs[4])
    refs = refs[:4]
    for n in range(data.shape[0]):
        store_phases(data[n, 0:8, :], *sizes, refs, n * own)


root = math.sqrt(math.log2(math.e))


def pair_basis(u, b):
    t = u - b * root
    return t, jnp.exp2(-(t * t))


def forward_kernel(
    sizes,
    dims,
    group,
    near_layers,
    early,
    mine,
    theirs,
    rex3,
    wcu3,
    rv_ref,
    radial,
    q_out,
    energy_out,
    pair_out,
    slope_out,
    readout_out,
    *rest,
):
    layers, strips = sizes
    own, width, tall, slots, kinds = dims
    if early:
        first, u_ref, w_ref, x_ref, energy_ref = rest
    else:
        cos_out, sin_out, first, u_ref, w_ref, x_ref, energy_ref, *tables = rest
    here = position_here()
    basis = radial.shape[0]
    channels = rv_ref.shape[0]
    total = mine.shape[0]
    near = 2 * near_layers
    lane8 = lanes((8, own))
    row8 = rows((8, own))
    energy_ref[...] = jnp.zeros_like(energy_ref)
    box = strips * width_x
    partner = (here[0], here[1] ^ 1)

    def first_step(i):
        g, p = domain_at(i, here, sizes)
        lower = theirs[slot_of(g, lax.rem(p + strips - 1, strips), partner, sizes)]
        upper = theirs[slot_of(g, lax.rem(p + 1, strips), partner, sizes)]
        at = jnp.broadcast_to(lower[ROW_INPLANE : ROW_INPLANE + 1], (8, own)).astype(i32)
        from_lower = pick(lower, at)
        at = jnp.broadcast_to(upper[ROW_INPLANE : ROW_INPLANE + 1], (8, own)).astype(i32)
        from_upper = pick(upper, at)
        down = jnp.where(p == 0, -box, 0.0)
        up = jnp.where(p == strips - 1, box, 0.0)
        shift = jnp.where(row8 == 0, jnp.where(lane8 < width, down, up), 0.0)
        first[i] = jnp.where(lane8 < width, from_lower, from_upper) + shift

    def first_steps(n, carry):
        for k in range(group):
            first_step(n * group + k)
        return carry

    lax.fori_loop(0, total // group, first_steps, 0)

    bound = jnp.where((row8 == ROW_KIND) | (row8 == ROW_ID), -1.0, 0.0)
    padding = jnp.where(row8 < 3, far_away, -1.0)
    spacing = basis_reach / (basis - 1)

    def normal_ghosts(g, p, move, row):
        other = lax.rem(g + move + layers, layers)
        j = slot_of(other, p, here, sizes)
        near_by = mine[j, 0:8, :]
        at = jnp.broadcast_to(near_by[row : row + 1], (8, own)).astype(i32)
        inside = at < own
        at = at & (own - 1)
        found = jnp.where(inside, pick(near_by, at), pick(first[j], at))
        beyond = (g + move < 0) | (g + move >= layers)
        return jnp.where(beyond, bound, found)

    def geometry(i, k):
        g, p = domain_at(i, here, sizes)
        record = mine[i, 0:8, :]
        below = normal_ghosts(g, p, -1, ROW_ABOVE)
        above = normal_ghosts(g, p, 1, ROW_BELOW)
        parts = (
            record,
            jnp.where(lane8 < 2 * width, first[i], below),
            jnp.where(lane8 < tall, above, padding),
        )
        index = mine[i, ROW_LISTS : ROW_LISTS + slots, :].astype(i32)
        part = index // own
        at = index & (own - 1)

        def gathered(r):
            a, b, c = [pick(jnp.broadcast_to(q[r : r + 1], (slots, own)), at) for q in parts]
            return jnp.where(part == 0, a, jnp.where(part == 1, b, c))

        dx = gathered(0) - record[0:1]
        dy = gathered(1) - record[1:2]
        dz = gathered(2) - record[2:3]
        code = gathered(ROW_KIND)
        d = jnp.sqrt(dx * dx + dy * dy + dz * dz + softening)
        quarter = d * (1.0 / envelope_reach)
        square = quarter * quarter
        envelope = 1.0 / (1.0 + square * square)
        u_ref[k] = d * (root / spacing)
        for s in range(kinds):
            w_ref[k, s] = jnp.where(code == float(s), envelope, 0.0)
        turn = lax.rem(g - here[0] + 1 + layers, layers)
        side = here[1] + 2 - 4 * (here[1] & 1)
        strip_step = jnp.where(p == here[1], 0, jnp.where(p == lax.rem(side + strips, strips), 1, 2))
        j = jnp.where((turn < near_layers) & (strip_step < 2), strip_step * near_layers + turn, near)
        pair_out[j, 0] = dx
        pair_out[j, 1] = dy
        pair_out[j, 2] = dz
        pair_out[j, 3] = code
        pair_out[j, 4] = gathered(ROW_ID)
        pair_out[j, 5] = d
        return record[ROW_KIND : ROW_KIND + 1], j

    def basis_sums(k, kind_row):
        centre = rows((basis, own)).astype(f32)
        sums = [jnp.zeros((basis, own), f32) for s in range(kinds)]
        for m in range(slots):
            t, e = pair_basis(u_ref[k, m : m + 1, :], centre)
            for s in range(kinds):
                sums[s] = sums[s] + e * w_ref[k, s, m : m + 1, :]
        tail = x_ref.shape[0] // 3 - kinds * basis
        one_hot = jnp.where(rows((tail, own)).astype(f32) == kind_row, 1.0, 0.0)
        x_ref[:, k * own : (k + 1) * own] = right3(jnp.concatenate(sums + [one_hot], axis=0))

    def group_step(n, place):
        start = n * group
        found = [geometry(start + k, k) for k in range(group)]
        for k in range(group):
            basis_sums(k, found[k][0])
        live = jnp.concatenate([kind_row for kind_row, _ in found], axis=1) >= 0.0
        pre = mm(rex3[...], x_ref[...])
        gate = sigmoid(pre)
        hidden = pre * gate
        both = mm(wcu3[...], right3(hidden))
        charges = jnp.where(live, both[:channels], 0.0)
        readout = both[channels:]
        readout_gate = sigmoid(readout)
        rv = jnp.concatenate([rv_ref[...]] * group, axis=1)
        scaled = jnp.where(live, rv * readout_gate, 0.0)
        local = scaled * readout
        slope = gate * (1.0 + pre * (1.0 - gate))
        back = scaled * (1.0 + readout * (1.0 - readout_gate))
        wide = jnp.sum(local.reshape(channels // 8, 8, group * own), axis=0)
        for k in range(group):
            energy_ref[...] += wide[:, k * own : (k + 1) * own]
        column = pl.multiple_of(place * own, own)
        high, low = split(charges)
        q_out[0:channels, pl.ds(column, group * own)] = high
        q_out[channels : 2 * channels, pl.ds(column, group * own)] = low
        for k in range(group):
            column = pl.multiple_of(found[k][1] * own, own)
            slope_out[:, pl.ds(column, own)] = slope[:, k * own : (k + 1) * own]
            readout_out[:, pl.ds(column, own)] = back[:, k * own : (k + 1) * own]

    if early:

        def steps(n, carry):
            group_step(n, n * group)
            return carry

        lax.fori_loop(0, total // group, steps, 0)
    else:
        chunk = q_out.shape[1] // own

        def chunk_step(c, carry):
            def steps(n, inner):
                group_step(c * (chunk // group) + n, n * group)
                return inner

            def phases(n, inner):
                record = mine[c * chunk + n, 0:8, :]
                store_phases(record, layers, strips, tables, pl.multiple_of(n * own, own))
                return inner

            lax.fori_loop(0, chunk // group, steps, 0)
            lax.fori_loop(0, chunk, phases, 0)
            for out, high, low in ((cos_out, *tables[:2]), (sin_out, *tables[2:])):
                part = structure_part(high, low, q_out, 0)

                @pl.when(c == 0)
                def _():
                    out[...] = part

                @pl.when(c > 0)
                def _():
                    out[...] += part

            return carry

        lax.fori_loop(0, total // chunk, chunk_step, 0)
    energy_out[...] = jnp.sum(energy_ref[...], axis=0, keepdims=True)
    if not early:
        cos_out[zero_row : zero_row + 1, :] = energy_out[...]


zero_row = (KGRID // 2) * KGRID + KGRID // 2


def structure_part(high, low, q, column):
    channels = q.shape[0] // 2
    at = slice(column, column + high.shape[1])
    wide = mm_nt(high[...], q[:, at])
    return wide[:, :channels] + wide[:, channels:] + mm_nt(low[...], q[0:channels, at])


def structure_kernel(first_half, chunks, *refs):
    *tables, q, energy, out = refs
    column = 0
    part = None
    for n in range(chunks):
        high, low = tables[2 * n : 2 * n + 2]
        more = structure_part(high, low, q, column)
        part = more if part is None else part + more
        column += high.shape[1]
    out[...] = part
    if first_half:
        out[zero_row : zero_row + 1, :] = energy[...]


def near_kernel(sizes, near_layers, basis, kinds, starts, mine, pairs, *refs):
    layers, strips = sizes
    *tables, cos_high, cos_low, sin_high, sin_low, live_out, fall_out = refs
    own = mine.shape[2]
    here = position_here()
    spacing = basis_reach / (basis - 1)
    outs = (cos_high, cos_low, sin_high, sin_low)
    for j in range(2 * near_layers):
        at = slice(j * own, (j + 1) * own)
        slot = slot_of(*near_domain(j, here, sizes, near_layers), here, sizes)
        record = mine[slot, 0:8, :]
        live = jnp.where(record[ROW_KIND : ROW_KIND + 1] >= 0.0, 1.0, 0.0)
        live_out[:, at] = jnp.broadcast_to(live, (8, own))
        if not starts:
            store_phases(record, layers, strips, outs, j * own)
        for n, start in enumerate(starts):
            parts = tables[4 * n : 4 * n + 4]
            if j < near_layers and n > 0:
                continue
            if j >= near_layers and n == 0:
                continue
            end = start + parts[0].shape[1] // own

            @pl.when((slot >= start) & (slot < end))
            def _():
                column = pl.multiple_of((slot - start) * own, own)
                for part, out in zip(parts, outs):
                    out[:, at] = part[:, pl.ds(column, own)]

        d = pairs[j, 5]
        quarter = d * (1.0 / envelope_reach)
        square = quarter * quarter
        envelope = 1.0 / (1.0 + square * square)
        over = 1.0 / d
        slope = -envelope * envelope * (4.0 / envelope_reach) * square * quarter * over
        lean = envelope * (-2.0 / (spacing * root)) * over
        u = d * (root / spacing)
        for b in range(basis):
            t, e = pair_basis(u, float(b))
            fall_out[j, b] = e * (lean * t + slope)


def backward_kernel(
    sizes,
    dims,
    all_atoms,
    near_layers,
    cos_own,
    cos_other,
    sin_own,
    sin_other,
    kernel_filter,
    cos_high,
    cos_low,
    sin_high,
    sin_low,
    live_in,
    fall_in,
    wb3,
    re3,
    pair_in,
    slope_in,
    readout_in,
    own_out,
    other_out,
    energy_out,
    weight_ref,
    b_ref,
    f_ref,
    t_ref,
    hot_ref,
    col_ref,
):
    layers, strips = sizes
    own, width, tall, slots, kinds = dims
    layer, strip = position_here()
    basis = fall_in.shape[1]
    channels = slope_in.shape[0]
    waves = KGRID**3
    domains = 2 * near_layers
    lanes_all = domains * own

    cos_sum = cos_own[...] + cos_other[...]
    sin_sum = sin_own[...] + sin_other[...]
    local = cos_sum[zero_row : zero_row + 1]
    keeper = jnp.where(rows((waves, channels)) == zero_row, 0.0, 1.0 / all_atoms)
    scale = keeper * kernel_filter[...]
    weight_cos = scale * cos_sum
    weight_sin = scale * sin_sum
    ewald = jnp.sum(weight_cos * cos_sum + weight_sin * sin_sum, axis=0, keepdims=True)
    energy = jnp.sum(local + 0.5 * ewald, axis=1, keepdims=True)
    energy_out[...] = jnp.broadcast_to(energy / all_atoms, energy_out.shape)

    grad = None
    for n, (weight, high, low) in enumerate(
        ((weight_cos, cos_high, cos_low), (weight_sin, sin_high, sin_low))
    ):
        top, bottom = split(weight.T)
        wide = mm(jnp.concatenate([top, bottom], axis=0), high[...])
        part = wide[:channels] + wide[channels:] + mm(top, low[...])
        grad = part if grad is None else grad + part
        weight_ref[n * waves : (n + 1) * waves, :] = left3(weight)
    grad = grad * live_in[0:1, :]
    both = jnp.concatenate([grad, readout_in[:, 0:lanes_all]], axis=0)
    grad = mm(wb3[...], right3(both)) * slope_in[:, 0:lanes_all]
    b_ref[...] = mm(re3[...], right3(grad))

    base = ((layer * strips + (strip - (strip & 1))) * own).astype(f32)
    groups = 8
    size = 2 * own // groups
    group = rows((groups, own))
    member = rows((size, own))
    found = None
    own_out[...] = jnp.zeros_like(own_out)
    for j in range(domains):
        code = pair_in[j, 3]
        same = [code == float(s) for s in range(kinds)]
        force = jnp.zeros((slots, own), f32)
        for b in range(basis):
            chosen = jnp.zeros((slots, own), f32)
            for s in range(kinds):
                k = s * basis + b
                row = b_ref[k : k + 1, j * own : (j + 1) * own]
                chosen = jnp.where(same[s], row, chosen)
            force = force + fall_in[j, b] * chosen
        target = (pair_in[j, 4] - base).astype(i32)
        t_ref[j, 0] = target // size
        t_ref[j, 1] = target & (size - 1)
        for r in range(3):
            part = force * pair_in[j, r]
            high = part.astype(bf16).astype(f32)
            f_ref[j, 2 * r] = high
            f_ref[j, 2 * r + 1] = part - high
            if j == 1:
                own_out[r : r + 1, :] = -jnp.sum(part, axis=0, keepdims=True)
        for m in range(slots):
            at = slice(m * own, (m + 1) * own)
            hit = t_ref[j, 0, m : m + 1, :] == group
            for r in range(3):
                hot = [
                    jnp.where(hit, f_ref[j, 2 * r + n, m : m + 1, :], 0.0) for n in range(2)
                ]
                here = slice(2 * r * groups, 2 * (r + 1) * groups)
                hot_ref[j, here, at] = jnp.concatenate(hot, axis=0).astype(bf16)
            one = jnp.where(t_ref[j, 1, m : m + 1, :] == member, 1.0, 0.0)
            col_ref[j, :, at] = one.astype(bf16)
        more = mm_nt(hot_ref[j], col_ref[j])
        found = more if found is None else found + more

    spread = jnp.where(rows((size, own)) == (lanes((size, own)) & (size - 1)), 1.0, 0.0)
    wide = jnp.dot(found, spread, precision=highest, preferred_element_type=f32)
    half = groups // 2
    fits = rows((half, own)) == lanes((half, own)) // size
    odd = (strip & 1) == 1
    other_out[...] = jnp.zeros_like(other_out)
    for r in range(3):
        both = wide[2 * r * groups : (2 * r + 1) * groups]
        both = both + wide[(2 * r + 1) * groups : (2 * r + 2) * groups]
        sides = [
            jnp.sum(jnp.where(fits, both[n * half : (n + 1) * half], 0.0), axis=0, keepdims=True)
            for n in range(2)
        ]
        own_out[r : r + 1, :] += jnp.where(odd, sides[1], sides[0])
        other_out[r : r + 1, :] = jnp.where(odd, sides[0], sides[1])


def ewald_kernel(sizes, weights, cos_high, cos_low, sin_high, sin_low, q_in, out):
    layers, strips = sizes
    channels = q_in.shape[0] // 2
    waves = cos_high.shape[0]
    own = out.shape[1]
    mine = slice(own, 2 * own)
    charge_high = q_in[0:channels, 0:own]
    charge_low = q_in[channels : 2 * channels, 0:own]
    along = mm(weights[...], jnp.concatenate([charge_high, charge_low, charge_high], axis=0))
    cosine = cos_high[:, mine].astype(f32) + cos_low[:, mine].astype(f32)
    sine = sin_high[:, mine].astype(f32) + sin_low[:, mine].astype(f32)
    turn = cosine * along[waves:] - sine * along[:waves]
    index = lanes((8, waves))
    axis = rows((8, waves))
    part_x = (index // (KGRID * KGRID)).astype(f32) / (strips * width_x)
    part_y = ((index // KGRID) % KGRID - KGRID // 2).astype(f32) / width_y
    part_z = (index % KGRID - KGRID // 2).astype(f32) / (layers * width_z)
    wave = jnp.where(axis == 0, part_x, jnp.where(axis == 1, part_y, part_z))
    wave = jnp.where(axis < 3, wave * (2.0 * math.pi), 0.0)
    out[...] = mm(left3(wave), right3(turn))


def final_kernel(pos, vel, frc, spec, mass, own, ewald, other, moved_out, vel_out, frc_out):
    factor = mass_of(spec[...], mass)
    half_velocity = vel[...] + 0.5 * time_step * frc[...] * factor
    moved_out[...] = pos[...] + time_step * half_velocity
    forces_new = -(own[0:3, :] + ewald[0:3, :] + other[0:3, :])
    frc_out[...] = forces_new
    vel_out[...] = half_velocity + 0.5 * time_step * forces_new * factor


def exchange(x, axis, bit):
    count = lax.axis_size(axis)
    return lax.ppermute(x, axis, [(i, i ^ bit) for i in range(count)])


MIB = 1024 * 1024
vmem = pl.BlockSpec(memory_space=pltpu.VMEM)
smem = pl.BlockSpec(memory_space=pltpu.SMEM)


def call(kernel, name, outs, ins, scratch=(), limit=8, scalars=(), unread=(), work=10**8):
    def spec(n):
        if n in unread:
            return pl.BlockSpec(memory_space=pl.ANY)
        return smem if n in scalars else vmem

    return pl.pallas_call(
        kernel,
        out_shape=[jax.ShapeDtypeStruct(shape, dtype) for shape, dtype in outs],
        in_specs=[spec(n) for n in range(len(ins))],
        out_specs=[vmem] * len(outs),
        scratch_shapes=[pltpu.VMEM(shape, dtype) for shape, dtype in scratch],
        compiler_params=pltpu.CompilerParams(vmem_limit_bytes=limit and limit * MIB),
        cost_estimate=pl.CostEstimate(flops=work, bytes_accessed=MIB, transcendentals=0),
        name=name,
    )(*ins)


def local(
    positions,
    velocities,
    forces,
    species,
    counts,
    neighbours,
    send_inplane,
    send_normal,
    embedding,
    inverse_mass,
    radial_weight,
    mix_weight,
    self_weight,
    charge_weight,
    readout_weight,
    readout_vector,
    kernel_filter,
):
    layers = lax.axis_size("gz")
    strips = lax.axis_size("xy")
    sizes = (layers, strips)
    own = positions.shape[1]
    slots = neighbours.shape[0]
    kinds, channels = embedding.shape
    basis = radial_weight.shape[0]
    dims = (own, send_inplane.shape[1], send_normal.shape[1], slots, kinds)
    all_atoms = own * layers * strips
    waves = KGRID**3
    kind_row = species[None, :]
    total = layers * (strips // 2)
    early = total <= 16
    group = min(8, total)
    near_layers = min(3, layers)
    near = 2 * near_layers
    depth = kinds * basis + -(-kinds // 16) * 16

    (block,) = call(
        functools.partial(pack_kernel, sizes),
        "pack",
        [((ROW_LISTS + slots, own), f32)],
        (
            counts,
            inverse_mass,
            positions,
            velocities,
            forces,
            kind_row,
            neighbours,
            send_inplane,
            send_normal,
        ),
        scalars=(0, 1),
        limit=None,
    )
    def phases(data):
        wide = data.shape[0] * own
        return call(
            functools.partial(tables_kernel, sizes),
            "tables",
            [((waves, wide), bf16)] * 4 + [((8, own), f32)],
            (data,),
            work=4 * 10**9,
        )

    arrived = exchange(block, "gz", 1)[None]
    (data,) = call(
        lift_kernel, "lift", [((1, *block.shape), f32)], (block,), limit=1, work=8 * 10**9
    )
    data = jnp.concatenate([data, arrived], axis=0)
    rex3, wcu3, wb3, re3, rv = call(
        weights_kernel,
        "weights",
        [
            ((channels, 3 * depth), bf16),
            ((2 * channels, 3 * channels), bf16),
            ((channels, 6 * channels), bf16),
            ((kinds * basis, 3 * channels), bf16),
            ((channels, channels), f32),
        ],
        (
            embedding,
            radial_weight,
            mix_weight,
            self_weight,
            charge_weight,
            readout_weight,
            readout_vector[None, :],
            data,
        ),
        limit=None,
        unread=(7,),
        work=4 * 10**9,
    )

    bit = 2
    while bit < layers:
        data = jnp.concatenate([data, exchange(data, "gz", bit)], axis=0)
        bit *= 2
    tables, starts, zeros = [], [], []
    if early:
        *table, zero = phases(data)
        tables.append(table)
        starts.append(0)
    bit = 2
    while bit < strips:
        bits = [3 * bit, bit, 2 * bit] if 2 * bit < strips else [bit]
        parts = [exchange(data, "xy", n) for n in bits]
        for n, part in enumerate(parts):
            if early:
                *table, zero = phases(part)
                zeros.append(zero)
                tables.append(table)
                starts.append((n + 1) * data.shape[0])
        data = jnp.concatenate([data] + parts, axis=0)
        bit *= 4
    records = data[:, 0:8, :]
    for zero in zeros[:2]:
        records = records + zero
    theirs = exchange(records, "xy", 1)

    chunk = min(16, total)
    outs = [
        ((2 * channels, chunk * own), bf16),
        ((1, channels), f32),
        ((near + 1, PAIR_BLOCKS, slots, own), f32),
        ((channels, (near + 1) * own), f32),
        ((channels, (near + 1) * own), f32),
    ]
    scratch = [
        ((total, 8, own), f32),
        ((group, slots, own), f32),
        ((group, kinds, slots, own), f32),
        ((3 * depth, group * own), bf16),
        ((8, own), f32),
    ]
    if not early:
        outs += [((waves, channels), f32)] * 2
        scratch += [((waves, chunk * own), bf16)] * 4
    q, energy_row, pairs, slope, readout, *sums = call(
        functools.partial(forward_kernel, sizes, dims, group, near_layers, early),
        "forward",
        outs,
        (data, theirs, rex3, wcu3, rv, radial_weight),
        scratch,
        limit=16 if early else 48,
    )
    for n in range(2 if early else 0):
        parts = [t for table in tables for t in table[2 * n : 2 * n + 2]]
        sums += call(
            functools.partial(structure_kernel, n == 0, len(tables)),
            "structure",
            [((waves, channels), f32)],
            (*parts, q, energy_row),
            limit=16,
            work=10**9,
        )
    others = [exchange(part, "xy", 1) for part in sums]
    near_parts = call(
        functools.partial(near_kernel, sizes, near_layers, basis, kinds, starts),
        "near",
        [((waves, near * own), bf16)] * 4
        + [((8, near * own), f32), ((near, basis, slots, own), f32)],
        (data, pairs, *[t for table in tables for t in table]),
        limit=8 if early else 32,
    )
    groups = 8
    own_grad, other_grad, energy, weights3 = call(
        functools.partial(backward_kernel, sizes, dims, all_atoms, near_layers),
        "backward",
        [
            ((8, own), f32),
            ((8, own), f32),
            ((1, channels), f32),
            ((2 * waves, 3 * channels), bf16),
        ],
        (
            sums[0],
            others[0],
            sums[1],
            others[1],
            kernel_filter,
            *near_parts,
            wb3,
            re3,
            pairs,
            slope,
            readout,
        ),
        [
            ((kinds * basis, near * own), f32),
            ((near, 6, slots, own), f32),
            ((near, 2, slots, own), i32),
            ((near, 6 * groups, slots * own), bf16),
            ((near, 2 * own // groups, slots * own), bf16),
        ],
        limit=16,
    )
    arrived = exchange(other_grad, "xy", 1)
    (ewald_grad,) = call(
        functools.partial(ewald_kernel, sizes),
        "ewald",
        [((8, own), f32)],
        (weights3, *near_parts[:4], q),
        work=4 * 10**9,
    )
    moved, velocities_new, forces_new = call(
        final_kernel,
        "final",
        [((3, own), f32)] * 3,
        (positions, velocities, forces, kind_row, inverse_mass, own_grad, ewald_grad, arrived),
        scalars=(4,),
        limit=1,
    )
    return (moved, velocities_new, forces_new, energy[0, 0])


def solution(mesh):
    return jax.shard_map(
        local,
        mesh=mesh,
        in_specs=(
            P(None, ("gz", "xy")),
            P(None, ("gz", "xy")),
            P(None, ("gz", "xy")),
            P(("gz", "xy")),
            P(("gz", "xy")),
            P(None, ("gz", "xy")),
            P(None, ("gz", "xy")),
            P(None, ("gz", "xy")),
            P(),
            P(),
            P(),
            P(),
            P(),
            P(),
            P(),
            P(),
            P(),
        ),
        out_specs=(P(None, ("gz", "xy")), P(None, ("gz", "xy")), P(None, ("gz", "xy")), P()),
        check_vma=False,
    )
```

```python
import functools
import math

import jax
import jax.numpy as jnp
from jax import lax
from jax.experimental import pallas as pl
from jax.experimental.pallas import tpu as pltpu
from jax.sharding import PartitionSpec as P

KGRID = 8

time_step = 0.5
width_x = 2.0
width_y = 4.0
width_z = 2.0
far_away = 1000.0
softening = 0.25
basis_reach = 6.0
envelope_reach = 4.0
highest = lax.Precision.HIGHEST
f32 = jnp.float32
bf16 = jnp.bfloat16
i32 = jnp.int32

ROW_KIND = 3
ROW_ID = 4
ROW_INPLANE = 5
ROW_ABOVE = 6
ROW_BELOW = 7
ROW_LISTS = 8
PAIR_BLOCKS = 6


def split(x):
    high = x.astype(bf16)
    return high, (x - high.astype(f32)).astype(bf16)


def mm(a, b):
    return jnp.dot(a, b, preferred_element_type=f32)


def mm_nt(a, b):
    return lax.dot_general(a, b, (((1,), (1,)), ((), ())), preferred_element_type=f32)


def left3(x):
    high, low = split(x)
    return jnp.concatenate([high, high, low], axis=1)


def right3(x):
    high, low = split(x)
    return jnp.concatenate([high, low, high], axis=0)


def lanes(shape):
    return lax.broadcasted_iota(i32, shape, len(shape) - 1)


def rows(shape):
    return lax.broadcasted_iota(i32, shape, len(shape) - 2)


def pick(table, index):
    return jnp.take_along_axis(table, index, axis=1)


def sigmoid(x):
    return 0.5 + 0.5 * jnp.tanh(0.5 * x)


def cos_sin(turns):
    half = math.pi * (turns - jnp.floor(turns + 0.5))
    sq = half * half
    sine = half * (
        1.0
        + sq
        * (
            -1.0 / 6
            + sq * (1.0 / 120 + sq * (-1.0 / 5040 + sq * (1.0 / 362880 - sq / 39916800.0)))
        )
    )
    cosine = 1.0 + sq * (
        -0.5
        + sq
        * (
            1.0 / 24
            + sq
            * (-1.0 / 720 + sq * (1.0 / 40320 + sq * (-1.0 / 3628800 + sq / 479001600.0)))
        )
    )
    return 1.0 - 2.0 * sine * sine, 2.0 * sine * cosine


def phase_tables(record, layers, strips):
    shape = (KGRID, record.shape[1])
    number = rows(shape).astype(f32)
    centred = number - float(KGRID // 2)
    cos_x, sin_x = cos_sin(number * record[0:1] / (strips * width_x))
    cos_y, sin_y = cos_sin(centred * record[1:2] / width_y)
    cos_z, sin_z = cos_sin(centred * record[2:3] / (layers * width_z))
    cos_yz, sin_yz = [], []
    for k in range(KGRID):
        c, s = cos_y[k : k + 1], sin_y[k : k + 1]
        cos_yz.append(c * cos_z - s * sin_z)
        sin_yz.append(s * cos_z + c * sin_z)
    return cos_x, sin_x, jnp.concatenate(cos_yz, axis=0), jnp.concatenate(sin_yz, axis=0)


def store_phases(record, layers, strips, refs, column):
    cos_high, cos_low, sin_high, sin_low = refs
    cos_x, sin_x, cos_yz, sin_yz = phase_tables(record, layers, strips)
    side = KGRID * KGRID
    at = pl.ds(column, record.shape[1])
    for k in range(KGRID):
        c, s = cos_x[k : k + 1], sin_x[k : k + 1]
        cosine = c * cos_yz - s * sin_yz
        sine = s * cos_yz + c * sin_yz
        here = slice(k * side, (k + 1) * side)
        cos_high[here, at], cos_low[here, at] = split(cosine)
        sin_high[here, at], sin_low[here, at] = split(sine)


def by_digits(x, strips, change):
    result, shift = 0, 0
    while 1 << (shift + 2) < strips:
        result = result | (change((x >> shift) & 3) << shift)
        shift += 2
    return result | ((x >> shift) << shift)


def to_place(d):
    return jnp.where(d == 0, 0, jnp.where(d == 3, 1, d + 1))


def from_place(d):
    return jnp.where(d == 0, 0, jnp.where(d == 1, 3, d - 1))


def domain_at(slot, here, sizes):
    layer, strip = here
    layers, strips = sizes
    x = by_digits(slot // layers, strips, from_place)
    return layer ^ (slot & (layers - 1)), strip ^ (2 * x)


def slot_of(g, p, here, sizes):
    layer, strip = here
    layers, strips = sizes
    return (g ^ layer) + layers * by_digits((p ^ strip) >> 1, strips, to_place)


def near_domain(j, here, sizes, near_layers):
    layer, strip = here
    layers, strips = sizes
    g = lax.rem(layer - 1 + j % near_layers + layers, layers)
    step = (j // near_layers) * (2 - 4 * (strip & 1))
    return g, lax.rem(strip + step + strips, strips)


def position_here():
    return lax.axis_index("gz").astype(i32), lax.axis_index("xy").astype(i32)


def mass_of(kind, mass):
    factor = jnp.zeros(kind.shape, f32)
    for s in range(mass.shape[1]):
        factor = factor + jnp.where(kind == s, mass[0:1, s : s + 1], 0.0)
    return factor


def pack_kernel(sizes, cnt, mass, pos, vel, frc, spec, nbr, inplane, normal, out):
    layers, strips = sizes
    own = pos.shape[1]
    layer, strip = position_here()
    kind = spec[...]
    half_velocity = vel[...] + 0.5 * time_step * frc[...] * mass_of(kind, mass)
    moved = pos[...] + time_step * half_velocity
    lane = lanes((1, own))
    code = jnp.where(lane < cnt[...], kind, -1).astype(f32)
    number = ((layer * strips + strip) * own + lane).astype(f32)
    out[0:3, :] = moved
    out[ROW_KIND : ROW_KIND + 1, :] = code
    out[ROW_ID : ROW_ID + 1, :] = number
    lists = inplane[...].astype(f32)
    width = lists.shape[1]
    out[ROW_INPLANE : ROW_BELOW + 1, :] = jnp.zeros((3, own), f32)
    out[ROW_INPLANE : ROW_INPLANE + 1, 0:width] = lists[1:2]
    out[ROW_INPLANE : ROW_INPLANE + 1, width : 2 * width] = lists[0:1]
    lists = normal[...].astype(f32)
    tall = lists.shape[1]
    out[ROW_ABOVE : ROW_ABOVE + 1, 2 * width : 2 * width + tall] = lists[1:2]
    out[ROW_BELOW : ROW_BELOW + 1, 0:tall] = lists[0:1]
    out[ROW_LISTS:, :] = nbr[...].astype(f32)


def mixed_table(embedding, radial, mix):
    mixed = jnp.dot(embedding[...], mix[...], precision=highest, preferred_element_type=f32)
    kinds = embedding.shape[0]
    return jnp.concatenate([mixed[s : s + 1] * radial[...] for s in range(kinds)], axis=0)


def weights_kernel(
    embedding,
    radial,
    mix,
    self_w,
    charge_w,
    readout_w,
    readout_v,
    ahead,
    rex3,
    wcu3,
    wb3,
    re3,
    rv_out,
):
    kinds, channels = embedding.shape
    table = mixed_table(embedding, radial, mix)
    selfed = jnp.dot(embedding[...], self_w[...], precision=highest, preferred_element_type=f32)
    rest = jnp.zeros((channels - table.shape[0] - kinds, channels), f32)
    wide = jnp.concatenate([table, selfed, rest], axis=0).T
    rex3[...] = left3(wide[:, : rex3.shape[1] // 3])
    wcu3[...] = left3(jnp.concatenate([charge_w[...].T, readout_w[...].T], axis=0))
    wb3[...] = left3(jnp.concatenate([charge_w[...], readout_w[...]], axis=1))
    re3[...] = left3(table)
    rv_out[...] = jnp.broadcast_to(readout_v[...], (channels, channels)).T


def lift_kernel(all_atoms, block, kernel_filter, out, filter_out):
    out[0] = block[...]
    keeper = jnp.where(rows(kernel_filter.shape) == zero_row, 0.0, 1.0 / all_atoms)
    filter_out[...] = keeper * kernel_filter[...]


def tables_kernel(sizes, data, ahead, *refs):
    own = data.shape[2]
    refs[4][...] = jnp.zeros_like(refs[4])
    refs = refs[:4]
    for n in range(data.shape[0]):
        store_phases(data[n, 0:8, :], *sizes, refs, n * own)


root = math.sqrt(math.log2(math.e))


def pair_basis(u, b):
    t = u - b * root
    return t, jnp.exp2(-(t * t))


def forward_kernel(
    sizes,
    dims,
    group,
    block,
    near_layers,
    early,
    mine,
    theirs,
    rex3,
    wcu3,
    rv_ref,
    radial,
    q_out,
    energy_out,
    pair_out,
    slope_out,
    readout_out,
    *rest,
):
    layers, strips = sizes
    own, width, tall, slots, kinds = dims
    if early:
        first, u_ref, w_ref, x_ref, energy_ref = rest
    else:
        cos_out, sin_out, first, u_ref, w_ref, x_ref, energy_ref, *tables = rest
    here = position_here()
    basis = radial.shape[0]
    channels = rv_ref.shape[0]
    total = mine.shape[0]
    near = 2 * near_layers
    lane8 = lanes((8, own))
    row8 = rows((8, own))
    energy_ref[...] = jnp.zeros_like(energy_ref)
    box = strips * width_x
    partner = (here[0], here[1] ^ 1)

    def first_step(i):
        g, p = domain_at(i, here, sizes)
        lower = theirs[slot_of(g, lax.rem(p + strips - 1, strips), partner, sizes)]
        upper = theirs[slot_of(g, lax.rem(p + 1, strips), partner, sizes)]
        at = jnp.broadcast_to(lower[ROW_INPLANE : ROW_INPLANE + 1], (8, own)).astype(i32)
        from_lower = pick(lower, at)
        at = jnp.broadcast_to(upper[ROW_INPLANE : ROW_INPLANE + 1], (8, own)).astype(i32)
        from_upper = pick(upper, at)
        down = jnp.where(p == 0, -box, 0.0)
        up = jnp.where(p == strips - 1, box, 0.0)
        shift = jnp.where(row8 == 0, jnp.where(lane8 < width, down, up), 0.0)
        first[i] = jnp.where(lane8 < width, from_lower, from_upper) + shift

    def first_steps(n, carry):
        for k in range(group):
            first_step(n * group + k)
        return carry

    local_first = group % layers == 0
    if not local_first:
        lax.fori_loop(0, total // group, first_steps, 0)

    bound = jnp.where((row8 == ROW_KIND) | (row8 == ROW_ID), -1.0, 0.0)
    padding = jnp.where(row8 < 3, far_away, -1.0)
    spacing = basis_reach / (basis - 1)

    def normal_ghosts(g, p, move, row):
        other = lax.rem(g + move + layers, layers)
        j = slot_of(other, p, here, sizes)
        near_by = mine[j, 0:8, :]
        at = jnp.broadcast_to(near_by[row : row + 1], (8, own)).astype(i32)
        inside = at < own
        at = at & (own - 1)
        found = jnp.where(inside, pick(near_by, at), pick(first[j], at))
        beyond = (g + move < 0) | (g + move >= layers)
        return jnp.where(beyond, bound, found)

    def geometry(i, k):
        g, p = domain_at(i, here, sizes)
        record = mine[i, 0:8, :]
        below = normal_ghosts(g, p, -1, ROW_ABOVE)
        above = normal_ghosts(g, p, 1, ROW_BELOW)
        parts = (
            record,
            jnp.where(lane8 < 2 * width, first[i], below),
            jnp.where(lane8 < tall, above, padding),
        )
        index = mine[i, ROW_LISTS : ROW_LISTS + slots, :].astype(i32)
        part = index // own
        at = index & (own - 1)

        def gathered(r):
            a, b, c = [pick(jnp.broadcast_to(q[r : r + 1], (slots, own)), at) for q in parts]
            return jnp.where(part == 0, a, jnp.where(part == 1, b, c))

        dx = gathered(0) - record[0:1]
        dy = gathered(1) - record[1:2]
        dz = gathered(2) - record[2:3]
        code = gathered(ROW_KIND)
        d = jnp.sqrt(dx * dx + dy * dy + dz * dz + softening)
        quarter = d * (1.0 / envelope_reach)
        square = quarter * quarter
        envelope = 1.0 / (1.0 + square * square)
        u_ref[k] = d * (root / spacing)
        for s in range(kinds):
            w_ref[k, s] = jnp.where(code == float(s), envelope, 0.0)
        turn = lax.rem(g - here[0] + 1 + layers, layers)
        side = here[1] + 2 - 4 * (here[1] & 1)
        strip_step = jnp.where(p == here[1], 0, jnp.where(p == lax.rem(side + strips, strips), 1, 2))
        j = jnp.where((turn < near_layers) & (strip_step < 2), strip_step * near_layers + turn, near)
        pair_out[j, 0] = dx
        pair_out[j, 1] = dy
        pair_out[j, 2] = dz
        pair_out[j, 3] = code
        pair_out[j, 4] = gathered(ROW_ID)
        pair_out[j, 5] = d
        return record[ROW_KIND : ROW_KIND + 1], j

    def basis_sums(k, kind_row):
        centre = rows((basis, own)).astype(f32)
        sums = [jnp.zeros((basis, own), f32) for s in range(kinds)]
        for m in range(slots):
            t, e = pair_basis(u_ref[k, m : m + 1, :], centre)
            for s in range(kinds):
                sums[s] = sums[s] + e * w_ref[k, s, m : m + 1, :]
        tail = x_ref.shape[0] // 3 - kinds * basis
        one_hot = jnp.where(rows((tail, own)).astype(f32) == kind_row, 1.0, 0.0)
        x_ref[:, k * own : (k + 1) * own] = right3(jnp.concatenate(sums + [one_hot], axis=0))

    def block_step(start, place, offset):
        found = [geometry(start + k, offset + k) for k in range(block)]
        for k in range(block):
            basis_sums(offset + k, found[k][0])
        live = jnp.concatenate([kind_row for kind_row, _ in found], axis=1) >= 0.0
        pre = mm(rex3[...], x_ref[:, offset * own : (offset + block) * own])
        gate = sigmoid(pre)
        hidden = pre * gate
        both = mm(wcu3[...], right3(hidden))
        charges = jnp.where(live, both[:channels], 0.0)
        readout = both[channels:]
        readout_gate = sigmoid(readout)
        rv = jnp.concatenate([rv_ref[...]] * block, axis=1)
        scaled = jnp.where(live, rv * readout_gate, 0.0)
        local = scaled * readout
        slope = gate * (1.0 + pre * (1.0 - gate))
        back = scaled * (1.0 + readout * (1.0 - readout_gate))
        wide = jnp.sum(local.reshape(channels // 8, 8, block * own), axis=0)
        for k in range(block):
            energy_ref[...] += wide[:, k * own : (k + 1) * own]
        column = pl.multiple_of(place * own, own)
        high, low = split(charges)
        q_out[0:channels, pl.ds(column, block * own)] = high
        q_out[channels : 2 * channels, pl.ds(column, block * own)] = low
        for k in range(block):
            column = pl.multiple_of(found[k][1] * own, own)
            slope_out[:, pl.ds(column, own)] = slope[:, k * own : (k + 1) * own]
            readout_out[:, pl.ds(column, own)] = back[:, k * own : (k + 1) * own]

    def group_step(n, place):
        if local_first:
            for k in range(group):
                first_step(n * group + k)
        for offset in range(0, group, block):
            block_step(n * group + offset, place + offset, offset)

    if early:

        def steps(n, carry):
            group_step(n, n * group)
            return carry

        lax.fori_loop(0, total // group, steps, 0, unroll=total == group)
    else:
        chunk = q_out.shape[1] // own

        def chunk_step(c, carry):
            def steps(n, inner):
                group_step(c * (chunk // group) + n, n * group)
                return inner

            def phases(n, inner):
                record = mine[c * chunk + n, 0:8, :]
                store_phases(record, layers, strips, tables, pl.multiple_of(n * own, own))
                return inner

            lax.fori_loop(0, chunk // group, steps, 0)
            lax.fori_loop(0, chunk, phases, 0)
            for out, high, low in ((cos_out, *tables[:2]), (sin_out, *tables[2:])):
                part = structure_part(high, low, q_out, 0)

                @pl.when(c == 0)
                def _():
                    out[...] = part

                @pl.when(c > 0)
                def _():
                    out[...] += part

            return carry

        lax.fori_loop(0, total // chunk, chunk_step, 0)
    energy_out[...] = jnp.sum(energy_ref[...], axis=0, keepdims=True)
    if not early:
        cos_out[zero_row : zero_row + 1, :] = energy_out[...]


zero_row = (KGRID // 2) * KGRID + KGRID // 2


def structure_part(high, low, q, column):
    channels = q.shape[0] // 2
    at = slice(column, column + high.shape[1])
    wide = mm_nt(high[...], q[:, at])
    return wide[:, :channels] + wide[:, channels:] + mm_nt(low[...], q[0:channels, at])


def structure_kernel(first_half, chunks, *refs):
    *tables, q, energy, out = refs
    column = 0
    part = None
    for n in range(chunks):
        high, low = tables[2 * n : 2 * n + 2]
        more = structure_part(high, low, q, column)
        part = more if part is None else part + more
        column += high.shape[1]
    out[...] = part
    if first_half:
        out[zero_row : zero_row + 1, :] = energy[...]


def near_kernel(sizes, near_layers, side, starts, mine, *refs):
    layers, strips = sizes
    tables, outs, live_out = refs[: 4 * len(starts)], refs[-5:-1], refs[-1]
    own = mine.shape[2]
    here = position_here()
    for j in range(side * near_layers, (side + 1) * near_layers):
        at = slice(j * own, (j + 1) * own)
        slot = slot_of(*near_domain(j, here, sizes, near_layers), here, sizes)
        record = mine[slot, 0:8, :]
        live = jnp.where(record[ROW_KIND : ROW_KIND + 1] >= 0.0, 1.0, 0.0)
        live_out[:, at] = jnp.broadcast_to(live, (8, own))
        if not starts:
            store_phases(record, layers, strips, outs, j * own)
        for n, start in enumerate(starts):
            parts = tables[4 * n : 4 * n + 4]
            end = start + parts[0].shape[1] // own

            def take():
                column = pl.multiple_of((slot - start) * own, own)
                for part, out in zip(parts, outs):
                    out[:, at] = part[:, pl.ds(column, own)]

            if len(starts) == 1:
                take()
            else:
                pl.when((slot >= start) & (slot < end))(take)


def column_kernel(sizes, near_layers, data, *refs):
    tables, outs = refs[:4], refs[4:]
    for n in range(data.shape[0]):
        store_phases(data[n, 0:8, :], *sizes, tables, n * data.shape[2])
    near_kernel(sizes, near_layers, 0, [0], data, *tables, *outs)


def fall_kernel(pairs, fall_out):
    domains, basis = fall_out.shape[0:2]
    spacing = basis_reach / (basis - 1)
    for j in range(domains):
        d = pairs[j, 5]
        quarter = d * (1.0 / envelope_reach)
        square = quarter * quarter
        envelope = 1.0 / (1.0 + square * square)
        over = 1.0 / d
        slope = -envelope * envelope * (4.0 / envelope_reach) * square * quarter * over
        lean = envelope * (-2.0 / (spacing * root)) * over
        u = d * (root / spacing)
        for b in range(basis):
            t, e = pair_basis(u, float(b))
            fall_out[j, b] = e * (lean * t + slope)


def wave_weights(part, other, scale):
    sums = part[...] + other[...]
    return sums, scale[...] * sums


def charge_gradient(weight, high, low):
    channels = weight.shape[1]
    top, bottom = split(weight.T)
    wide = mm(jnp.concatenate([top, bottom], axis=0), high[...])
    return wide[:channels] + wide[channels:] + mm(top, low[...])


def pull_kernel(part, other, scale, high, low, grad_out, energy_out):
    sums, weight = wave_weights(part, other, scale)
    grad_out[...] = charge_gradient(weight, high, low)
    energy_out[...] = jnp.sum(weight * sums, axis=0, keepdims=True)


def backward_kernel(
    sizes,
    dims,
    all_atoms,
    near_layers,
    cos_own,
    cos_other,
    grad_in,
    sin_energy,
    scale,
    cos_high,
    cos_low,
    live_in,
    fall_in,
    wb3,
    re3,
    pair_in,
    slope_in,
    readout_in,
    own_out,
    other_out,
    energy_out,
    b_ref,
    f_ref,
    t_ref,
    hot_ref,
    col_ref,
):
    layers, strips = sizes
    own, width, tall, slots, kinds = dims
    layer, strip = position_here()
    basis = fall_in.shape[1]
    channels = slope_in.shape[0]
    domains = 2 * near_layers
    lanes_all = domains * own

    base = ((layer * strips + (strip - (strip & 1))) * own).astype(f32)
    groups = 8
    size = 2 * own // groups
    group = rows((groups, own))
    member = rows((size, own))
    for j in range(domains):
        target = (pair_in[j, 4] - base).astype(i32)
        t_ref[j, 0] = target // size
        t_ref[j, 1] = target & (size - 1)
        for m in range(slots):
            one = jnp.where(t_ref[j, 1, m : m + 1, :] == member, 1.0, 0.0)
            col_ref[j, :, m * own : (m + 1) * own] = one.astype(bf16)

    sums, weight = wave_weights(cos_own, cos_other, scale)
    grad = grad_in[...] + charge_gradient(weight, cos_high, cos_low)
    grad = grad * live_in[0:1, :]
    both = jnp.concatenate([grad, readout_in[:, 0:lanes_all]], axis=0)
    grad = mm(wb3[...], right3(both)) * slope_in[:, 0:lanes_all]
    b_ref[...] = mm(re3[...], right3(grad))

    found = None
    own_out[...] = jnp.zeros_like(own_out)
    for j in range(domains):
        code = pair_in[j, 3]
        same = [code == float(s) for s in range(kinds)]
        force = jnp.zeros((slots, own), f32)
        for b in range(basis):
            chosen = jnp.zeros((slots, own), f32)
            for s in range(kinds):
                k = s * basis + b
                row = b_ref[k : k + 1, j * own : (j + 1) * own]
                chosen = jnp.where(same[s], row, chosen)
            force = force + fall_in[j, b] * chosen
        for r in range(3):
            part = force * pair_in[j, r]
            high = part.astype(bf16).astype(f32)
            f_ref[j, 2 * r] = high
            f_ref[j, 2 * r + 1] = part - high
            if j == 1:
                own_out[r : r + 1, :] = -jnp.sum(part, axis=0, keepdims=True)
        for m in range(slots):
            at = slice(m * own, (m + 1) * own)
            hit = t_ref[j, 0, m : m + 1, :] == group
            for r in range(3):
                hot = [
                    jnp.where(hit, f_ref[j, 2 * r + n, m : m + 1, :], 0.0) for n in range(2)
                ]
                here = slice(2 * r * groups, 2 * (r + 1) * groups)
                hot_ref[j, here, at] = jnp.concatenate(hot, axis=0).astype(bf16)
        more = mm_nt(hot_ref[j], col_ref[j])
        found = more if found is None else found + more

    spread = jnp.where(rows((size, own)) == (lanes((size, own)) & (size - 1)), 1.0, 0.0)
    wide = jnp.dot(found, spread, precision=highest, preferred_element_type=f32)
    half = groups // 2
    fits = rows((half, own)) == lanes((half, own)) // size
    odd = (strip & 1) == 1
    other_out[...] = jnp.zeros_like(other_out)
    for r in range(3):
        both = wide[2 * r * groups : (2 * r + 1) * groups]
        both = both + wide[(2 * r + 1) * groups : (2 * r + 2) * groups]
        sides = [
            jnp.sum(jnp.where(fits, both[n * half : (n + 1) * half], 0.0), axis=0, keepdims=True)
            for n in range(2)
        ]
        own_out[r : r + 1, :] += jnp.where(odd, sides[1], sides[0])
        other_out[r : r + 1, :] = jnp.where(odd, sides[0], sides[1])

    local = sums[zero_row : zero_row + 1]
    ewald = sin_energy[...] + jnp.sum(weight * sums, axis=0, keepdims=True)
    energy = jnp.sum(local + 0.5 * ewald, axis=1, keepdims=True)
    energy_out[...] = jnp.broadcast_to(energy / all_atoms, energy_out.shape)


def ewald_kernel(
    sizes,
    cos_own,
    cos_other,
    sin_own,
    sin_other,
    scale,
    cos_high,
    cos_low,
    sin_high,
    sin_low,
    q_in,
    out,
):
    layers, strips = sizes
    channels = q_in.shape[0] // 2
    waves = cos_high.shape[0]
    own = out.shape[1]
    mine = slice(own, 2 * own)
    charge_high = q_in[0:channels, 0:own]
    charge_low = q_in[channels : 2 * channels, 0:own]
    charges = jnp.concatenate([charge_high, charge_low, charge_high], axis=0)
    halves = ((cos_own, cos_other), (sin_own, sin_other))
    along_cos, along_sin = [
        mm(left3(wave_weights(part, other, scale)[1]), charges)
        for part, other in halves
    ]
    cosine = cos_high[:, mine].astype(f32) + cos_low[:, mine].astype(f32)
    sine = sin_high[:, mine].astype(f32) + sin_low[:, mine].astype(f32)
    turn = cosine * along_sin - sine * along_cos
    index = lanes((8, waves))
    axis = rows((8, waves))
    part_x = (index // (KGRID * KGRID)).astype(f32) / (strips * width_x)
    part_y = ((index // KGRID) % KGRID - KGRID // 2).astype(f32) / width_y
    part_z = (index % KGRID - KGRID // 2).astype(f32) / (layers * width_z)
    wave = jnp.where(axis == 0, part_x, jnp.where(axis == 1, part_y, part_z))
    wave = jnp.where(axis < 3, wave * (2.0 * math.pi), 0.0)
    out[...] = mm(left3(wave), right3(turn))


def final_kernel(pos, vel, frc, spec, mass, own, ewald, other, moved_out, vel_out, frc_out):
    factor = mass_of(spec[...], mass)
    half_velocity = vel[...] + 0.5 * time_step * frc[...] * factor
    moved_out[...] = pos[...] + time_step * half_velocity
    forces_new = -(own[0:3, :] + ewald[0:3, :] + other[0:3, :])
    frc_out[...] = forces_new
    vel_out[...] = half_velocity + 0.5 * time_step * forces_new * factor


def exchange(x, axis, bit):
    count = lax.axis_size(axis)
    return lax.ppermute(x, axis, [(i, i ^ bit) for i in range(count)])


MIB = 1024 * 1024
vmem = pl.BlockSpec(memory_space=pltpu.VMEM)


def call(kernel, name, outs, ins, scratch=(), unread=(), alias={}, limit=8, work=10**8):
    anywhere = pl.BlockSpec(memory_space=pl.ANY)

    return pl.pallas_call(
        kernel,
        out_shape=[jax.ShapeDtypeStruct(shape, dtype) for shape, dtype in outs],
        in_specs=[anywhere if n in unread else vmem for n in range(len(ins))],
        out_specs=[vmem] * len(outs),
        scratch_shapes=[pltpu.VMEM(shape, dtype) for shape, dtype in scratch],
        compiler_params=pltpu.CompilerParams(vmem_limit_bytes=limit and limit * MIB),
        cost_estimate=pl.CostEstimate(flops=work, bytes_accessed=MIB, transcendentals=0),
        input_output_aliases=alias,
        name=name,
    )(*ins)


def local(
    positions,
    velocities,
    forces,
    species,
    counts,
    neighbours,
    send_inplane,
    send_normal,
    embedding,
    inverse_mass,
    radial_weight,
    mix_weight,
    self_weight,
    charge_weight,
    readout_weight,
    readout_vector,
    kernel_filter,
):
    layers = lax.axis_size("gz")
    strips = lax.axis_size("xy")
    sizes = (layers, strips)
    own = positions.shape[1]
    slots = neighbours.shape[0]
    kinds, channels = embedding.shape
    basis = radial_weight.shape[0]
    dims = (own, send_inplane.shape[1], send_normal.shape[1], slots, kinds)
    all_atoms = own * layers * strips
    waves = KGRID**3
    kind_row = species[None, :]
    total = layers * (strips // 2)
    early = total <= 16
    group = min(16, total)
    block_size = min(4, group)
    near_layers = min(3, layers)
    near = 2 * near_layers
    depth = kinds * basis + -(-kinds // 16) * 16

    (block,) = call(
        functools.partial(pack_kernel, sizes),
        "pack",
        [((ROW_LISTS + slots, own), f32)],
        (
            counts[None],
            inverse_mass[None],
            positions,
            velocities,
            forces,
            kind_row,
            neighbours,
            send_inplane,
            send_normal,
        ),
        limit=None,
    )
    def near_part(side, data, tables, starts, given=()):
        parts = [t for table in tables for t in table]
        return call(
            functools.partial(near_kernel, sizes, near_layers, side, starts),
            "near",
            [((waves, near * own), bf16)] * 4 + [((8, near * own), f32)],
            (data, *parts, *given),
            unread=range(1 + len(parts), 1 + len(parts) + len(given)),
            alias={1 + len(parts) + n: n for n in range(len(given))},
            limit=8 if early else 32,
            work=4 * 10**9,
        )

    def phases(data, ahead):
        wide = data.shape[0] * own
        return call(
            functools.partial(tables_kernel, sizes),
            "tables",
            [((waves, wide), bf16)] * 4 + [((8, own), f32)],
            (data, ahead),
            unread=(1,),
            work=4 * 10**9,
        )

    arrived = exchange(block, "gz", 1)[None]
    data, scale = call(
        functools.partial(lift_kernel, all_atoms),
        "lift",
        [((1, *block.shape), f32), (kernel_filter.shape, f32)],
        (block, kernel_filter),
        limit=1,
        work=8 * 10**9,
    )
    data = jnp.concatenate([data, arrived], axis=0)
    rex3, wcu3, wb3, re3, rv = call(
        weights_kernel,
        "weights",
        [
            ((channels, 3 * depth), bf16),
            ((2 * channels, 3 * channels), bf16),
            ((channels, 6 * channels), bf16),
            ((kinds * basis, 3 * channels), bf16),
            ((channels, channels), f32),
        ],
        (
            embedding,
            radial_weight,
            mix_weight,
            self_weight,
            charge_weight,
            readout_weight,
            readout_vector[None, :],
            data,
        ),
        limit=None,
        unread=(7,),
        work=4 * 10**9,
    )
    bit = 2
    while bit < layers:
        data = jnp.concatenate([data, exchange(data, "gz", bit)], axis=0)
        bit *= 2
    tables, starts, zeros = [], [], []
    if early:
        *both, zero = call(
            functools.partial(column_kernel, sizes, near_layers),
            "column",
            [((waves, layers * own), bf16)] * 4
            + [((waves, near * own), bf16)] * 4
            + [((8, near * own), f32)],
            (data,),
            work=4 * 10**9,
        )
        tables.append(both[:4])
        starts.append(0)
        near_tables = [*both[4:], zero]
    else:
        near_tables = near_part(0, data, tables, starts)
    bit = 2
    while bit < strips:
        bits = [3 * bit, bit, 2 * bit] if 2 * bit < strips else [bit]
        parts = [exchange(data, "xy", n) for n in bits]
        for n, part in enumerate(parts):
            if early:
                *table, zero = phases(part, near_tables[4] if n == 0 else block)
                zeros.append(zero)
                tables.append(table)
                starts.append((n + 1) * data.shape[0])
        data = jnp.concatenate([data] + parts, axis=0)
        bit *= 4
    records = data[:, 0:8, :]
    for zero in zeros[:2]:
        records = records + zero
    theirs = exchange(records, "xy", 1)

    *near_tables, live = near_part(1, data, tables[1:3], starts[1:3], near_tables)
    chunk = min(16, total)
    outs = [
        ((2 * channels, chunk * own), bf16),
        ((1, channels), f32),
        ((near + 1, PAIR_BLOCKS, slots, own), f32),
        ((channels, (near + 1) * own), f32),
        ((channels, (near + 1) * own), f32),
    ]
    scratch = [
        ((total, 8, own), f32),
        ((group, slots, own), f32),
        ((group, kinds, slots, own), f32),
        ((3 * depth, group * own), bf16),
        ((8, own), f32),
    ]
    if not early:
        outs += [((waves, channels), f32)] * 2
        scratch += [((waves, chunk * own), bf16)] * 4
    q, energy_row, pairs, slope, readout, *sums = call(
        functools.partial(forward_kernel, sizes, dims, group, block_size, near_layers, early),
        "forward",
        outs,
        (data, theirs, rex3, wcu3, rv, radial_weight),
        scratch,
        limit=16 if early else 48,
    )
    for n in range(2 if early else 0):
        parts = [t for table in tables for t in table[2 * n : 2 * n + 2]]
        sums += call(
            functools.partial(structure_kernel, n == 0, len(tables)),
            "structure",
            [((waves, channels), f32)],
            (*parts, q, energy_row),
            limit=16,
            work=10**9,
        )
    others = [exchange(part, "xy", 1) for part in sums]
    (fall,) = call(
        fall_kernel, "fall", [((near, basis, slots, own), f32)], (pairs,), work=10**9
    )
    grad, sin_energy = call(
        pull_kernel,
        "pull",
        [((channels, near * own), f32), ((1, channels), f32)],
        (sums[1], others[1], scale, *near_tables[2:]),
        limit=16,
        work=10**9,
    )
    groups = 8
    own_grad, other_grad, energy = call(
        functools.partial(backward_kernel, sizes, dims, all_atoms, near_layers),
        "backward",
        [((8, own), f32), ((8, own), f32), ((1, channels), f32)],
        (
            sums[0],
            others[0],
            grad,
            sin_energy,
            scale,
            *near_tables[:2],
            live,
            fall,
            wb3,
            re3,
            pairs,
            slope,
            readout,
        ),
        [
            ((kinds * basis, near * own), f32),
            ((near, 6, slots, own), f32),
            ((near, 2, slots, own), i32),
            ((near, 6 * groups, slots * own), bf16),
            ((near, 2 * own // groups, slots * own), bf16),
        ],
        limit=16,
    )
    arrived = exchange(other_grad, "xy", 1)
    (ewald_grad,) = call(
        functools.partial(ewald_kernel, sizes),
        "ewald",
        [((8, own), f32)],
        (sums[0], others[0], sums[1], others[1], scale, *near_tables, q),
        work=4 * 10**9,
    )
    moved, velocities_new, forces_new = call(
        final_kernel,
        "final",
        [((3, own), f32)] * 3,
        (positions, velocities, forces, kind_row, inverse_mass[None], own_grad, ewald_grad, arrived),
        limit=1,
    )
    return (moved, velocities_new, forces_new, energy[0, 0])


def solution(mesh):
    return jax.shard_map(
        local,
        mesh=mesh,
        in_specs=(
            P(None, ("gz", "xy")),
            P(None, ("gz", "xy")),
            P(None, ("gz", "xy")),
            P(("gz", "xy")),
            P(("gz", "xy")),
            P(None, ("gz", "xy")),
            P(None, ("gz", "xy")),
            P(None, ("gz", "xy")),
            P(),
            P(),
            P(),
            P(),
            P(),
            P(),
            P(),
            P(),
            P(),
        ),
        out_specs=(P(None, ("gz", "xy")), P(None, ("gz", "xy")), P(None, ("gz", "xy")), P()),
        check_vma=False,
    )
```

```python
import functools
import math

import jax
import jax.numpy as jnp
from jax import lax
from jax.experimental import pallas as pl
from jax.experimental.pallas import tpu as pltpu
from jax.sharding import PartitionSpec as P

KGRID = 8

time_step = 0.5
width_x = 2.0
width_y = 4.0
width_z = 2.0
far_away = 1000.0
softening = 0.25
basis_reach = 6.0
envelope_reach = 4.0
highest = lax.Precision.HIGHEST
f32 = jnp.float32
bf16 = jnp.bfloat16
i32 = jnp.int32

ROW_KIND = 3
ROW_ID = 4
ROW_INPLANE = 5
ROW_ABOVE = 6
ROW_BELOW = 7
ROW_LISTS = 8
PAIR_BLOCKS = 6


def split(x):
    high = x.astype(bf16)
    return high, (x - high.astype(f32)).astype(bf16)


def mm(a, b):
    return jnp.dot(a, b, preferred_element_type=f32)


def mm_nt(a, b):
    return lax.dot_general(a, b, (((1,), (1,)), ((), ())), preferred_element_type=f32)


def left3(x):
    high, low = split(x)
    return jnp.concatenate([high, high, low], axis=1)


def right3(x):
    high, low = split(x)
    return jnp.concatenate([high, low, high], axis=0)


def lanes(shape):
    return lax.broadcasted_iota(i32, shape, len(shape) - 1)


def rows(shape):
    return lax.broadcasted_iota(i32, shape, len(shape) - 2)


def pick(table, index):
    return jnp.take_along_axis(table, index, axis=1)


def sigmoid(x):
    return 0.5 + 0.5 * jnp.tanh(0.5 * x)


def cos_sin(turns):
    half = math.pi * (turns - jnp.floor(turns + 0.5))
    sq = half * half
    sine = half * (
        1.0
        + sq
        * (
            -1.0 / 6
            + sq * (1.0 / 120 + sq * (-1.0 / 5040 + sq * (1.0 / 362880 - sq / 39916800.0)))
        )
    )
    cosine = 1.0 + sq * (
        -0.5
        + sq
        * (
            1.0 / 24
            + sq
            * (-1.0 / 720 + sq * (1.0 / 40320 + sq * (-1.0 / 3628800 + sq / 479001600.0)))
        )
    )
    return 1.0 - 2.0 * sine * sine, 2.0 * sine * cosine


def phase_tables(record, layers, strips):
    shape = (KGRID, record.shape[1])
    number = rows(shape).astype(f32)
    centred = number - float(KGRID // 2)
    cos_x, sin_x = cos_sin(number * record[0:1] / (strips * width_x))
    cos_y, sin_y = cos_sin(centred * record[1:2] / width_y)
    cos_z, sin_z = cos_sin(centred * record[2:3] / (layers * width_z))
    cos_yz, sin_yz = [], []
    for k in range(KGRID):
        c, s = cos_y[k : k + 1], sin_y[k : k + 1]
        cos_yz.append(c * cos_z - s * sin_z)
        sin_yz.append(s * cos_z + c * sin_z)
    return cos_x, sin_x, jnp.concatenate(cos_yz, axis=0), jnp.concatenate(sin_yz, axis=0)


def store_phases(record, layers, strips, refs, column):
    cos_high, cos_low, sin_high, sin_low = refs
    cos_x, sin_x, cos_yz, sin_yz = phase_tables(record, layers, strips)
    side = KGRID * KGRID
    at = pl.ds(column, record.shape[1])
    for k in range(KGRID):
        c, s = cos_x[k : k + 1], sin_x[k : k + 1]
        cosine = c * cos_yz - s * sin_yz
        sine = s * cos_yz + c * sin_yz
        here = slice(k * side, (k + 1) * side)
        cos_high[here, at], cos_low[here, at] = split(cosine)
        sin_high[here, at], sin_low[here, at] = split(sine)


ORDER_GZ = (0, 2, 3, 1)
ORDER_XY = (0, 3, 1, 2)


def by_digits(x, count, table):
    result, shift = 0, 0
    while 1 << (shift + 1) < count:
        d = (x >> shift) & 3
        mapped = jnp.where(d == 1, table[1], jnp.where(d == 2, table[2], table[3]))
        result = result | (jnp.where(d == 0, 0, mapped) << shift)
        shift += 2
    return result | ((x >> shift) << shift)


def inverse(order):
    return tuple(order.index(n) for n in range(4))


def domain_at(slot, here, sizes):
    layer, strip = here
    layers, strips = sizes
    z = by_digits(slot & (layers - 1), layers, ORDER_GZ)
    x = by_digits(slot // layers, strips // 2, ORDER_XY)
    return layer ^ z, strip ^ (2 * x)


def slot_of(g, p, here, sizes):
    layer, strip = here
    layers, strips = sizes
    z = by_digits(g ^ layer, layers, inverse(ORDER_GZ))
    x = by_digits((p ^ strip) >> 1, strips // 2, inverse(ORDER_XY))
    return z + layers * x


def near_domain(j, here, sizes, near_layers):
    layer, strip = here
    layers, strips = sizes
    g = lax.rem(layer - 1 + j % near_layers + layers, layers)
    step = (j // near_layers) * (2 - 4 * (strip & 1))
    return g, lax.rem(strip + step + strips, strips)


def position_here():
    return lax.axis_index("gz").astype(i32), lax.axis_index("xy").astype(i32)


def mass_of(kind, mass):
    factor = jnp.zeros(kind.shape, f32)
    for s in range(mass.shape[1]):
        factor = factor + jnp.where(kind == s, mass[0:1, s : s + 1], 0.0)
    return factor


def pack_kernel(sizes, cnt, mass, pos, vel, frc, spec, nbr, inplane, normal, out):
    layers, strips = sizes
    own = pos.shape[1]
    layer, strip = position_here()
    kind = spec[...]
    half_velocity = vel[...] + 0.5 * time_step * frc[...] * mass_of(kind, mass)
    moved = pos[...] + time_step * half_velocity
    lane = lanes((1, own))
    code = jnp.where(lane < cnt[...], kind, -1).astype(f32)
    number = ((layer * strips + strip) * own + lane).astype(f32)
    out[0:3, :] = moved
    out[ROW_KIND : ROW_KIND + 1, :] = code
    out[ROW_ID : ROW_ID + 1, :] = number
    lists = inplane[...].astype(f32)
    width = lists.shape[1]
    out[ROW_INPLANE : ROW_BELOW + 1, :] = jnp.zeros((3, own), f32)
    out[ROW_INPLANE : ROW_INPLANE + 1, 0:width] = lists[1:2]
    out[ROW_INPLANE : ROW_INPLANE + 1, width : 2 * width] = lists[0:1]
    lists = normal[...].astype(f32)
    tall = lists.shape[1]
    out[ROW_ABOVE : ROW_ABOVE + 1, 2 * width : 2 * width + tall] = lists[1:2]
    out[ROW_BELOW : ROW_BELOW + 1, 0:tall] = lists[0:1]
    out[ROW_LISTS:, :] = nbr[...].astype(f32)


def weights_kernel(
    embedding,
    radial,
    mix,
    self_w,
    charge_w,
    readout_w,
    readout_v,
    ahead,
    rex3,
    wcu3,
    wb3,
    re3,
    rv_out,
):
    kinds, channels = embedding.shape
    both = jnp.concatenate([mix[...], self_w[...]], axis=1)
    both = jnp.dot(embedding[...], both, precision=highest, preferred_element_type=f32)
    mixed, selfed = both[:, :channels], both[:, channels:]
    table = jnp.concatenate([mixed[s : s + 1] * radial[...] for s in range(kinds)], axis=0)
    rest = jnp.zeros((channels - table.shape[0] - kinds, channels), f32)
    wide = jnp.concatenate([table, selfed, rest], axis=0).T
    rex3[...] = left3(wide[:, : rex3.shape[1] // 3])
    wcu3[...] = left3(jnp.concatenate([charge_w[...].T, readout_w[...].T], axis=0))
    wb3[...] = left3(jnp.concatenate([charge_w[...], readout_w[...]], axis=1))
    re3[...] = left3(table)
    rv_out[...] = jnp.broadcast_to(readout_v[...], (channels, channels)).T


def lift_kernel(all_atoms, block, kernel_filter, out, filter_out):
    out[0] = block[...]
    keeper = jnp.where(rows(kernel_filter.shape) == zero_row, 0.0, 1.0 / all_atoms)
    filter_out[...] = keeper * kernel_filter[...]


def tables_kernel(sizes, data, ahead, *refs):
    own = data.shape[2]
    refs[4][...] = jnp.zeros_like(refs[4])
    refs = refs[:4]
    for n in range(data.shape[0]):
        store_phases(data[n, 0:8, :], *sizes, refs, n * own)


root = math.sqrt(math.log2(math.e))


def pair_basis(u, b):
    t = u - b * root
    return t, jnp.exp2(-(t * t))


def forward_kernel(
    sizes,
    dims,
    group,
    block,
    near_layers,
    early,
    mine,
    theirs,
    rex3,
    wcu3,
    rv_ref,
    radial,
    later_wb3,
    later_re3,
    q_out,
    energy_out,
    pair_out,
    slope_out,
    readout_out,
    *rest,
):
    layers, strips = sizes
    own, width, tall, slots, kinds = dims
    if early:
        first, u_ref, w_ref, x_ref, energy_ref = rest
    else:
        cos_out, sin_out, first, u_ref, w_ref, x_ref, energy_ref, *tables = rest
    here = position_here()
    basis = radial.shape[0]
    channels = rv_ref.shape[0]
    total = mine.shape[0]
    near = 2 * near_layers
    lane8 = lanes((8, own))
    row8 = rows((8, own))
    energy_ref[...] = jnp.zeros_like(energy_ref)
    box = strips * width_x
    partner = (here[0], here[1] ^ 1)

    def first_step(i):
        g, p = domain_at(i, here, sizes)
        lower = theirs[slot_of(g, lax.rem(p + strips - 1, strips), partner, sizes)]
        upper = theirs[slot_of(g, lax.rem(p + 1, strips), partner, sizes)]
        at = jnp.broadcast_to(lower[ROW_INPLANE : ROW_INPLANE + 1], (8, own)).astype(i32)
        from_lower = pick(lower, at)
        at = jnp.broadcast_to(upper[ROW_INPLANE : ROW_INPLANE + 1], (8, own)).astype(i32)
        from_upper = pick(upper, at)
        down = jnp.where(p == 0, -box, 0.0)
        up = jnp.where(p == strips - 1, box, 0.0)
        shift = jnp.where(row8 == 0, jnp.where(lane8 < width, down, up), 0.0)
        first[i] = jnp.where(lane8 < width, from_lower, from_upper) + shift

    def first_steps(n, carry):
        for k in range(group):
            first_step(n * group + k)
        return carry

    local_first = group % layers == 0
    if not local_first:
        lax.fori_loop(0, total // group, first_steps, 0)

    bound = jnp.where((row8 == ROW_KIND) | (row8 == ROW_ID), -1.0, 0.0)
    padding = jnp.where(row8 < 3, far_away, -1.0)
    spacing = basis_reach / (basis - 1)

    def normal_ghosts(g, p, move, row):
        other = lax.rem(g + move + layers, layers)
        j = slot_of(other, p, here, sizes)
        near_by = mine[j, 0:8, :]
        at = jnp.broadcast_to(near_by[row : row + 1], (8, own)).astype(i32)
        inside = at < own
        at = at & (own - 1)
        found = jnp.where(inside, pick(near_by, at), pick(first[j], at))
        beyond = (g + move < 0) | (g + move >= layers)
        return jnp.where(beyond, bound, found)

    def geometry(i, k):
        g, p = domain_at(i, here, sizes)
        record = mine[i, 0:8, :]
        below = normal_ghosts(g, p, -1, ROW_ABOVE)
        above = normal_ghosts(g, p, 1, ROW_BELOW)
        parts = (
            record,
            jnp.where(lane8 < 2 * width, first[i], below),
            jnp.where(lane8 < tall, above, padding),
        )
        index = mine[i, ROW_LISTS : ROW_LISTS + slots, :].astype(i32)
        part = index // own
        at = index & (own - 1)

        def gathered(r):
            a, b, c = [pick(jnp.broadcast_to(q[r : r + 1], (slots, own)), at) for q in parts]
            return jnp.where(part == 0, a, jnp.where(part == 1, b, c))

        dx = gathered(0) - record[0:1]
        dy = gathered(1) - record[1:2]
        dz = gathered(2) - record[2:3]
        code = gathered(ROW_KIND)
        d = jnp.sqrt(dx * dx + dy * dy + dz * dz + softening)
        quarter = d * (1.0 / envelope_reach)
        square = quarter * quarter
        envelope = 1.0 / (1.0 + square * square)
        u_ref[k] = d * (root / spacing)
        for s in range(kinds):
            w_ref[k, s] = jnp.where(code == float(s), envelope, 0.0)
        turn = lax.rem(g - here[0] + 1 + layers, layers)
        side = here[1] + 2 - 4 * (here[1] & 1)
        strip_step = jnp.where(p == here[1], 0, jnp.where(p == lax.rem(side + strips, strips), 1, 2))
        j = jnp.where((turn < near_layers) & (strip_step < 2), strip_step * near_layers + turn, near)
        pair_out[j, 0] = dx
        pair_out[j, 1] = dy
        pair_out[j, 2] = dz
        pair_out[j, 3] = code
        pair_out[j, 4] = gathered(ROW_ID)
        pair_out[j, 5] = d
        return record[ROW_KIND : ROW_KIND + 1], j

    def basis_sums(k, kind_row):
        centre = rows((basis, own)).astype(f32)
        sums = [jnp.zeros((basis, own), f32) for s in range(kinds)]
        for m in range(slots):
            t, e = pair_basis(u_ref[k, m : m + 1, :], centre)
            for s in range(kinds):
                sums[s] = sums[s] + e * w_ref[k, s, m : m + 1, :]
        tail = x_ref.shape[0] // 3 - kinds * basis
        one_hot = jnp.where(rows((tail, own)).astype(f32) == kind_row, 1.0, 0.0)
        x_ref[:, k * own : (k + 1) * own] = right3(jnp.concatenate(sums + [one_hot], axis=0))

    def block_step(start, place, offset):
        found = [geometry(start + k, offset + k) for k in range(block)]
        for k in range(block):
            basis_sums(offset + k, found[k][0])
        live = jnp.concatenate([kind_row for kind_row, _ in found], axis=1) >= 0.0
        pre = mm(rex3[...], x_ref[:, offset * own : (offset + block) * own])
        gate = sigmoid(pre)
        hidden = pre * gate
        both = mm(wcu3[...], right3(hidden))
        charges = jnp.where(live, both[:channels], 0.0)
        readout = both[channels:]
        readout_gate = sigmoid(readout)
        rv = jnp.concatenate([rv_ref[...]] * block, axis=1)
        scaled = jnp.where(live, rv * readout_gate, 0.0)
        local = scaled * readout
        slope = gate * (1.0 + pre * (1.0 - gate))
        back = scaled * (1.0 + readout * (1.0 - readout_gate))
        wide = jnp.sum(local.reshape(channels // 8, 8, block * own), axis=0)
        for k in range(block):
            energy_ref[...] += wide[:, k * own : (k + 1) * own]
        column = pl.multiple_of(place * own, own)
        high, low = split(charges)
        q_out[0:channels, pl.ds(column, block * own)] = high
        q_out[channels : 2 * channels, pl.ds(column, block * own)] = low
        for k in range(block):
            column = pl.multiple_of(found[k][1] * own, own)
            slope_out[:, pl.ds(column, own)] = slope[:, k * own : (k + 1) * own]
            readout_out[:, pl.ds(column, own)] = back[:, k * own : (k + 1) * own]

    def group_step(n, place):
        if local_first:
            for k in range(group):
                first_step(n * group + k)
        for offset in range(0, group, block):
            block_step(n * group + offset, place + offset, offset)

    if early:

        def steps(n, carry):
            group_step(n, n * group)
            return carry

        lax.fori_loop(0, total // group, steps, 0, unroll=total == group)
    else:
        chunk = q_out.shape[1] // own

        def chunk_step(c, carry):
            def steps(n, inner):
                group_step(c * (chunk // group) + n, n * group)
                return inner

            def phases(n, inner):
                record = mine[c * chunk + n, 0:8, :]
                store_phases(record, layers, strips, tables, pl.multiple_of(n * own, own))
                return inner

            lax.fori_loop(0, chunk // group, steps, 0)
            lax.fori_loop(0, chunk, phases, 0)
            for out, high, low in ((cos_out, *tables[:2]), (sin_out, *tables[2:])):
                part = structure_part(high, low, q_out, 0)

                @pl.when(c == 0)
                def _():
                    out[...] = part

                @pl.when(c > 0)
                def _():
                    out[...] += part

            return carry

        lax.fori_loop(0, total // chunk, chunk_step, 0)
    energy_out[...] = jnp.sum(energy_ref[...], axis=0, keepdims=True)
    if not early:
        cos_out[zero_row : zero_row + 1, :] = energy_out[...]


zero_row = (KGRID // 2) * KGRID + KGRID // 2


def structure_part(high, low, q, column):
    channels = q.shape[0] // 2
    at = slice(column, column + high.shape[1])
    wide = mm_nt(high[...], q[:, at])
    return wide[:, :channels] + wide[:, channels:] + mm_nt(low[...], q[0:channels, at])


def structure_kernel(first_half, chunks, *refs):
    *tables, q, energy, out = refs
    column = 0
    part = None
    for n in range(chunks):
        high, low = tables[2 * n : 2 * n + 2]
        more = structure_part(high, low, q, column)
        part = more if part is None else part + more
        column += high.shape[1]
    out[...] = part
    if first_half:
        out[zero_row : zero_row + 1, :] = energy[...]


def near_kernel(sizes, near_layers, side, starts, mine, *refs):
    layers, strips = sizes
    tables, outs, live_out = refs[: 4 * len(starts)], refs[-5:-1], refs[-1]
    own = mine.shape[2]
    here = position_here()
    for j in range(side * near_layers, (side + 1) * near_layers):
        at = slice(j * own, (j + 1) * own)
        slot = slot_of(*near_domain(j, here, sizes, near_layers), here, sizes)
        record = mine[slot, 0:8, :]
        live = jnp.where(record[ROW_KIND : ROW_KIND + 1] >= 0.0, 1.0, 0.0)
        live_out[:, at] = jnp.broadcast_to(live, (8, own))
        if not starts:
            store_phases(record, layers, strips, outs, j * own)
        for n, start in enumerate(starts):
            parts = tables[4 * n : 4 * n + 4]
            end = start + parts[0].shape[1] // own

            def take():
                column = pl.multiple_of((slot - start) * own, own)
                for part, out in zip(parts, outs):
                    out[:, at] = part[:, pl.ds(column, own)]

            if len(starts) == 1:
                take()
            else:
                pl.when((slot >= start) & (slot < end))(take)


def column_kernel(sizes, near_layers, data, *refs):
    tables, outs = refs[:4], refs[4:]
    for n in range(data.shape[0]):
        store_phases(data[n, 0:8, :], *sizes, tables, n * data.shape[2])
    near_kernel(sizes, near_layers, 0, [0], data, *tables, *outs)


def fall_kernel(pairs, fall_out):
    domains, basis = fall_out.shape[0:2]
    spacing = basis_reach / (basis - 1)
    for j in range(domains):
        d = pairs[j, 5]
        quarter = d * (1.0 / envelope_reach)
        square = quarter * quarter
        envelope = 1.0 / (1.0 + square * square)
        over = 1.0 / d
        slope = -envelope * envelope * (4.0 / envelope_reach) * square * quarter * over
        lean = envelope * (-2.0 / (spacing * root)) * over
        u = d * (root / spacing)
        for b in range(basis):
            t, e = pair_basis(u, float(b))
            fall_out[j, b] = e * (lean * t + slope)


def wave_weights(part, other, scale):
    sums = part[...] + other[...]
    return sums, scale[...] * sums


def charge_gradient(weight, high, low):
    channels = weight.shape[1]
    top, bottom = split(weight.T)
    wide = mm(jnp.concatenate([top, bottom], axis=0), high[...])
    return wide[:channels] + wide[channels:] + mm(top, low[...])


def pull_kernel(part, other, scale, high, low, grad_out, energy_out):
    sums, weight = wave_weights(part, other, scale)
    grad_out[...] = charge_gradient(weight, high, low)
    energy_out[...] = jnp.sum(weight * sums, axis=0, keepdims=True)


def backward_kernel(
    sizes,
    dims,
    all_atoms,
    near_layers,
    cos_own,
    cos_other,
    grad_in,
    sin_energy,
    scale,
    cos_high,
    cos_low,
    live_in,
    fall_in,
    wb3,
    re3,
    pair_in,
    slope_in,
    readout_in,
    own_out,
    other_out,
    energy_out,
    b_ref,
    f_ref,
    t_ref,
    hot_ref,
    col_ref,
):
    layers, strips = sizes
    own, width, tall, slots, kinds = dims
    layer, strip = position_here()
    basis = fall_in.shape[1]
    channels = slope_in.shape[0]
    domains = 2 * near_layers
    lanes_all = domains * own

    base = ((layer * strips + (strip - (strip & 1))) * own).astype(f32)
    groups = 8
    size = 2 * own // groups
    group = rows((groups, own))
    member = rows((size, own))
    for j in range(domains):
        target = (pair_in[j, 4] - base).astype(i32)
        t_ref[j, 0] = target // size
        t_ref[j, 1] = target & (size - 1)
        for m in range(slots):
            one = jnp.where(t_ref[j, 1, m : m + 1, :] == member, 1.0, 0.0)
            col_ref[j, :, m * own : (m + 1) * own] = one.astype(bf16)

    sums, weight = wave_weights(cos_own, cos_other, scale)
    grad = grad_in[...] + charge_gradient(weight, cos_high, cos_low)
    grad = grad * live_in[0:1, :]
    both = jnp.concatenate([grad, readout_in[:, 0:lanes_all]], axis=0)
    grad = mm(wb3[...], right3(both)) * slope_in[:, 0:lanes_all]
    b_ref[...] = mm(re3[...], right3(grad))

    found = None
    own_out[...] = jnp.zeros_like(own_out)
    for j in range(domains):
        code = pair_in[j, 3]
        same = [code == float(s) for s in range(kinds)]
        force = jnp.zeros((slots, own), f32)
        for b in range(basis):
            chosen = jnp.zeros((slots, own), f32)
            for s in range(kinds):
                k = s * basis + b
                row = b_ref[k : k + 1, j * own : (j + 1) * own]
                chosen = jnp.where(same[s], row, chosen)
            force = force + fall_in[j, b] * chosen
        for r in range(3):
            part = force * pair_in[j, r]
            high = part.astype(bf16).astype(f32)
            f_ref[j, 2 * r] = high
            f_ref[j, 2 * r + 1] = part - high
            if j == 1:
                own_out[r : r + 1, :] = -jnp.sum(part, axis=0, keepdims=True)
        for m in range(slots):
            at = slice(m * own, (m + 1) * own)
            hit = t_ref[j, 0, m : m + 1, :] == group
            for r in range(3):
                hot = [
                    jnp.where(hit, f_ref[j, 2 * r + n, m : m + 1, :], 0.0) for n in range(2)
                ]
                here = slice(2 * r * groups, 2 * (r + 1) * groups)
                hot_ref[j, here, at] = jnp.concatenate(hot, axis=0).astype(bf16)
        more = mm_nt(hot_ref[j], col_ref[j])
        found = more if found is None else found + more

    spread = jnp.where(rows((size, own)) == (lanes((size, own)) & (size - 1)), 1.0, 0.0)
    wide = jnp.dot(found, spread, precision=highest, preferred_element_type=f32)
    half = groups // 2
    fits = rows((half, own)) == lanes((half, own)) // size
    odd = (strip & 1) == 1
    other_out[...] = jnp.zeros_like(other_out)
    for r in range(3):
        both = wide[2 * r * groups : (2 * r + 1) * groups]
        both = both + wide[(2 * r + 1) * groups : (2 * r + 2) * groups]
        sides = [
            jnp.sum(jnp.where(fits, both[n * half : (n + 1) * half], 0.0), axis=0, keepdims=True)
            for n in range(2)
        ]
        own_out[r : r + 1, :] += jnp.where(odd, sides[1], sides[0])
        other_out[r : r + 1, :] = jnp.where(odd, sides[0], sides[1])

    local = sums[zero_row : zero_row + 1]
    ewald = sin_energy[...] + jnp.sum(weight * sums, axis=0, keepdims=True)
    energy = jnp.sum(local + 0.5 * ewald, axis=1, keepdims=True)
    energy_out[...] = jnp.broadcast_to(energy / all_atoms, energy_out.shape)


def ewald_kernel(
    sizes,
    cos_own,
    cos_other,
    sin_own,
    sin_other,
    scale,
    cos_high,
    cos_low,
    sin_high,
    sin_low,
    q_in,
    out,
):
    layers, strips = sizes
    channels = q_in.shape[0] // 2
    waves = cos_high.shape[0]
    own = out.shape[1]
    mine = slice(own, 2 * own)
    charge_high = q_in[0:channels, 0:own]
    charge_low = q_in[channels : 2 * channels, 0:own]
    charges = jnp.concatenate([charge_high, charge_low, charge_high], axis=0)
    halves = ((cos_own, cos_other), (sin_own, sin_other))
    along_cos, along_sin = [
        mm(left3(wave_weights(part, other, scale)[1]), charges)
        for part, other in halves
    ]
    cosine = cos_high[:, mine].astype(f32) + cos_low[:, mine].astype(f32)
    sine = sin_high[:, mine].astype(f32) + sin_low[:, mine].astype(f32)
    turn = cosine * along_sin - sine * along_cos
    index = lanes((8, waves))
    axis = rows((8, waves))
    part_x = (index // (KGRID * KGRID)).astype(f32) / (strips * width_x)
    part_y = ((index // KGRID) % KGRID - KGRID // 2).astype(f32) / width_y
    part_z = (index % KGRID - KGRID // 2).astype(f32) / (layers * width_z)
    wave = jnp.where(axis == 0, part_x, jnp.where(axis == 1, part_y, part_z))
    wave = jnp.where(axis < 3, wave * (2.0 * math.pi), 0.0)
    out[...] = mm(left3(wave), right3(turn))


def final_kernel(pos, vel, frc, spec, mass, own, ewald, other, moved_out, vel_out, frc_out):
    factor = mass_of(spec[...], mass)
    half_velocity = vel[...] + 0.5 * time_step * frc[...] * factor
    moved_out[...] = pos[...] + time_step * half_velocity
    forces_new = -(own[0:3, :] + ewald[0:3, :] + other[0:3, :])
    frc_out[...] = forces_new
    vel_out[...] = half_velocity + 0.5 * time_step * forces_new * factor


def exchange(x, axis, bit):
    count = lax.axis_size(axis)
    return lax.ppermute(x, axis, [(i, i ^ bit) for i in range(count)])


MIB = 1024 * 1024
vmem = pl.BlockSpec(memory_space=pltpu.VMEM)


def call(kernel, name, outs, ins, scratch=(), unread=(), alias={}, limit=8, work=10**8):
    anywhere = pl.BlockSpec(memory_space=pl.ANY)

    return pl.pallas_call(
        kernel,
        out_shape=[jax.ShapeDtypeStruct(shape, dtype) for shape, dtype in outs],
        in_specs=[anywhere if n in unread else vmem for n in range(len(ins))],
        out_specs=[vmem] * len(outs),
        scratch_shapes=[pltpu.VMEM(shape, dtype) for shape, dtype in scratch],
        compiler_params=pltpu.CompilerParams(vmem_limit_bytes=limit and limit * MIB),
        cost_estimate=pl.CostEstimate(flops=work, bytes_accessed=MIB, transcendentals=0),
        input_output_aliases=alias,
        name=name,
    )(*ins)


def local(
    positions,
    velocities,
    forces,
    species,
    counts,
    neighbours,
    send_inplane,
    send_normal,
    embedding,
    inverse_mass,
    radial_weight,
    mix_weight,
    self_weight,
    charge_weight,
    readout_weight,
    readout_vector,
    kernel_filter,
):
    layers = lax.axis_size("gz")
    strips = lax.axis_size("xy")
    sizes = (layers, strips)
    own = positions.shape[1]
    slots = neighbours.shape[0]
    kinds, channels = embedding.shape
    basis = radial_weight.shape[0]
    dims = (own, send_inplane.shape[1], send_normal.shape[1], slots, kinds)
    all_atoms = own * layers * strips
    waves = KGRID**3
    kind_row = species[None, :]
    total = layers * (strips // 2)
    early = total <= 16
    group = min(16, total)
    block_size = min(4, group)
    near_layers = min(3, layers)
    near = 2 * near_layers
    depth = kinds * basis + -(-kinds // 16) * 16

    (block,) = call(
        functools.partial(pack_kernel, sizes),
        "pack",
        [((ROW_LISTS + slots, own), f32)],
        (
            counts[None],
            inverse_mass[None],
            positions,
            velocities,
            forces,
            kind_row,
            neighbours,
            send_inplane,
            send_normal,
        ),
        limit=None,
    )
    def near_part(side, data, tables, starts, given=()):
        parts = [t for table in tables for t in table]
        return call(
            functools.partial(near_kernel, sizes, near_layers, side, starts),
            "near",
            [((waves, near * own), bf16)] * 4 + [((8, near * own), f32)],
            (data, *parts, *given),
            unread=range(1 + len(parts), 1 + len(parts) + len(given)),
            alias={1 + len(parts) + n: n for n in range(len(given))},
            limit=8 if early else 32,
            work=4 * 10**9,
        )

    def phases(data, ahead):
        wide = data.shape[0] * own
        return call(
            functools.partial(tables_kernel, sizes),
            "tables",
            [((waves, wide), bf16)] * 4 + [((8, own), f32)],
            (data, ahead),
            unread=(1,),
            work=4 * 10**9,
        )

    data, scale = call(
        functools.partial(lift_kernel, all_atoms),
        "lift",
        [((1, *block.shape), f32), (kernel_filter.shape, f32)],
        (block, kernel_filter),
        limit=1,
        work=8 * 10**9,
    )
    rex3, wcu3, wb3, re3, rv = call(
        weights_kernel,
        "weights",
        [
            ((channels, 3 * depth), bf16),
            ((2 * channels, 3 * channels), bf16),
            ((channels, 6 * channels), bf16),
            ((kinds * basis, 3 * channels), bf16),
            ((channels, channels), f32),
        ],
        (
            embedding,
            radial_weight,
            mix_weight,
            self_weight,
            charge_weight,
            readout_weight,
            readout_vector[None, :],
            block,
        ),
        limit=None,
        unread=(7,),
        work=4 * 10**9,
    )
    bit = 1
    while bit < layers:
        bits = [bit * n for n in ORDER_GZ[1:]] if 2 * bit < layers else [bit]
        source = block[None] if bit == 1 else data
        data = jnp.concatenate([data] + [exchange(source, "gz", n) for n in bits], axis=0)
        bit *= 4

    tables, starts, zeros = [], [], []
    if early:
        *both, zero = call(
            functools.partial(column_kernel, sizes, near_layers),
            "column",
            [((waves, layers * own), bf16)] * 4
            + [((waves, near * own), bf16)] * 4
            + [((8, near * own), f32)],
            (data,),
            work=10**9,
        )
        tables.append(both[:4])
        starts.append(0)
        near_tables = [*both[4:], zero]
    else:
        near_tables = near_part(0, data, tables, starts)
    bit = 2
    while bit < strips:
        bits = [bit * n for n in ORDER_XY[1:]] if 2 * bit < strips else [bit]
        parts = [exchange(data, "xy", n) for n in bits]
        for n, part in enumerate(parts):
            if early:
                *table, zero = phases(part, near_tables[4] if n == 0 else block)
                zeros.append(zero)
                tables.append(table)
                starts.append((n + 1) * data.shape[0])
        data = jnp.concatenate([data] + parts, axis=0)
        bit *= 4
    records = data[:, 0:8, :]
    for zero in zeros[:2]:
        records = records + zero
    theirs = exchange(records, "xy", 1)

    *near_tables, live = near_part(1, data, tables[1:3], starts[1:3], near_tables)
    chunk = min(16, total)
    outs = [
        ((2 * channels, chunk * own), bf16),
        ((1, channels), f32),
        ((near + 1, PAIR_BLOCKS, slots, own), f32),
        ((channels, (near + 1) * own), f32),
        ((channels, (near + 1) * own), f32),
    ]
    scratch = [
        ((total, 8, own), f32),
        ((group, slots, own), f32),
        ((group, kinds, slots, own), f32),
        ((3 * depth, group * own), bf16),
        ((8, own), f32),
    ]
    if not early:
        outs += [((waves, channels), f32)] * 2
        scratch += [((waves, chunk * own), bf16)] * 4
    q, energy_row, pairs, slope, readout, *sums = call(
        functools.partial(forward_kernel, sizes, dims, group, block_size, near_layers, early),
        "forward",
        outs,
        (data, theirs, rex3, wcu3, rv, radial_weight, wb3, re3),
        scratch,
        limit=16 if early else 48,
    )
    for n in range(2 if early else 0):
        parts = [t for table in tables for t in table[2 * n : 2 * n + 2]]
        sums += call(
            functools.partial(structure_kernel, n == 0, len(tables)),
            "structure",
            [((waves, channels), f32)],
            (*parts, q, energy_row),
            limit=16,
            work=10**9,
        )
    others = [exchange(part, "xy", 1) for part in sums]
    (fall,) = call(
        fall_kernel, "fall", [((near, basis, slots, own), f32)], (pairs,), work=10**9
    )
    grad, sin_energy = call(
        pull_kernel,
        "pull",
        [((channels, near * own), f32), ((1, channels), f32)],
        (sums[1], others[1], scale, *near_tables[2:]),
        limit=16,
        work=10**9,
    )
    groups = 8
    own_grad, other_grad, energy = call(
        functools.partial(backward_kernel, sizes, dims, all_atoms, near_layers),
        "backward",
        [((8, own), f32), ((8, own), f32), ((1, channels), f32)],
        (
            sums[0],
            others[0],
            grad,
            sin_energy,
            scale,
            *near_tables[:2],
            live,
            fall,
            wb3,
            re3,
            pairs,
            slope,
            readout,
        ),
        [
            ((kinds * basis, near * own), f32),
            ((near, 6, slots, own), f32),
            ((near, 2, slots, own), i32),
            ((near, 6 * groups, slots * own), bf16),
            ((near, 2 * own // groups, slots * own), bf16),
        ],
        limit=16,
    )
    arrived = exchange(other_grad, "xy", 1)
    (ewald_grad,) = call(
        functools.partial(ewald_kernel, sizes),
        "ewald",
        [((8, own), f32)],
        (sums[0], others[0], sums[1], others[1], scale, *near_tables, q),
        work=4 * 10**9,
    )
    moved, velocities_new, forces_new = call(
        final_kernel,
        "final",
        [((3, own), f32)] * 3,
        (positions, velocities, forces, kind_row, inverse_mass[None], own_grad, ewald_grad, arrived),
        limit=1,
    )
    return (moved, velocities_new, forces_new, energy[0, 0])


def solution(mesh):
    return jax.shard_map(
        local,
        mesh=mesh,
        in_specs=(
            P(None, ("gz", "xy")),
            P(None, ("gz", "xy")),
            P(None, ("gz", "xy")),
            P(("gz", "xy")),
            P(("gz", "xy")),
            P(None, ("gz", "xy")),
            P(None, ("gz", "xy")),
            P(None, ("gz", "xy")),
            P(),
            P(),
            P(),
            P(),
            P(),
            P(),
            P(),
            P(),
            P(),
        ),
        out_specs=(P(None, ("gz", "xy")), P(None, ("gz", "xy")), P(None, ("gz", "xy")), P()),
        check_vma=False,
    )
```

```python
import functools
import math

import jax
import jax.numpy as jnp
from jax import lax
from jax.experimental import pallas as pl
from jax.experimental.pallas import tpu as pltpu
from jax.sharding import PartitionSpec as P

KGRID = 8

time_step = 0.5
width_x = 2.0
width_y = 4.0
width_z = 2.0
far_away = 1000.0
softening = 0.25
basis_reach = 6.0
envelope_reach = 4.0
highest = lax.Precision.HIGHEST
f32 = jnp.float32
bf16 = jnp.bfloat16
i32 = jnp.int32

ROW_KIND = 3
ROW_ID = 4
ROW_INPLANE = 5
ROW_ABOVE = 6
ROW_BELOW = 7
ROW_LISTS = 8
PAIR_BLOCKS = 6


def split(x):
    high = x.astype(bf16)
    return high, (x - high.astype(f32)).astype(bf16)


def mm(a, b):
    return jnp.dot(a, b, preferred_element_type=f32)


def mm_nt(a, b):
    return lax.dot_general(a, b, (((1,), (1,)), ((), ())), preferred_element_type=f32)


def left3(x):
    high, low = split(x)
    return jnp.concatenate([high, high, low], axis=1)


def right3(x):
    high, low = split(x)
    return jnp.concatenate([high, low, high], axis=0)


def lanes(shape):
    return lax.broadcasted_iota(i32, shape, len(shape) - 1)


def rows(shape):
    return lax.broadcasted_iota(i32, shape, len(shape) - 2)


def pick(table, index):
    return jnp.take_along_axis(table, index, axis=1)


def sigmoid(x):
    return 0.5 + 0.5 * jnp.tanh(0.5 * x)


def cos_sin(turns):
    half = math.pi * (turns - jnp.floor(turns + 0.5))
    sq = half * half
    sine = half * (
        1.0
        + sq
        * (
            -1.0 / 6
            + sq * (1.0 / 120 + sq * (-1.0 / 5040 + sq * (1.0 / 362880 - sq / 39916800.0)))
        )
    )
    cosine = 1.0 + sq * (
        -0.5
        + sq
        * (
            1.0 / 24
            + sq
            * (-1.0 / 720 + sq * (1.0 / 40320 + sq * (-1.0 / 3628800 + sq / 479001600.0)))
        )
    )
    return 1.0 - 2.0 * sine * sine, 2.0 * sine * cosine


def phase_tables(record, layers, strips):
    shape = (KGRID, record.shape[1])
    number = rows(shape).astype(f32)
    centred = number - float(KGRID // 2)
    cos_x, sin_x = cos_sin(number * record[0:1] / (strips * width_x))
    cos_y, sin_y = cos_sin(centred * record[1:2] / width_y)
    cos_z, sin_z = cos_sin(centred * record[2:3] / (layers * width_z))
    cos_yz, sin_yz = [], []
    for k in range(KGRID):
        c, s = cos_y[k : k + 1], sin_y[k : k + 1]
        cos_yz.append(c * cos_z - s * sin_z)
        sin_yz.append(s * cos_z + c * sin_z)
    return cos_x, sin_x, jnp.concatenate(cos_yz, axis=0), jnp.concatenate(sin_yz, axis=0)


def store_phases(record, layers, strips, refs, column):
    cos_high, cos_low, sin_high, sin_low = refs
    cos_x, sin_x, cos_yz, sin_yz = phase_tables(record, layers, strips)
    side = KGRID * KGRID
    at = pl.ds(column, record.shape[1])
    for k in range(KGRID):
        c, s = cos_x[k : k + 1], sin_x[k : k + 1]
        cosine = c * cos_yz - s * sin_yz
        sine = s * cos_yz + c * sin_yz
        here = slice(k * side, (k + 1) * side)
        cos_high[here, at], cos_low[here, at] = split(cosine)
        sin_high[here, at], sin_low[here, at] = split(sine)


ORDER_GZ = (0, 2, 3, 1)
ORDER_XY = (0, 3, 1, 2)


def by_digits(x, count, table):
    result, shift = 0, 0
    while 1 << (shift + 1) < count:
        d = (x >> shift) & 3
        mapped = jnp.where(d == 1, table[1], jnp.where(d == 2, table[2], table[3]))
        result = result | (jnp.where(d == 0, 0, mapped) << shift)
        shift += 2
    return result | ((x >> shift) << shift)


def inverse(order):
    return tuple(order.index(n) for n in range(4))


def domain_at(slot, here, sizes):
    layer, strip = here
    layers, strips = sizes
    z = by_digits(slot & (layers - 1), layers, ORDER_GZ)
    x = by_digits(slot // layers, strips // 2, ORDER_XY)
    return layer ^ z, strip ^ (2 * x)


def slot_of(g, p, here, sizes):
    layer, strip = here
    layers, strips = sizes
    z = by_digits(g ^ layer, layers, inverse(ORDER_GZ))
    x = by_digits((p ^ strip) >> 1, strips // 2, inverse(ORDER_XY))
    return z + layers * x


def near_domain(j, here, sizes, near_layers):
    layer, strip = here
    layers, strips = sizes
    g = lax.rem(layer - 1 + j % near_layers + layers, layers)
    step = (j // near_layers) * (2 - 4 * (strip & 1))
    return g, lax.rem(strip + step + strips, strips)


def position_here():
    return lax.axis_index("gz").astype(i32), lax.axis_index("xy").astype(i32)


def mass_of(kind, mass):
    factor = jnp.zeros(kind.shape, f32)
    for s in range(mass.shape[1]):
        factor = factor + jnp.where(kind == s, mass[0:1, s : s + 1], 0.0)
    return factor


def pack_kernel(sizes, cnt, mass, pos, vel, frc, spec, nbr, inplane, normal, out):
    layers, strips = sizes
    own = pos.shape[1]
    layer, strip = position_here()
    kind = spec[...]
    half_velocity = vel[...] + 0.5 * time_step * frc[...] * mass_of(kind, mass)
    moved = pos[...] + time_step * half_velocity
    lane = lanes((1, own))
    code = jnp.where(lane < cnt[...], kind, -1).astype(f32)
    number = ((layer * strips + strip) * own + lane).astype(f32)
    out[0:3, :] = moved
    out[ROW_KIND : ROW_KIND + 1, :] = code
    out[ROW_ID : ROW_ID + 1, :] = number
    lists = inplane[...].astype(f32)
    width = lists.shape[1]
    out[ROW_INPLANE : ROW_BELOW + 1, :] = jnp.zeros((3, own), f32)
    out[ROW_INPLANE : ROW_INPLANE + 1, 0:width] = lists[1:2]
    out[ROW_INPLANE : ROW_INPLANE + 1, width : 2 * width] = lists[0:1]
    lists = normal[...].astype(f32)
    tall = lists.shape[1]
    out[ROW_ABOVE : ROW_ABOVE + 1, 2 * width : 2 * width + tall] = lists[1:2]
    out[ROW_BELOW : ROW_BELOW + 1, 0:tall] = lists[0:1]
    out[ROW_LISTS:, :] = nbr[...].astype(f32)


def weights_kernel(
    embedding,
    radial,
    mix,
    self_w,
    charge_w,
    readout_w,
    readout_v,
    ahead,
    rex3,
    wcu3,
    wb3,
    re3,
    rv_out,
):
    kinds, channels = embedding.shape
    both = jnp.concatenate([mix[...], self_w[...]], axis=1)
    both = jnp.dot(embedding[...], both, precision=highest, preferred_element_type=f32)
    mixed, selfed = both[:, :channels], both[:, channels:]
    table = jnp.concatenate([mixed[s : s + 1] * radial[...] for s in range(kinds)], axis=0)
    rest = jnp.zeros((channels - table.shape[0] - kinds, channels), f32)
    wide = jnp.concatenate([table, selfed, rest], axis=0).T
    rex3[...] = left3(wide[:, : rex3.shape[1] // 3])
    wcu3[...] = left3(jnp.concatenate([charge_w[...].T, readout_w[...].T], axis=0))
    wb3[...] = left3(jnp.concatenate([charge_w[...], readout_w[...]], axis=1))
    re3[...] = left3(table)
    rv_out[...] = jnp.broadcast_to(readout_v[...], (channels, channels)).T


def lift_kernel(all_atoms, block, kernel_filter, out, filter_out):
    out[0] = block[...]
    keeper = jnp.where(rows(kernel_filter.shape) == zero_row, 0.0, 1.0 / all_atoms)
    filter_out[...] = keeper * kernel_filter[...]


def tables_kernel(sizes, data, ahead, *refs):
    own = data.shape[2]
    refs[4][...] = jnp.zeros_like(refs[4])
    refs = refs[:4]
    for n in range(data.shape[0]):
        store_phases(data[n, 0:8, :], *sizes, refs, n * own)


root = math.sqrt(math.log2(math.e))


def pair_basis(u, b):
    t = u - b * root
    return t, jnp.exp2(-(t * t))


def forward_kernel(
    sizes,
    dims,
    group,
    block,
    near_layers,
    early,
    mine,
    theirs,
    rex3,
    wcu3,
    rv_ref,
    radial,
    later_wb3,
    later_re3,
    q_out,
    energy_out,
    pair_out,
    slope_out,
    readout_out,
    *rest,
):
    layers, strips = sizes
    own, width, tall, slots, kinds = dims
    if early:
        first, u_ref, w_ref, x_ref, energy_ref = rest
    else:
        cos_out, sin_out, first, u_ref, w_ref, x_ref, energy_ref, *tables = rest
    here = position_here()
    basis = radial.shape[0]
    channels = rv_ref.shape[0]
    total = mine.shape[0]
    near = 2 * near_layers
    lane8 = lanes((8, own))
    row8 = rows((8, own))
    energy_ref[...] = jnp.zeros_like(energy_ref)
    box = strips * width_x
    partner = (here[0], here[1] ^ 1)

    def first_step(i):
        g, p = domain_at(i, here, sizes)
        lower = theirs[slot_of(g, lax.rem(p + strips - 1, strips), partner, sizes)]
        upper = theirs[slot_of(g, lax.rem(p + 1, strips), partner, sizes)]
        at = jnp.broadcast_to(lower[ROW_INPLANE : ROW_INPLANE + 1], (8, own)).astype(i32)
        from_lower = pick(lower, at)
        at = jnp.broadcast_to(upper[ROW_INPLANE : ROW_INPLANE + 1], (8, own)).astype(i32)
        from_upper = pick(upper, at)
        down = jnp.where(p == 0, -box, 0.0)
        up = jnp.where(p == strips - 1, box, 0.0)
        shift = jnp.where(row8 == 0, jnp.where(lane8 < width, down, up), 0.0)
        first[i] = jnp.where(lane8 < width, from_lower, from_upper) + shift

    def first_steps(n, carry):
        for k in range(group):
            first_step(n * group + k)
        return carry

    local_first = group % layers == 0
    if not local_first:
        lax.fori_loop(0, total // group, first_steps, 0)

    bound = jnp.where((row8 == ROW_KIND) | (row8 == ROW_ID), -1.0, 0.0)
    padding = jnp.where(row8 < 3, far_away, -1.0)
    spacing = basis_reach / (basis - 1)

    def normal_ghosts(g, p, move, row):
        other = lax.rem(g + move + layers, layers)
        j = slot_of(other, p, here, sizes)
        near_by = mine[j, 0:8, :]
        at = jnp.broadcast_to(near_by[row : row + 1], (8, own)).astype(i32)
        inside = at < own
        at = at & (own - 1)
        found = jnp.where(inside, pick(near_by, at), pick(first[j], at))
        beyond = (g + move < 0) | (g + move >= layers)
        return jnp.where(beyond, bound, found)

    def geometry(i, k):
        g, p = domain_at(i, here, sizes)
        record = mine[i, 0:8, :]
        below = normal_ghosts(g, p, -1, ROW_ABOVE)
        above = normal_ghosts(g, p, 1, ROW_BELOW)
        parts = (
            record,
            jnp.where(lane8 < 2 * width, first[i], below),
            jnp.where(lane8 < tall, above, padding),
        )
        index = mine[i, ROW_LISTS : ROW_LISTS + slots, :].astype(i32)
        part = index // own
        at = index & (own - 1)

        def gathered(r):
            a, b, c = [pick(jnp.broadcast_to(q[r : r + 1], (slots, own)), at) for q in parts]
            return jnp.where(part == 0, a, jnp.where(part == 1, b, c))

        dx = gathered(0) - record[0:1]
        dy = gathered(1) - record[1:2]
        dz = gathered(2) - record[2:3]
        code = gathered(ROW_KIND)
        d = jnp.sqrt(dx * dx + dy * dy + dz * dz + softening)
        quarter = d * (1.0 / envelope_reach)
        square = quarter * quarter
        envelope = 1.0 / (1.0 + square * square)
        u_ref[k] = d * (root / spacing)
        for s in range(kinds):
            w_ref[k, s] = jnp.where(code == float(s), envelope, 0.0)
        turn = lax.rem(g - here[0] + 1 + layers, layers)
        side = here[1] + 2 - 4 * (here[1] & 1)
        strip_step = jnp.where(p == here[1], 0, jnp.where(p == lax.rem(side + strips, strips), 1, 2))
        j = jnp.where((turn < near_layers) & (strip_step < 2), strip_step * near_layers + turn, near)
        pair_out[j, 0] = dx
        pair_out[j, 1] = dy
        pair_out[j, 2] = dz
        pair_out[j, 3] = code
        pair_out[j, 4] = gathered(ROW_ID)
        pair_out[j, 5] = d
        return record[ROW_KIND : ROW_KIND + 1], j

    def basis_sums(k, kind_row):
        centre = rows((basis, own)).astype(f32)
        sums = [jnp.zeros((basis, own), f32) for s in range(kinds)]
        for m in range(slots):
            t, e = pair_basis(u_ref[k, m : m + 1, :], centre)
            for s in range(kinds):
                sums[s] = sums[s] + e * w_ref[k, s, m : m + 1, :]
        tail = x_ref.shape[0] // 3 - kinds * basis
        one_hot = jnp.where(rows((tail, own)).astype(f32) == kind_row, 1.0, 0.0)
        x_ref[:, k * own : (k + 1) * own] = right3(jnp.concatenate(sums + [one_hot], axis=0))

    def block_step(start, place, offset):
        found = [geometry(start + k, offset + k) for k in range(block)]
        for k in range(block):
            basis_sums(offset + k, found[k][0])
        live = jnp.concatenate([kind_row for kind_row, _ in found], axis=1) >= 0.0
        pre = mm(rex3[...], x_ref[:, offset * own : (offset + block) * own])
        gate = sigmoid(pre)
        hidden = pre * gate
        both = mm(wcu3[...], right3(hidden))
        charges = jnp.where(live, both[:channels], 0.0)
        readout = both[channels:]
        readout_gate = sigmoid(readout)
        rv = jnp.concatenate([rv_ref[...]] * block, axis=1)
        scaled = jnp.where(live, rv * readout_gate, 0.0)
        local = scaled * readout
        slope = gate * (1.0 + pre * (1.0 - gate))
        back = scaled * (1.0 + readout * (1.0 - readout_gate))
        wide = jnp.sum(local.reshape(channels // 8, 8, block * own), axis=0)
        for k in range(block):
            energy_ref[...] += wide[:, k * own : (k + 1) * own]
        column = pl.multiple_of(place * own, own)
        high, low = split(charges)
        q_out[0:channels, pl.ds(column, block * own)] = high
        q_out[channels : 2 * channels, pl.ds(column, block * own)] = low
        for k in range(block):
            column = pl.multiple_of(found[k][1] * own, own)
            slope_out[:, pl.ds(column, own)] = slope[:, k * own : (k + 1) * own]
            readout_out[:, pl.ds(column, own)] = back[:, k * own : (k + 1) * own]

    def group_step(n, place):
        if local_first:
            for k in range(group):
                first_step(n * group + k)
        for offset in range(0, group, block):
            block_step(n * group + offset, place + offset, offset)

    if early:

        def steps(n, carry):
            group_step(n, n * group)
            return carry

        lax.fori_loop(0, total // group, steps, 0, unroll=total == group)
    else:
        chunk = q_out.shape[1] // own

        def chunk_step(c, carry):
            place = total // chunk - 1 - c

            def steps(n, inner):
                group_step(place * (chunk // group) + n, n * group)
                return inner

            def phases(n, inner):
                record = mine[place * chunk + n, 0:8, :]
                store_phases(record, layers, strips, tables, pl.multiple_of(n * own, own))
                return inner

            lax.fori_loop(0, chunk // group, steps, 0)
            lax.fori_loop(0, chunk, phases, 0)
            for out, high, low in ((cos_out, *tables[:2]), (sin_out, *tables[2:])):
                part = structure_part(high, low, q_out, 0)

                @pl.when(c == 0)
                def _():
                    out[...] = part

                @pl.when(c > 0)
                def _():
                    out[...] += part

            return carry

        lax.fori_loop(0, total // chunk, chunk_step, 0)
    energy_out[...] = jnp.sum(energy_ref[...], axis=0, keepdims=True)
    if not early:
        cos_out[zero_row : zero_row + 1, :] = energy_out[...]


zero_row = (KGRID // 2) * KGRID + KGRID // 2


def structure_part(high, low, q, column):
    channels = q.shape[0] // 2
    at = slice(column, column + high.shape[1])
    wide = mm_nt(high[...], q[:, at])
    return wide[:, :channels] + wide[:, channels:] + mm_nt(low[...], q[0:channels, at])


def structure_kernel(first_half, chunks, *refs):
    *tables, q, energy, out = refs
    column = 0
    part = None
    for n in range(chunks):
        high, low = tables[2 * n : 2 * n + 2]
        more = structure_part(high, low, q, column)
        part = more if part is None else part + more
        column += high.shape[1]
    out[...] = part
    if first_half:
        out[zero_row : zero_row + 1, :] = energy[...]


def near_kernel(sizes, near_layers, side, starts, mine, *refs):
    layers, strips = sizes
    tables, outs, live_out = refs[: 4 * len(starts)], refs[-5:-1], refs[-1]
    own = mine.shape[2]
    here = position_here()
    for j in range(side * near_layers, (side + 1) * near_layers):
        at = slice(j * own, (j + 1) * own)
        slot = slot_of(*near_domain(j, here, sizes, near_layers), here, sizes)
        record = mine[slot, 0:8, :]
        live = jnp.where(record[ROW_KIND : ROW_KIND + 1] >= 0.0, 1.0, 0.0)
        live_out[:, at] = jnp.broadcast_to(live, (8, own))
        if not starts:
            store_phases(record, layers, strips, outs, j * own)
        for n, start in enumerate(starts):
            parts = tables[4 * n : 4 * n + 4]
            end = start + parts[0].shape[1] // own

            def take():
                column = pl.multiple_of((slot - start) * own, own)
                for part, out in zip(parts, outs):
                    out[:, at] = part[:, pl.ds(column, own)]

            if len(starts) == 1:
                take()
            else:
                pl.when((slot >= start) & (slot < end))(take)


def column_kernel(sizes, near_layers, data, *refs):
    tables, outs = refs[:4], refs[4:]
    for n in range(data.shape[0]):
        store_phases(data[n, 0:8, :], *sizes, tables, n * data.shape[2])
    near_kernel(sizes, near_layers, 0, [0], data, *tables, *outs)


def fall_kernel(pairs, fall_out):
    domains, basis = fall_out.shape[0:2]
    spacing = basis_reach / (basis - 1)
    for j in range(domains):
        d = pairs[j, 5]
        quarter = d * (1.0 / envelope_reach)
        square = quarter * quarter
        envelope = 1.0 / (1.0 + square * square)
        over = 1.0 / d
        slope = -envelope * envelope * (4.0 / envelope_reach) * square * quarter * over
        lean = envelope * (-2.0 / (spacing * root)) * over
        u = d * (root / spacing)
        for b in range(basis):
            t, e = pair_basis(u, float(b))
            fall_out[j, b] = e * (lean * t + slope)


def wave_weights(part, other, scale):
    sums = part[...] + other[...]
    return sums, scale[...] * sums


def charge_gradient(weight, high, low):
    channels = weight.shape[1]
    top, bottom = split(weight.T)
    wide = mm(jnp.concatenate([top, bottom], axis=0), high[...])
    return wide[:channels] + wide[channels:] + mm(top, low[...])


def pull_kernel(part, other, scale, high, low, grad_out, energy_out):
    sums, weight = wave_weights(part, other, scale)
    grad_out[...] = charge_gradient(weight, high, low)
    energy_out[...] = jnp.sum(weight * sums, axis=0, keepdims=True)


def backward_kernel(
    sizes,
    dims,
    all_atoms,
    near_layers,
    cos_own,
    cos_other,
    grad_in,
    sin_energy,
    scale,
    cos_high,
    cos_low,
    live_in,
    fall_in,
    wb3,
    re3,
    pair_in,
    slope_in,
    readout_in,
    own_out,
    other_out,
    energy_out,
    b_ref,
    f_ref,
    t_ref,
    hot_ref,
    col_ref,
):
    layers, strips = sizes
    own, width, tall, slots, kinds = dims
    layer, strip = position_here()
    basis = fall_in.shape[1]
    channels = slope_in.shape[0]
    domains = 2 * near_layers
    lanes_all = domains * own

    base = ((layer * strips + (strip - (strip & 1))) * own).astype(f32)
    groups = 8
    size = 2 * own // groups
    group = rows((groups, own))
    member = rows((size, own))
    for j in range(domains):
        target = (pair_in[j, 4] - base).astype(i32)
        t_ref[j, 0] = target // size
        t_ref[j, 1] = target & (size - 1)
        for m in range(slots):
            one = jnp.where(t_ref[j, 1, m : m + 1, :] == member, 1.0, 0.0)
            col_ref[j, :, m * own : (m + 1) * own] = one.astype(bf16)

    sums, weight = wave_weights(cos_own, cos_other, scale)
    grad = grad_in[...] + charge_gradient(weight, cos_high, cos_low)
    grad = grad * live_in[0:1, :]
    both = jnp.concatenate([grad, readout_in[:, 0:lanes_all]], axis=0)
    grad = mm(wb3[...], right3(both)) * slope_in[:, 0:lanes_all]
    b_ref[...] = mm(re3[...], right3(grad))

    found = None
    own_out[...] = jnp.zeros_like(own_out)
    for j in range(domains):
        code = pair_in[j, 3]
        same = [code == float(s) for s in range(kinds)]
        force = jnp.zeros((slots, own), f32)
        for b in range(basis):
            chosen = jnp.zeros((slots, own), f32)
            for s in range(kinds):
                k = s * basis + b
                row = b_ref[k : k + 1, j * own : (j + 1) * own]
                chosen = jnp.where(same[s], row, chosen)
            force = force + fall_in[j, b] * chosen
        for r in range(3):
            part = force * pair_in[j, r]
            high = part.astype(bf16).astype(f32)
            f_ref[j, 2 * r] = high
            f_ref[j, 2 * r + 1] = part - high
            if j == 1:
                own_out[r : r + 1, :] = -jnp.sum(part, axis=0, keepdims=True)
        for m in range(slots):
            at = slice(m * own, (m + 1) * own)
            hit = t_ref[j, 0, m : m + 1, :] == group
            for r in range(3):
                hot = [
                    jnp.where(hit, f_ref[j, 2 * r + n, m : m + 1, :], 0.0) for n in range(2)
                ]
                here = slice(2 * r * groups, 2 * (r + 1) * groups)
                hot_ref[j, here, at] = jnp.concatenate(hot, axis=0).astype(bf16)
        more = mm_nt(hot_ref[j], col_ref[j])
        found = more if found is None else found + more

    spread = jnp.where(rows((size, own)) == (lanes((size, own)) & (size - 1)), 1.0, 0.0)
    wide = jnp.dot(found, spread, precision=highest, preferred_element_type=f32)
    half = groups // 2
    fits = rows((half, own)) == lanes((half, own)) // size
    odd = (strip & 1) == 1
    other_out[...] = jnp.zeros_like(other_out)
    for r in range(3):
        both = wide[2 * r * groups : (2 * r + 1) * groups]
        both = both + wide[(2 * r + 1) * groups : (2 * r + 2) * groups]
        sides = [
            jnp.sum(jnp.where(fits, both[n * half : (n + 1) * half], 0.0), axis=0, keepdims=True)
            for n in range(2)
        ]
        own_out[r : r + 1, :] += jnp.where(odd, sides[1], sides[0])
        other_out[r : r + 1, :] = jnp.where(odd, sides[0], sides[1])

    local = sums[zero_row : zero_row + 1]
    ewald = sin_energy[...] + jnp.sum(weight * sums, axis=0, keepdims=True)
    energy = jnp.sum(local + 0.5 * ewald, axis=1, keepdims=True)
    energy_out[...] = jnp.broadcast_to(energy / all_atoms, energy_out.shape)


def ewald_kernel(
    sizes,
    cos_own,
    cos_other,
    sin_own,
    sin_other,
    scale,
    cos_high,
    cos_low,
    sin_high,
    sin_low,
    q_in,
    out,
):
    layers, strips = sizes
    channels = q_in.shape[0] // 2
    waves = cos_high.shape[0]
    own = out.shape[1]
    mine = slice(own, 2 * own)
    charge_high = q_in[0:channels, 0:own]
    charge_low = q_in[channels : 2 * channels, 0:own]
    charges = jnp.concatenate([charge_high, charge_low, charge_high], axis=0)
    halves = ((cos_own, cos_other), (sin_own, sin_other))
    along_cos, along_sin = [
        mm(left3(wave_weights(part, other, scale)[1]), charges)
        for part, other in halves
    ]
    cosine = cos_high[:, mine].astype(f32) + cos_low[:, mine].astype(f32)
    sine = sin_high[:, mine].astype(f32) + sin_low[:, mine].astype(f32)
    turn = cosine * along_sin - sine * along_cos
    index = lanes((8, waves))
    axis = rows((8, waves))
    part_x = (index // (KGRID * KGRID)).astype(f32) / (strips * width_x)
    part_y = ((index // KGRID) % KGRID - KGRID // 2).astype(f32) / width_y
    part_z = (index % KGRID - KGRID // 2).astype(f32) / (layers * width_z)
    wave = jnp.where(axis == 0, part_x, jnp.where(axis == 1, part_y, part_z))
    wave = jnp.where(axis < 3, wave * (2.0 * math.pi), 0.0)
    out[...] = mm(left3(wave), right3(turn))


def final_kernel(pos, vel, frc, spec, mass, own, ewald, other, moved_out, vel_out, frc_out):
    factor = mass_of(spec[...], mass)
    half_velocity = vel[...] + 0.5 * time_step * frc[...] * factor
    moved_out[...] = pos[...] + time_step * half_velocity
    forces_new = -(own[0:3, :] + ewald[0:3, :] + other[0:3, :])
    frc_out[...] = forces_new
    vel_out[...] = half_velocity + 0.5 * time_step * forces_new * factor


def exchange(x, axis, bit):
    count = lax.axis_size(axis)
    return lax.ppermute(x, axis, [(i, i ^ bit) for i in range(count)])


MIB = 1024 * 1024
vmem = pl.BlockSpec(memory_space=pltpu.VMEM)


def call(kernel, name, outs, ins, scratch=(), unread=(), alias={}, limit=8, work=10**8):
    anywhere = pl.BlockSpec(memory_space=pl.ANY)

    return pl.pallas_call(
        kernel,
        out_shape=[jax.ShapeDtypeStruct(shape, dtype) for shape, dtype in outs],
        in_specs=[anywhere if n in unread else vmem for n in range(len(ins))],
        out_specs=[vmem] * len(outs),
        scratch_shapes=[pltpu.VMEM(shape, dtype) for shape, dtype in scratch],
        compiler_params=pltpu.CompilerParams(vmem_limit_bytes=limit and limit * MIB),
        cost_estimate=pl.CostEstimate(flops=work, bytes_accessed=MIB, transcendentals=0),
        input_output_aliases=alias,
        name=name,
    )(*ins)


def local(
    positions,
    velocities,
    forces,
    species,
    counts,
    neighbours,
    send_inplane,
    send_normal,
    embedding,
    inverse_mass,
    radial_weight,
    mix_weight,
    self_weight,
    charge_weight,
    readout_weight,
    readout_vector,
    kernel_filter,
):
    layers = lax.axis_size("gz")
    strips = lax.axis_size("xy")
    sizes = (layers, strips)
    own = positions.shape[1]
    slots = neighbours.shape[0]
    kinds, channels = embedding.shape
    basis = radial_weight.shape[0]
    dims = (own, send_inplane.shape[1], send_normal.shape[1], slots, kinds)
    all_atoms = own * layers * strips
    waves = KGRID**3
    kind_row = species[None, :]
    total = layers * (strips // 2)
    early = total <= 16 and strips <= 8
    group = min(16, total)
    block_size = min(4, group)
    near_layers = min(3, layers)
    near = 2 * near_layers
    depth = kinds * basis + -(-kinds // 16) * 16

    (block,) = call(
        functools.partial(pack_kernel, sizes),
        "pack",
        [((ROW_LISTS + slots, own), f32)],
        (
            counts[None],
            inverse_mass[None],
            positions,
            velocities,
            forces,
            kind_row,
            neighbours,
            send_inplane,
            send_normal,
        ),
        limit=None,
    )
    def near_part(side, data, tables, starts, given=()):
        parts = [t for table in tables for t in table]
        return call(
            functools.partial(near_kernel, sizes, near_layers, side, starts),
            "near",
            [((waves, near * own), bf16)] * 4 + [((8, near * own), f32)],
            (data, *parts, *given),
            unread=range(1 + len(parts), 1 + len(parts) + len(given)),
            alias={1 + len(parts) + n: n for n in range(len(given))},
            limit=8 if early else 32,
            work=4 * 10**9,
        )

    def phases(data, ahead):
        wide = data.shape[0] * own
        return call(
            functools.partial(tables_kernel, sizes),
            "tables",
            [((waves, wide), bf16)] * 4 + [((8, own), f32)],
            (data, ahead),
            unread=(1,),
            work=4 * 10**9,
        )

    data, scale = call(
        functools.partial(lift_kernel, all_atoms),
        "lift",
        [((1, *block.shape), f32), (kernel_filter.shape, f32)],
        (block, kernel_filter),
        limit=1,
        work=8 * 10**9,
    )
    rex3, wcu3, wb3, re3, rv = call(
        weights_kernel,
        "weights",
        [
            ((channels, 3 * depth), bf16),
            ((2 * channels, 3 * channels), bf16),
            ((channels, 6 * channels), bf16),
            ((kinds * basis, 3 * channels), bf16),
            ((channels, channels), f32),
        ],
        (
            embedding,
            radial_weight,
            mix_weight,
            self_weight,
            charge_weight,
            readout_weight,
            readout_vector[None, :],
            block,
        ),
        limit=None,
        unread=(7,),
        work=4 * 10**9,
    )
    bit = 1
    while bit < layers:
        bits = [bit * n for n in ORDER_GZ[1:]] if 2 * bit < layers else [bit]
        source = block[None] if bit == 1 else data
        data = jnp.concatenate([data] + [exchange(source, "gz", n) for n in bits], axis=0)
        bit *= 4

    tables, starts, zeros = [], [], []
    if early:
        *both, zero = call(
            functools.partial(column_kernel, sizes, near_layers),
            "column",
            [((waves, layers * own), bf16)] * 4
            + [((waves, near * own), bf16)] * 4
            + [((8, near * own), f32)],
            (data,),
            work=10**9,
        )
        tables.append(both[:4])
        starts.append(0)
        near_tables = [*both[4:], zero]
    else:
        near_tables = near_part(0, data, tables, starts)
    bit = 2
    while bit < strips:
        bits = [bit * n for n in ORDER_XY[1:]] if 2 * bit < strips else [bit]
        parts = [exchange(data, "xy", n) for n in bits]
        for n, part in enumerate(parts):
            if early:
                *table, zero = phases(part, near_tables[4] if n == 0 else block)
                zeros.append(zero)
                tables.append(table)
                starts.append((n + 1) * data.shape[0])
        data = jnp.concatenate([data] + parts, axis=0)
        bit *= 4
    records = data[:, 0:8, :]
    for zero in zeros[:2]:
        records = records + zero
    theirs = exchange(records, "xy", 1)

    *near_tables, live = near_part(1, data, tables[1:3], starts[1:3], near_tables)
    chunk = min(16, total)
    outs = [
        ((2 * channels, chunk * own), bf16),
        ((1, channels), f32),
        ((near + 1, PAIR_BLOCKS, slots, own), f32),
        ((channels, (near + 1) * own), f32),
        ((channels, (near + 1) * own), f32),
    ]
    scratch = [
        ((total, 8, own), f32),
        ((group, slots, own), f32),
        ((group, kinds, slots, own), f32),
        ((3 * depth, group * own), bf16),
        ((8, own), f32),
    ]
    if not early:
        outs += [((waves, channels), f32)] * 2
        scratch += [((waves, chunk * own), bf16)] * 4
    q, energy_row, pairs, slope, readout, *sums = call(
        functools.partial(forward_kernel, sizes, dims, group, block_size, near_layers, early),
        "forward",
        outs,
        (data, theirs, rex3, wcu3, rv, radial_weight, wb3, re3),
        scratch,
        limit=16 if early else 48,
    )
    for n in range(2 if early else 0):
        parts = [t for table in tables for t in table[2 * n : 2 * n + 2]]
        sums += call(
            functools.partial(structure_kernel, n == 0, len(tables)),
            "structure",
            [((waves, channels), f32)],
            (*parts, q, energy_row),
            limit=16,
            work=10**9,
        )
    others = [exchange(part, "xy", 1) for part in sums]
    (fall,) = call(
        fall_kernel, "fall", [((near, basis, slots, own), f32)], (pairs,), work=10**9
    )
    grad, sin_energy = call(
        pull_kernel,
        "pull",
        [((channels, near * own), f32), ((1, channels), f32)],
        (sums[1], others[1], scale, *near_tables[2:]),
        limit=16,
        work=10**9,
    )
    groups = 8
    own_grad, other_grad, energy = call(
        functools.partial(backward_kernel, sizes, dims, all_atoms, near_layers),
        "backward",
        [((8, own), f32), ((8, own), f32), ((1, channels), f32)],
        (
            sums[0],
            others[0],
            grad,
            sin_energy,
            scale,
            *near_tables[:2],
            live,
            fall,
            wb3,
            re3,
            pairs,
            slope,
            readout,
        ),
        [
            ((kinds * basis, near * own), f32),
            ((near, 6, slots, own), f32),
            ((near, 2, slots, own), i32),
            ((near, 6 * groups, slots * own), bf16),
            ((near, 2 * own // groups, slots * own), bf16),
        ],
        limit=16,
    )
    arrived = exchange(other_grad, "xy", 1)
    (ewald_grad,) = call(
        functools.partial(ewald_kernel, sizes),
        "ewald",
        [((8, own), f32)],
        (sums[0], others[0], sums[1], others[1], scale, *near_tables, q),
        work=4 * 10**9,
    )
    moved, velocities_new, forces_new = call(
        final_kernel,
        "final",
        [((3, own), f32)] * 3,
        (positions, velocities, forces, kind_row, inverse_mass[None], own_grad, ewald_grad, arrived),
        limit=1,
    )
    return (moved, velocities_new, forces_new, energy[0, 0])


def solution(mesh):
    return jax.shard_map(
        local,
        mesh=mesh,
        in_specs=(
            P(None, ("gz", "xy")),
            P(None, ("gz", "xy")),
            P(None, ("gz", "xy")),
            P(("gz", "xy")),
            P(("gz", "xy")),
            P(None, ("gz", "xy")),
            P(None, ("gz", "xy")),
            P(None, ("gz", "xy")),
            P(),
            P(),
            P(),
            P(),
            P(),
            P(),
            P(),
            P(),
            P(),
        ),
        out_specs=(P(None, ("gz", "xy")), P(None, ("gz", "xy")), P(None, ("gz", "xy")), P()),
        check_vma=False,
    )
```
